256 devices in a mesh: blocks: 128 (over z, y, x), slab: 2 (over core).
Axes of the slice: x: 4, y: 4, z: 8, core: 2. Of those that a mesh axis runs over, the one named last changes fastest.
Arguments:
- state: float32 [4096, 32, 1024], P('blocks', 'slab'), may hold values from -6 to 6
- courant_row: float32 [32], P('slab'), may hold values from -0.8 to 0.8
- courant_col: float32 [32], P('slab'), may hold values from -0.8 to 0.8
- mixing: float32 [32], P('slab'), may hold values from 0.05 to 0.25
- nbr_block: int32 [4096, 4], P('blocks'), may hold values from 0 to 4095, as said below
- nbr_side: int32 [4096, 4], P('blocks'), may hold values from 0 to 3
- nbr_flip: int32 [4096, 4], P('blocks'), may hold values from 0 to 1
- send_idx: int32 [128, 128, 2], P('blocks'), may hold values from 0 to 511
- fine_slot: int32 [128, 192], P('blocks'), may hold values from 0 to 255, as said below
- fine_count: int32 [128], P('blocks'), may hold values from 48 to 192, as said below
Outputs:
- advanced: float32 [4096, 32, 1024], P('blocks', 'slab')
- refined: bfloat16 [24576, 32, 1024], P('blocks', 'slab')
The draws below stay inside these ranges and needn't reach their ends.
Inputs may be any that keep to these rules, and one draw needn't show every extreme that they name: `nbr_block`: every neighbour block lies on the device that holds the block or on the device just before or after it in block order, cyclically. `fine_slot`: the slots of one new owner are distinct. `fine_count`: some new owner uses all 192 slots.
All inputs are finite; a program needn't handle non-finite values.
Results may differ from the reference program's by a relative error of at most 0.001.
Values sent between devices are 32-bit elements; how exact they have to be, the bound alone decides.
No kernel may reach another device: no remote copies, remote signals or barrier semaphores. Data moves between devices by JAX's collectives and lax.ppermute only.
A program may use at most 128 MiB of HBM per device.

```python
import math
import jax
import jax.numpy as jnp
import numpy as np
from jax import lax

CELL = 32
CAP = 2
NB_DEV = 32
FINE_DEV = 192
NBLK = 4096
LEV = 32
N_BLOCKS = 128


def draw_nbr_block(key, part):
    key = jax.random.fold_in(key, 1)
    first, second = jax.random.split(key)
    owner = (jnp.arange(NBLK, dtype=jnp.int32) // NB_DEV)[:, None]
    offset = jax.random.randint(first, (NBLK, 4), -1, 2, dtype=jnp.int32)
    local = jax.random.randint(second, (NBLK, 4), 0, NB_DEV, dtype=jnp.int32)
    return (owner + offset) % N_BLOCKS * NB_DEV + local


def draw_fine_slot(key, part):
    key = jax.random.fold_in(key, 2)
    keys = jax.random.split(key, N_BLOCKS)
    return jax.vmap(lambda k: jax.random.permutation(k, N_BLOCKS * CAP)[:FINE_DEV])(keys).astype(jnp.int32)


def draw_fine_count(key, part):
    key = jax.random.fold_in(key, 3)
    first, second = jax.random.split(key)
    lowest = max(FINE_DEV // 4, 1)
    counts = jax.random.randint(first, (N_BLOCKS,), lowest, FINE_DEV + 1, dtype=jnp.int32)
    fullest = jax.random.randint(second, (), 0, N_BLOCKS, dtype=jnp.int32)
    return jnp.where(jnp.arange(N_BLOCKS, dtype=jnp.int32) == fullest, FINE_DEV, counts).astype(jnp.int32)


def set_ends(entries, rng, smallest, largest):
    longest = entries.shape.index(max(entries.shape))
    spots = []
    for shift in (0, 1):
        where = [jax.random.randint(jax.random.fold_in(rng, axis), (), 0, length) for axis, length in enumerate(entries.shape)]
        where[longest] = (where[longest] + shift) % entries.shape[longest]
        spots.append(tuple(where))
    return entries.at[spots[0]].set(smallest).at[spots[1]].set(largest)


def levels(key, extent, pieces, smallest, top_value):
    factor_of = 1.0
    for axis_at, shards_of in pieces:
        steps = jax.random.uniform(jax.random.fold_in(jax.random.fold_in(key, 6), axis_at), (shards_of,), jnp.float32, smallest / len(pieces), top_value / len(pieces))
        factor_of = factor_of * jnp.repeat(jnp.exp(steps), extent[axis_at] // shards_of).reshape((-1,) + (1,) * (len(extent) - 1 - axis_at))
    return factor_of


def gaussian(key, extent, spread, bound, pieces=(), kind=jnp.bfloat16):
    factor_of = levels(key, extent, pieces, -0.22, 0.18) if pieces else 1.0
    array = jax.random.normal(key, extent, jnp.float32) * spread * factor_of
    return jnp.minimum(jnp.maximum(array, -bound), bound).astype(kind)


def setup_inputs(seed: int = 0) -> dict:
    key_list = jax.random.split(jax.random.key(seed), 11)
    state = gaussian(key_list[0], (NBLK, LEV, CELL * CELL), 1.0, 6.0, ((0, 128), (1, 2)), jnp.float32)
    courant_row = jnp.clip(jax.random.uniform(key_list[1], (LEV,), jnp.float32, -0.8, 0.8) * levels(key_list[1], (LEV,), ((0, 2),), -0.4, 0.0), -0.8, 0.8)
    courant_col = jnp.clip(jax.random.uniform(key_list[2], (LEV,), jnp.float32, -0.8, 0.8) * levels(key_list[2], (LEV,), ((0, 2),), -0.4, 0.0), -0.8, 0.8)
    mixing = jnp.clip(jnp.exp(math.log(0.25) - 1.609438 * jax.random.uniform(key_list[3], (LEV,), jnp.float32) ** levels(key_list[3], (LEV,), ((0, 2),), -0.2, 0.2)), 0.05, 0.25)
    nbr_block = draw_nbr_block(jax.random.fold_in(key_list[10], 71), 0)
    nbr_side = set_ends(jax.random.randint(key_list[5], (NBLK, 4), 0, 4), jax.random.fold_in(key_list[5], 1), 0, 3).astype(jnp.int32)
    nbr_flip = set_ends(jax.random.randint(key_list[6], (NBLK, 4), 0, 2), jax.random.fold_in(key_list[6], 1), 0, 1).astype(jnp.int32)
    send_idx = set_ends(jax.random.randint(key_list[7], (N_BLOCKS, N_BLOCKS, CAP), 0, NB_DEV * 16), jax.random.fold_in(key_list[7], 1), 0, (NB_DEV * 16) - 1).astype(jnp.int32)
    fine_slot = draw_fine_slot(jax.random.fold_in(key_list[10], 71), 0)
    fine_count = draw_fine_count(jax.random.fold_in(key_list[10], 71), 0)
    return {"state": state, "courant_row": courant_row, "courant_col": courant_col, "mixing": mixing, "nbr_block": nbr_block, "nbr_side": nbr_side, "nbr_flip": nbr_flip, "send_idx": send_idx, "fine_slot": fine_slot, "fine_count": fine_count}


def interp_table():
    table = np.zeros((32, 8))
    for fine in range(32):
        x = (fine + 0.5) / 4.0
        start = min(max(int(np.floor(x - 0.5)) - 1, 0), 4)
        nodes = start + np.arange(4) + 0.5
        for a in range(4):
            weight = 1.0
            for b in range(4):
                if b != a:
                    weight *= (x - nodes[b]) / (nodes[a] - nodes[b])
            table[fine, start + a] = weight
    return np.kron(table, table).T.astype(np.float32)


def edge_strips(grid):
    sides = [
        jnp.stack([grid[:, :, 0, :], grid[:, :, 1, :]], 1),
        jnp.stack([grid[:, :, 31, :], grid[:, :, 30, :]], 1),
        jnp.stack([grid[:, :, :, 0], grid[:, :, :, 1]], 1),
        jnp.stack([grid[:, :, :, 31], grid[:, :, :, 30]], 1),
    ]
    return jnp.stack(sides, 1)


def advance(state, ghost, vert, courant_row, courant_col, mixing):
    count, lev = state.shape[0], state.shape[1]
    grid = state.reshape(count, lev, 32, 32)
    ext_row = jnp.concatenate([ghost[:, 0, 1][:, :, None, :], ghost[:, 0, 0][:, :, None, :], grid,
                               ghost[:, 1, 0][:, :, None, :], ghost[:, 1, 1][:, :, None, :]], 2)
    ext_col = jnp.concatenate([ghost[:, 2, 1][..., None], ghost[:, 2, 0][..., None], grid,
                               ghost[:, 3, 0][..., None], ghost[:, 3, 1][..., None]], 3)
    row_diff = (8.0 * (ext_row[:, :, 3:35] - ext_row[:, :, 1:33]) - (ext_row[:, :, 4:36] - ext_row[:, :, 0:32])) / 12.0
    col_diff = (8.0 * (ext_col[..., 3:35] - ext_col[..., 1:33]) - (ext_col[..., 4:36] - ext_col[..., 0:32])) / 12.0
    tend = -courant_row[None, :, None, None] * row_diff - courant_col[None, :, None, None] * col_diff
    return state + tend.reshape(count, lev, 1024) + mixing[None, :, None] * vert


def windows_of(advanced):
    count, lev = advanced.shape[0], advanced.shape[1]
    grid = advanced.reshape(count, lev, 4, 8, 4, 8)
    return grid.transpose(0, 2, 4, 1, 3, 5).reshape(count * 16, lev, 64)


def reference(state, courant_row, courant_col, mixing, nbr_block, nbr_side, nbr_flip, send_idx, fine_slot, fine_count):
    count, lev = state.shape[0], state.shape[1]
    strips = edge_strips(state.reshape(count, lev, 32, 32))
    flat = strips.reshape(count * 4, 2, lev, 32)
    ghost = flat[(nbr_block * 4 + nbr_side).reshape(-1)].reshape(count, 4, 2, lev, 32)
    ghost = jnp.where(nbr_flip[:, :, None, None, None] == 1, ghost[..., ::-1], ghost)
    padded = jnp.pad(state, ((0, 0), (1, 1), (0, 0)))
    vert = padded[:, 2:] - 2.0 * state + padded[:, :-2]
    advanced = advance(state, ghost, vert, courant_row, courant_col, mixing)
    windows = windows_of(advanced)
    peers = fine_slot.shape[0]
    src = fine_slot // CAP
    slot_k = fine_slot % CAP
    dst = jnp.arange(peers, dtype=jnp.int32)[:, None]
    local = send_idx[src, dst, slot_k]
    parent = windows[(src * (NB_DEV * 16) + local).reshape(-1)]
    table = jnp.asarray(interp_table())
    fine = jnp.einsum("flc,cp->flp", parent, table, precision=lax.Precision.HIGHEST)
    live = (jnp.arange(FINE_DEV, dtype=jnp.int32)[None, :] < fine_count[:, None]).reshape(-1)
    fine = jnp.where(live[:, None, None], fine, 0.0).astype(jnp.bfloat16)
    return advanced, fine
```

```python
import jax
import jax.numpy as jnp
import ml_dtypes
import numpy as np
from jax import lax
from jax.experimental import pallas as pl
from jax.experimental.pallas import tpu as pltpu
from jax.sharding import PartitionSpec as P

CHUNK = 8
VMEM_LIMIT = 48 * 1024 * 1024


def interp_1d():
    table = np.zeros((32, 8))
    for fine in range(32):
        x = (fine + 0.5) / 4.0
        start = min(max(int(np.floor(x - 0.5)) - 1, 0), 4)
        nodes = start + np.arange(4) + 0.5
        for a in range(4):
            weight = 1.0
            for b in range(4):
                if b != a:
                    weight *= (x - nodes[b]) / (nodes[a] - nodes[b])
            table[fine, start + a] = weight
    return table


def as_bf16(array):
    return np.asarray(array, np.float32).astype(ml_dtypes.bfloat16)


def refine_table():
    table = interp_1d()
    full = np.kron(table, table).T.astype(np.float32)
    high = as_bf16(full)
    low = as_bf16(full - high.astype(np.float32))
    return np.concatenate([high, low, high, low], 0)


def strip_cell(side, depth, t):
    line = depth if side in (0, 2) else 31 - depth
    return line * 32 + t if side < 2 else t * 32 + line


def strip_map():
    pick = np.zeros((1024, 256))
    for side in range(4):
        for depth in range(2):
            for t in range(32):
                pick[strip_cell(side, depth, t), side * 64 + depth * 32 + t] = 1.0
    return as_bf16(pick)


def ghost_map(side):
    first = side in (0, 2)
    out = np.zeros((128, 1024))
    for flip in range(2):
        for t in range(32):
            to = 31 - t if flip else t
            near = flip * 64 + t
            far = flip * 64 + 32 + t
            sign = 1.0 if first else -1.0
            out[near, strip_cell(side, 0, to)] += 8.0 * sign
            out[far, strip_cell(side, 0, to)] -= sign
            out[near, strip_cell(side, 1, to)] -= sign
    return as_bf16(np.concatenate([out, out], 0))


def stencil_map():
    own = np.zeros((128, 256))
    other = np.zeros((128, 256))
    weights = {-2: -1.0, -1: 8.0, 1: -8.0, 2: 1.0}
    for row in range(4):
        for col in range(32):
            lane = row * 32 + col
            for step, weight in weights.items():
                r = row + step
                if 0 <= r < 4:
                    own[r * 32 + col, lane] += weight
                else:
                    other[(r % 4) * 32 + col, lane] += weight
                c = col + step
                if 0 <= c < 32:
                    own[row * 32 + c, 128 + lane] += weight
    return as_bf16(np.concatenate([own, own, other, other], 0))


def window_map():
    pick = np.zeros((256, 256))
    for row in range(8):
        for col in range(32):
            pick[row * 32 + col, (col // 8) * 64 + row * 8 + col % 8] = 1.0
    return as_bf16(np.concatenate([pick, pick], 0))


def split(x):
    high = x.astype(jnp.bfloat16)
    low = (x - high.astype(jnp.float32)).astype(jnp.bfloat16)
    return high, low


def dot(a, b):
    return jnp.dot(a, b, preferred_element_type=jnp.float32)


def strips_kernel(state_ref, pick_ref, strips_ref, edge_ref):
    slab = lax.axis_index("slab")
    count, lev = state_ref.shape[0], state_ref.shape[1]

    def step(i, carry):
        b = i * CHUNK
        x = state_ref[pl.ds(b, CHUNK)]
        high, low = split(x.reshape(CHUNK * lev, 1024))
        s = dot(high, pick_ref[...]) + dot(low, pick_ref[...])
        s = s.reshape(CHUNK, lev, 256)
        strips_ref[pl.ds(b, CHUNK), 0] = s[:, :, :128]
        strips_ref[pl.ds(b, CHUNK), 1] = s[:, :, 128:]
        edge_ref[pl.ds(b, CHUNK), :] = jnp.where(slab == 0, x[:, lev - 1, :], x[:, 0, :])
        return carry

    lax.fori_loop(0, count // CHUNK, step, 0)


def levels_of(ref, lev):
    at = lax.broadcasted_iota(jnp.int32, (lev, 128), 0)
    out = jnp.zeros((lev, 128), jnp.float32)
    for l in range(lev):
        out = jnp.where(at == l, ref[l], out)
    return out


def advance_kernel(
    block_ref,
    side_ref,
    flip_ref,
    send_ref,
    crow_ref,
    ccol_ref,
    mix_ref,
    state_ref,
    edge_ref,
    prev_ref,
    own_ref,
    next_ref,
    col_ref,
    row0_ref,
    row1_ref,
    sten_ref,
    win_ref,
    adv_ref,
    pay_ref,
    near,
    ghosts,
    wins,
):
    slab = lax.axis_index("slab")
    here = lax.axis_index("blocks")
    peers = lax.axis_size("blocks")
    count, lev = state_ref.shape[0], state_ref.shape[1]
    near[0] = prev_ref[...]
    near[1] = own_ref[...]
    near[2] = next_ref[...]
    a_row = levels_of(crow_ref, lev) * (1.0 / 12.0)
    a_col = levels_of(ccol_ref, lev) * (1.0 / 12.0)
    mix = levels_of(mix_ref, lev)
    half = lax.broadcasted_iota(jnp.int32, (lev, 128), 1) // 64

    def gather(b, carry):
        for s in range(4):
            block = block_ref[b, s]
            side = side_ref[b, s]
            flip = flip_ref[b, s]
            rel = block // count - here + 1
            rel = jnp.where(rel < 0, rel + peers, rel)
            rel = jnp.where(rel >= peers, rel - peers, rel)
            x = near[rel, block % count, side // 2]
            x = jnp.where(side % 2 == flip, x, pltpu.roll(x, 64, 1))
            x = jnp.where(half == flip, x, 0.0) * (a_row if s < 2 else a_col)
            high, low = split(x)
            rows = pl.ds(pl.multiple_of(b * lev, lev), lev)
            ghosts[rows, s * 256 : s * 256 + 128] = high
            ghosts[rows, s * 256 + 128 : s * 256 + 256] = low
        return carry

    lax.fori_loop(0, count, gather, 0)

    rows = CHUNK * lev
    lane = lax.broadcasted_iota(jnp.int32, (rows, 128), 1)
    level = lax.broadcasted_iota(jnp.int32, (CHUNK, lev, 128), 1)

    def step(i, carry):
        b = i * CHUNK
        r = pl.ds(pl.multiple_of(i * rows, rows), rows)
        side_cols = dot(ghosts[r, 512:1024], col_ref[...])
        side_rows = {0: dot(ghosts[r, 0:256], row0_ref[...]), 7: dot(ghosts[r, 256:512], row1_ref[...])}
        tiles = [state_ref[pl.ds(b, CHUNK), :, 128 * j : 128 * j + 128] for j in range(8)]
        flat = [t.reshape(rows, 128) for t in tiles]
        zero = jnp.zeros((rows, 128), jnp.float32)
        done = []
        for j in range(8):
            other = jnp.where(lane < 64, flat[j + 1] if j < 7 else zero, flat[j - 1] if j else zero)
            diff = dot(jnp.concatenate(split(flat[j]) + split(other), 1), sten_ref[...])
            diff = diff.reshape(CHUNK, lev, 256)
            x = tiles[j]
            edge = edge_ref[pl.ds(b, CHUNK), 128 * j : 128 * j + 128][:, None, :]
            below = jnp.where(level == 0, jnp.where(slab == 0, 0.0, edge), pltpu.roll(x, 1, 1))
            above = jnp.where(level == lev - 1, jnp.where(slab == 0, edge, 0.0), pltpu.roll(x, lev - 1, 1))
            vert = above - 2.0 * x + below
            side_part = side_cols[:, 128 * j : 128 * j + 128]
            if j in side_rows:
                side_part = side_part + side_rows[j]
            out = x + a_row * diff[:, :, :128] + a_col * diff[:, :, 128:] + mix * vert
            out = out + side_part.reshape(CHUNK, lev, 128)
            adv_ref[pl.ds(b, CHUNK), :, 128 * j : 128 * j + 128] = out
            done.append(out.reshape(rows, 128))
            if j % 2:
                pair = jnp.concatenate(done[-2:], 1)
                w = dot(jnp.concatenate(split(pair), 1), win_ref[...])
                w = w.reshape(CHUNK, lev, 256)
                wins[pl.ds(b, CHUNK), j // 2, 0] = w[:, :, :128]
                wins[pl.ds(b, CHUNK), j // 2, 1] = w[:, :, 128:]
        return carry

    lax.fori_loop(0, count // CHUNK, step, 0)

    def pack(d, carry):
        parts = []
        for k in range(2):
            w = send_ref[d, k]
            x = wins[w // 16, (w // 4) % 4, (w // 2) % 2]
            parts.append(jnp.where(w % 2 == k, x, pltpu.roll(x, 64, 1)))
        pay_ref[d] = jnp.where(half == 0, parts[0], parts[1])
        return carry

    lax.fori_loop(0, peers, pack, 0)


def refine_kernel(slot_ref, count_ref, recv_ref, table_ref, out_ref, parents):
    start = pl.program_id(0) * out_ref.shape[0]
    lev = recv_ref.shape[1]
    half = lax.broadcasted_iota(jnp.int32, (lev, 128), 1) // 64
    live = count_ref[0]
    for f in range(out_ref.shape[0]):
        slot = slot_ref[0, start + f]
        x = recv_ref[slot // 2]
        x = jnp.where(half == slot % 2, x, pltpu.roll(x, 64, 1))
        x = jnp.where(start + f < live, x, 0.0)
        high, low = split(x)
        parents[f * lev : (f + 1) * lev, :128] = high
        parents[f * lev : (f + 1) * lev, 128:] = low
    fine = dot(parents[...], table_ref[...])
    out_ref[...] = fine.astype(jnp.bfloat16).reshape(out_ref.shape)


VMEM = pl.BlockSpec(memory_space=pltpu.VMEM)
SMEM = pl.BlockSpec(memory_space=pltpu.SMEM)


def make_strips(state):
    count, lev = state.shape[:2]
    return pl.pallas_call(
        strips_kernel,
        out_shape=(
            jax.ShapeDtypeStruct((count, 2, lev, 128), jnp.float32),
            jax.ShapeDtypeStruct((count, 1024), jnp.float32),
        ),
        in_specs=[VMEM, VMEM],
        out_specs=(VMEM, VMEM),
        compiler_params=pltpu.CompilerParams(vmem_limit_bytes=VMEM_LIMIT),
        name="strips",
    )(state, jnp.asarray(strip_map()))


def make_advanced(ints, coefs, state, edge, nearby, peers):
    count, lev = state.shape[:2]
    col = np.concatenate([ghost_map(2), ghost_map(3)], 0)
    maps = [col, ghost_map(0)[:, :128], ghost_map(1)[:, 896:], stencil_map(), window_map()]
    return pl.pallas_call(
        advance_kernel,
        out_shape=(
            jax.ShapeDtypeStruct(state.shape, jnp.float32),
            jax.ShapeDtypeStruct((peers, lev, 128), jnp.float32),
        ),
        in_specs=[SMEM] * 7 + [VMEM] * 10,
        out_specs=(VMEM, VMEM),
        scratch_shapes=[
            pltpu.VMEM((3, count, 2, lev, 128), jnp.float32),
            pltpu.VMEM((count * lev, 1024), jnp.bfloat16),
            pltpu.VMEM((count, 4, 2, lev, 128), jnp.float32),
        ],
        compiler_params=pltpu.CompilerParams(vmem_limit_bytes=VMEM_LIMIT),
        name="advance",
    )(*ints, *coefs, state, edge, *nearby, *[jnp.asarray(m) for m in maps])


def make_refined(slots, live, received):
    fine = slots.shape[1]
    peers, lev = received.shape[:2]
    size = next(n for n in (24, 16, 8, 6, 4, 2, 1) if fine % n == 0)
    return pl.pallas_call(
        refine_kernel,
        grid=(fine // size,),
        out_shape=jax.ShapeDtypeStruct((fine, lev, 1024), jnp.bfloat16),
        in_specs=[SMEM, SMEM, VMEM, VMEM],
        out_specs=pl.BlockSpec((size, lev, 1024), lambda i: (i, 0, 0)),
        scratch_shapes=[pltpu.VMEM((size * lev, 256), jnp.bfloat16)],
        compiler_params=pltpu.CompilerParams(vmem_limit_bytes=VMEM_LIMIT),
        name="refine",
    )(slots, live, received, jnp.asarray(refine_table()))


def body(
    state,
    courant_row,
    courant_col,
    mixing,
    nbr_block,
    nbr_side,
    nbr_flip,
    send_idx,
    fine_slot,
    fine_count,
):
    peers = lax.axis_size("blocks")
    strips, edge = make_strips(state)
    up = [(i, (i + 1) % peers) for i in range(peers)]
    down = [(j, i) for i, j in up]
    before = lax.ppermute(strips, "blocks", up)
    after = lax.ppermute(strips, "blocks", down)
    edge = lax.ppermute(edge, "slab", [(0, 1), (1, 0)])
    advanced, payload = make_advanced(
        (nbr_block, nbr_side, nbr_flip, send_idx[0]),
        (courant_row, courant_col, mixing),
        state,
        edge,
        (before, strips, after),
        peers,
    )
    received = lax.all_to_all(payload, "blocks", split_axis=0, concat_axis=0, tiled=True)
    return advanced, make_refined(fine_slot, fine_count, received)


def solution(mesh):
    in_specs = (
        P("blocks", "slab", None),
        P("slab"),
        P("slab"),
        P("slab"),
        P("blocks", None),
        P("blocks", None),
        P("blocks", None),
        P("blocks", None, None),
        P("blocks", None),
        P("blocks"),
    )
    out_specs = (P("blocks", "slab", None), P("blocks", "slab", None))
    return jax.shard_map(body, mesh=mesh, in_specs=in_specs, out_specs=out_specs, check_vma=False)
```

```python
import jax
import jax.numpy as jnp
import ml_dtypes
import numpy as np
from jax import lax
from jax.experimental import pallas as pl
from jax.experimental.pallas import tpu as pltpu
from jax.sharding import PartitionSpec as P

CHUNK = 8
PACK = 16
VMEM_LIMIT = 24 * 1024 * 1024


def interp_1d():
    table = np.zeros((32, 8))
    for fine in range(32):
        x = (fine + 0.5) / 4.0
        start = min(max(int(np.floor(x - 0.5)) - 1, 0), 4)
        nodes = start + np.arange(4) + 0.5
        for a in range(4):
            weight = 1.0
            for b in range(4):
                if b != a:
                    weight *= (x - nodes[b]) / (nodes[a] - nodes[b])
            table[fine, start + a] = weight
    return table


def as_bf16(array):
    return np.asarray(array, np.float32).astype(ml_dtypes.bfloat16)


def refine_table():
    table = interp_1d()
    full = np.kron(table, table).T.astype(np.float32)
    high = as_bf16(full)
    low = as_bf16(full - high.astype(np.float32))
    return np.concatenate([high, low, high, low], 0)


def strip_cell(side, depth, t):
    line = depth if side in (0, 2) else 31 - depth
    return line * 32 + t if side < 2 else t * 32 + line


def ghost_map(side):
    first = side in (0, 2)
    out = np.zeros((128, 1024))
    for flip in range(2):
        for t in range(32):
            to = 31 - t if flip else t
            near = flip * 64 + t
            far = flip * 64 + 32 + t
            sign = 1.0 if first else -1.0
            out[near, strip_cell(side, 0, to)] += 8.0 * sign
            out[far, strip_cell(side, 0, to)] -= sign
            out[near, strip_cell(side, 1, to)] -= sign
    return as_bf16(np.concatenate([out, out], 0))


def window_order(table):
    out = np.zeros_like(table)
    for row in range(32):
        for col in range(32):
            to = (row // 8) * 256 + (col // 8) * 64 + (row % 8) * 8 + col % 8
            out[:, to] = table[:, row * 32 + col]
    return out


def stencil_map():
    own = np.zeros((128, 256))
    other = np.zeros((128, 256))
    weights = {-2: -1.0, -1: 8.0, 1: -8.0, 2: 1.0}
    for row in range(4):
        for col in range(32):
            lane = row * 32 + col
            for step, weight in weights.items():
                r = row + step
                if 0 <= r < 4:
                    own[r * 32 + col, lane] += weight
                else:
                    other[(r % 4) * 32 + col, lane] += weight
                c = col + step
                if 0 <= c < 32:
                    own[row * 32 + c, 128 + lane] += weight
    return as_bf16(np.concatenate([own, own, other, other], 0))


def window_map():
    pick = np.zeros((256, 256))
    for row in range(8):
        for col in range(32):
            pick[row * 32 + col, (col // 8) * 64 + row * 8 + col % 8] = 1.0
    return as_bf16(np.concatenate([pick, pick], 0))


def split(x):
    high = x.astype(jnp.bfloat16)
    low = (x - high.astype(jnp.float32)).astype(jnp.bfloat16)
    return high, low


def dot(a, b):
    return jnp.dot(a, b, preferred_element_type=jnp.float32)


def strips_kernel(state_ref, strips_ref, edge_ref, held, sems):
    slab = lax.axis_index("slab")
    count, lev = state_ref.shape[0], state_ref.shape[1]
    steps = count // CHUNK
    copies = []
    for i in range(steps):
        part = pl.ds(i * CHUNK, CHUNK)
        copies.append(pltpu.make_async_copy(state_ref.at[part], held.at[part], sems.at[i]))
        copies[i].start()
    cell = lax.broadcasted_iota(jnp.int32, (1024, 128), 0)
    to = lax.broadcasted_iota(jnp.int32, (1024, 128), 1)
    line = to // 32
    line = jnp.where(line < 2, line, 33 - line)
    pick = jnp.where((cell // 32 == to % 32) & (cell % 32 == line), 1.0, 0.0).astype(jnp.bfloat16)
    rows = CHUNK * lev
    lane = lax.broadcasted_iota(jnp.int32, (rows, 128), 1)
    for i in range(steps):
        copies[i].wait()
        part = slice(i * CHUNK, i * CHUNK + CHUNK)
        x = held[part]
        tail = x[:, :, 896:].reshape(rows, 128)
        tail = jnp.where((lane // 32) % 2 == 0, pltpu.roll(tail, 96, 1), pltpu.roll(tail, 32, 1))
        strips_ref[part, 0] = jnp.where(lane < 64, x[:, :, :128].reshape(rows, 128), tail).reshape(CHUNK, lev, 128)
        high, low = split(x.reshape(rows, 1024))
        strips_ref[part, 1] = (dot(high, pick) + dot(low, pick)).reshape(CHUNK, lev, 128)
        edge_ref[part] = jnp.where(slab == 0, x[:, lev - 1, :], x[:, 0, :])


def levels_of(ref, lev):
    at = lax.broadcasted_iota(jnp.int32, (lev, 128), 0)
    out = jnp.zeros((lev, 128), jnp.float32)
    for l in range(lev):
        out = jnp.where(at == l, ref[l], out)
    return out


def local_kernel(crow_ref, ccol_ref, mix_ref, state_ref, edge_ref, sten_ref, win_ref, base_ref, wins_ref):
    slab = lax.axis_index("slab")
    count, lev = state_ref.shape[0], state_ref.shape[1]
    a_row = levels_of(crow_ref, lev) * (1.0 / 12.0)
    a_col = levels_of(ccol_ref, lev) * (1.0 / 12.0)
    mix = levels_of(mix_ref, lev)
    rows = CHUNK * lev
    lane = lax.broadcasted_iota(jnp.int32, (rows, 128), 1)
    level = lax.broadcasted_iota(jnp.int32, (CHUNK, lev, 128), 1)
    zero = jnp.zeros((rows, 128), jnp.float32)

    def step(i, carry):
        blocks = pl.ds(pl.multiple_of(i * CHUNK, CHUNK), CHUNK)
        tiles = [state_ref[blocks, :, 128 * j : 128 * j + 128] for j in range(8)]
        flat = [t.reshape(rows, 128) for t in tiles]
        left = []
        for j in range(8):
            other = jnp.where(lane < 64, flat[j + 1] if j < 7 else zero, flat[j - 1] if j else zero)
            left.append(jnp.concatenate(split(flat[j]) + split(other), 1))
        diff = dot(jnp.concatenate(left, 0), sten_ref[...])
        done = []
        for j in range(8):
            lanes = slice(128 * j, 128 * j + 128)
            x = tiles[j]
            edge = edge_ref[blocks, lanes][:, None, :]
            below = jnp.where(level == 0, jnp.where(slab == 0, 0.0, edge), pltpu.roll(x, 1, 1))
            above = jnp.where(level == lev - 1, jnp.where(slab == 0, edge, 0.0), pltpu.roll(x, lev - 1, 1))
            vert = above - 2.0 * x + below
            d = diff[rows * j : rows * j + rows].reshape(CHUNK, lev, 256)
            out = x + a_row * d[:, :, :128] + a_col * d[:, :, 128:] + mix * vert
            base_ref[blocks, :, lanes] = out
            done.append(out.reshape(rows, 128))
        pairs = []
        for j in range(4):
            pairs.append(jnp.concatenate(split(jnp.concatenate(done[2 * j : 2 * j + 2], 1)), 1))
        w = dot(jnp.concatenate(pairs, 0), win_ref[...])
        for j in range(4):
            v = w[rows * j : rows * j + rows].reshape(CHUNK, lev, 256)
            wins_ref[blocks, 2 * j] = v[:, :, :128]
            wins_ref[blocks, 2 * j + 1] = v[:, :, 128:]
        return carry

    lax.fori_loop(0, count // CHUNK, step, 0)


def pack_kernel(
    code_ref,
    send_ref,
    crow_ref,
    ccol_ref,
    base_ref,
    prev_ref,
    own_ref,
    next_ref,
    col0_ref,
    col1_ref,
    row0_ref,
    row1_ref,
    pay_ref,
    ghosts_ref,
    near,
    wins,
):
    count, lev = own_ref.shape[0], own_ref.shape[2]
    near[0:count] = prev_ref[...]
    near[count : 2 * count] = own_ref[...]
    near[2 * count :] = next_ref[...]
    a_row = levels_of(crow_ref, lev) * (1.0 / 12.0)
    a_col = levels_of(ccol_ref, lev) * (1.0 / 12.0)
    half = lax.broadcasted_iota(jnp.int32, (lev, 128), 1) // 64
    rows = CHUNK * lev

    def gather(i, carry):
        for s in range(4):
            parts = []
            for n in range(CHUNK):
                code = code_ref[s, i * CHUNK + n]
                x = near[code >> 3, (code >> 2) & 1]
                x = jnp.where((code & 2) == 0, x, pltpu.roll(x, 64, 1))
                parts.append(jnp.where(half == (code & 1), x, 0.0))
            x = jnp.stack(parts) * (a_row if s < 2 else a_col)
            high, low = split(x.reshape(rows, 128))
            at = pl.ds(pl.multiple_of(i * rows, rows), rows)
            ghosts_ref[at, s * 256 : s * 256 + 128] = high
            ghosts_ref[at, s * 256 + 128 : s * 256 + 256] = low
        return carry

    lax.fori_loop(0, count // CHUNK, gather, 0)

    def add(i, carry):
        blocks = pl.ds(pl.multiple_of(i * CHUNK, CHUNK), CHUNK)
        at = pl.ds(pl.multiple_of(i * rows, rows), rows)
        row0 = dot(ghosts_ref[at, 0:256], row0_ref[...]).reshape(CHUNK, lev, 256)
        row1 = dot(ghosts_ref[at, 256:512], row1_ref[...]).reshape(CHUNK, lev, 256)
        for h, col_ref in enumerate((col0_ref, col1_ref)):
            c = dot(ghosts_ref[at, 512 + 256 * h : 768 + 256 * h], col_ref[...]).reshape(CHUNK, lev, 512)
            for j in range(4):
                v = base_ref[blocks, 2 * j + h] + c[:, :, 128 * j : 128 * j + 128]
                if j == 0:
                    v = v + row0[:, :, 128 * h : 128 * h + 128]
                if j == 3:
                    v = v + row1[:, :, 128 * h : 128 * h + 128]
                wins[blocks, 2 * j + h] = v
        return carry

    lax.fori_loop(0, count // CHUNK, add, 0)

    def pack(d, carry):
        parts = []
        for k in range(2):
            w = send_ref[k, d]
            x = wins[w >> 4, (w >> 1) & 7]
            parts.append(jnp.where((w & 1) == k, x, pltpu.roll(x, 64, 1)))
        pay_ref[d] = jnp.where(half == 0, parts[0], parts[1])
        return carry

    lax.fori_loop(0, pay_ref.shape[0], pack, 0, unroll=PACK)


def finish_kernel(base_ref, ghosts_ref, col_ref, row0_ref, row1_ref, out_ref):
    blocks, lev = base_ref.shape[0], base_ref.shape[1]
    c = dot(ghosts_ref[:, 512:1024], col_ref[...]).reshape(blocks, lev, 1024)
    out_ref[...] = base_ref[...] + c
    out_ref[:, :, :128] += dot(ghosts_ref[:, 0:256], row0_ref[...]).reshape(blocks, lev, 128)
    out_ref[:, :, 896:] += dot(ghosts_ref[:, 256:512], row1_ref[...]).reshape(blocks, lev, 128)


def refine_kernel(slot_ref, count_ref, recv_ref, table_ref, out_ref, parents, held, sems):
    lev = recv_ref.shape[1]
    steps = sems.shape[0]
    size = out_ref.shape[0] // steps
    half = lax.broadcasted_iota(jnp.int32, (lev, 128), 1) // 64
    live = count_ref[0]

    def copy(i):
        part = pl.ds(i * size, size)
        return pltpu.make_async_copy(held.at[part], out_ref.at[part], sems.at[i])

    def step(i, carry):
        start = i * size
        for f in range(size):
            slot = slot_ref[0, start + f]
            x = recv_ref[slot >> 1]
            x = jnp.where(half == (slot & 1), x, pltpu.roll(x, 64, 1))
            x = jnp.where(start + f < live, x, 0.0)
            high, low = split(x)
            parents[f * lev : (f + 1) * lev, :128] = high
            parents[f * lev : (f + 1) * lev, 128:] = low
        fine = dot(parents[...], table_ref[...])
        held[pl.ds(start, size)] = fine.astype(jnp.bfloat16).reshape(size, lev, 1024)
        copy(i).start()
        return carry

    lax.fori_loop(0, steps, step, 0)
    for i in range(steps):
        copy(i).wait()


VMEM = pl.BlockSpec(memory_space=pltpu.VMEM)
SMEM = pl.BlockSpec(memory_space=pltpu.SMEM)
HBM = pl.BlockSpec(memory_space=pltpu.HBM)
PARAMS = pltpu.CompilerParams(vmem_limit_bytes=VMEM_LIMIT)


def cost(flops, size):
    return pl.CostEstimate(flops=flops, bytes_accessed=size, transcendentals=0)


def make_strips(state):
    count, lev = state.shape[:2]
    return pl.pallas_call(
        strips_kernel,
        out_shape=(
            jax.ShapeDtypeStruct((count, 2, lev, 128), jnp.float32),
            jax.ShapeDtypeStruct((count, 1024), jnp.float32),
        ),
        in_specs=[HBM],
        out_specs=(VMEM, VMEM),
        scratch_shapes=[pltpu.VMEM(state.shape, jnp.float32), pltpu.SemaphoreType.DMA((count // CHUNK,))],
        compiler_params=PARAMS,
        name="strips",
    )(pltpu.with_memory_space_constraint(state, pltpu.HBM))


def make_local(coefs, state, edge):
    count, lev = state.shape[:2]
    return pl.pallas_call(
        local_kernel,
        out_shape=(
            jax.ShapeDtypeStruct(state.shape, jnp.float32),
            jax.ShapeDtypeStruct((count, 8, lev, 128), jnp.float32),
        ),
        in_specs=[SMEM] * 3 + [VMEM] * 4,
        out_specs=(VMEM, VMEM),
        compiler_params=PARAMS,
        cost_estimate=cost(4 * 10**9, 8 * 10**6),
        name="local",
    )(*coefs, state, edge, jnp.asarray(stencil_map()), jnp.asarray(window_map()))


def make_payload(code, send, coefs, base, nearby):
    count, lev = base.shape[0], base.shape[2]
    sides = [window_order(ghost_map(s)) for s in range(4)]
    cols = [m.reshape(256, 4, 256)[:, :, 128 * h : 128 * h + 128].reshape(256, 512) for h, m in enumerate(sides[2:])]
    maps = cols + [sides[0][:, :256], sides[1][:, 768:]]
    return pl.pallas_call(
        pack_kernel,
        out_shape=(
            jax.ShapeDtypeStruct((send.shape[1], lev, 128), jnp.float32),
            jax.ShapeDtypeStruct((count * lev, 1024), jnp.bfloat16),
        ),
        in_specs=[SMEM] * 4 + [VMEM] * 8,
        out_specs=(VMEM, VMEM),
        scratch_shapes=[
            pltpu.VMEM((3 * count, 2, lev, 128), jnp.float32),
            pltpu.VMEM((count, 8, lev, 128), jnp.float32),
        ],
        compiler_params=PARAMS,
        cost_estimate=cost(10**9, 8 * 10**6),
        name="pack",
    )(code, send, *coefs[:2], base, *nearby, *[jnp.asarray(m) for m in maps])


def make_advanced(base, ghosts):
    count, lev = base.shape[:2]
    maps = [np.concatenate([ghost_map(2), ghost_map(3)], 0), ghost_map(0)[:, :128], ghost_map(1)[:, 896:]]
    return pl.pallas_call(
        finish_kernel,
        grid=(count // CHUNK,),
        out_shape=jax.ShapeDtypeStruct(base.shape, jnp.float32),
        in_specs=[
            pl.BlockSpec((CHUNK, lev, 1024), lambda i: (i, 0, 0)),
            pl.BlockSpec((CHUNK * lev, 1024), lambda i: (i, 0)),
            VMEM,
            VMEM,
            VMEM,
        ],
        out_specs=pl.BlockSpec((CHUNK, lev, 1024), lambda i: (i, 0, 0)),
        compiler_params=PARAMS,
        cost_estimate=cost(2 * 10**9, 8 * 10**6),
        name="finish",
    )(base, ghosts, *[jnp.asarray(m) for m in maps])


def make_refined(slots, live, received):
    fine = slots.shape[1]
    lev = received.shape[1]
    size = next(n for n in (24, 16, 8, 6, 4, 2, 1) if fine % n == 0)
    return pl.pallas_call(
        refine_kernel,
        out_shape=jax.ShapeDtypeStruct((fine, lev, 1024), jnp.bfloat16),
        in_specs=[SMEM, SMEM, VMEM, VMEM],
        out_specs=HBM,
        scratch_shapes=[
            pltpu.VMEM((size * lev, 256), jnp.bfloat16),
            pltpu.VMEM((fine, lev, 1024), jnp.bfloat16),
            pltpu.SemaphoreType.DMA((fine // size,)),
        ],
        compiler_params=PARAMS,
        name="refine",
    )(slots, live, received, jnp.asarray(refine_table()))


def ghost_codes(nbr_block, nbr_side, nbr_flip, count, peers, here):
    rel = (nbr_block // count - here + 1 + peers) % peers
    rel = jnp.where(here % 2 == 0, 2 - rel, rel)
    swap = (nbr_side % 2) ^ nbr_flip
    near = rel * count + nbr_block % count
    return near * 8 + (nbr_side // 2) * 4 + swap * 2 + nbr_flip


def body(
    state,
    courant_row,
    courant_col,
    mixing,
    nbr_block,
    nbr_side,
    nbr_flip,
    send_idx,
    fine_slot,
    fine_count,
):
    peers = lax.axis_size("blocks")
    here = lax.axis_index("blocks")
    strips, edge = make_strips(state)
    first = [(i, i ^ 1) for i in range(peers)]
    second = [(i, (i + (1 if i % 2 else -1)) % peers) for i in range(peers)]
    before = lax.ppermute(strips, "blocks", first)
    after = lax.ppermute(strips, "blocks", second)
    edge = lax.ppermute(edge, "slab", [(0, 1), (1, 0)])
    coefs = (courant_row, courant_col, mixing)
    base, wins = make_local(coefs, state, edge)
    code = ghost_codes(nbr_block.T, nbr_side.T, nbr_flip.T, state.shape[0], peers, here)
    payload, ghosts = make_payload(code, send_idx[0].T, coefs, wins, (before, strips, after))
    received = lax.all_to_all(payload, "blocks", split_axis=0, concat_axis=0, tiled=True)
    advanced = make_advanced(base, ghosts)
    return advanced, make_refined(fine_slot, fine_count, received)


def solution(mesh):
    in_specs = (
        P("blocks", "slab", None),
        P("slab"),
        P("slab"),
        P("slab"),
        P("blocks", None),
        P("blocks", None),
        P("blocks", None),
        P("blocks", None, None),
        P("blocks", None),
        P("blocks"),
    )
    out_specs = (P("blocks", "slab", None), P("blocks", "slab", None))
    return jax.shard_map(body, mesh=mesh, in_specs=in_specs, out_specs=out_specs, check_vma=False)
```

```python
import functools

import jax
import jax.numpy as jnp
import ml_dtypes
import numpy as np
from jax import lax
from jax.experimental import pallas as pl
from jax.experimental.pallas import tpu as pltpu
from jax.sharding import PartitionSpec as P

CHUNK = 8
PACK = 128
REFINE = (32, 32, 32, 32, 32, 32)
VMEM_LIMIT = 24 * 1024 * 1024


def interp_1d():
    table = np.zeros((32, 8))
    for fine in range(32):
        x = (fine + 0.5) / 4.0
        start = min(max(int(np.floor(x - 0.5)) - 1, 0), 4)
        nodes = start + np.arange(4) + 0.5
        for a in range(4):
            weight = 1.0
            for b in range(4):
                if b != a:
                    weight *= (x - nodes[b]) / (nodes[a] - nodes[b])
            table[fine, start + a] = weight
    return table


def as_bf16(array):
    return np.asarray(array, np.float32).astype(ml_dtypes.bfloat16)


def refine_table():
    table = interp_1d()
    full = np.kron(table, table).T.astype(np.float32)
    high = as_bf16(full)
    low = as_bf16(full - high.astype(np.float32))
    return np.concatenate([high, low, high, low], 0)


def strip_cell(side, depth, t):
    line = depth if side in (0, 2) else 31 - depth
    return line * 32 + t if side < 2 else t * 32 + line


def ghost_map(side):
    first = side in (0, 2)
    out = np.zeros((128, 1024))
    for flip in range(2):
        for t in range(32):
            to = 31 - t if flip else t
            near = flip * 64 + t
            far = flip * 64 + 32 + t
            sign = 1.0 if first else -1.0
            out[near, strip_cell(side, 0, to)] += 8.0 * sign
            out[far, strip_cell(side, 0, to)] -= sign
            out[near, strip_cell(side, 1, to)] -= sign
    return as_bf16(np.concatenate([out, out], 0))


def window_order(table):
    out = np.zeros_like(table)
    for row in range(32):
        for col in range(32):
            to = (row // 8) * 256 + (col // 8) * 64 + (row % 8) * 8 + col % 8
            out[:, to] = table[:, row * 32 + col]
    return out


def stencil_map():
    own = np.zeros((128, 256))
    other = np.zeros((128, 256))
    weights = {-2: -1.0, -1: 8.0, 1: -8.0, 2: 1.0}
    for row in range(4):
        for col in range(32):
            lane = row * 32 + col
            for step, weight in weights.items():
                r = row + step
                if 0 <= r < 4:
                    own[r * 32 + col, lane] += weight
                else:
                    other[(r % 4) * 32 + col, lane] += weight
                c = col + step
                if 0 <= c < 32:
                    own[row * 32 + c, 128 + lane] += weight
    return as_bf16(np.concatenate([own, own, other, other], 0))


def window_map():
    pick = np.zeros((256, 256))
    for row in range(8):
        for col in range(32):
            pick[row * 32 + col, (col // 8) * 64 + row * 8 + col % 8] = 1.0
    return as_bf16(np.concatenate([pick, pick], 0))


def split(x):
    high = x.astype(jnp.bfloat16)
    low = (x - high.astype(jnp.float32)).astype(jnp.bfloat16)
    return high, low


def dot(a, b):
    return jnp.dot(a, b, preferred_element_type=jnp.float32)


def strips_kernel(state_ref, rows_ref, cols_ref, edge_ref, held, sems):
    slab = lax.axis_index("slab")
    count, lev = state_ref.shape[0], state_ref.shape[1]
    steps = count // CHUNK
    copies = []
    for i in range(steps):
        part = pl.ds(i * CHUNK, CHUNK)
        copies.append(pltpu.make_async_copy(state_ref.at[part], held.at[part], sems.at[i]))
        copies[i].start()
    cell = lax.broadcasted_iota(jnp.int32, (1024, 128), 0)
    to = lax.broadcasted_iota(jnp.int32, (1024, 128), 1)
    line = to // 32
    line = jnp.where(line < 2, line, 33 - line)
    pick = jnp.where((cell // 32 == to % 32) & (cell % 32 == line), 1.0, 0.0).astype(jnp.bfloat16)
    rows = CHUNK * lev
    lane = lax.broadcasted_iota(jnp.int32, (rows, 128), 1)
    for i in range(steps):
        copies[i].wait()
        part = slice(i * CHUNK, i * CHUNK + CHUNK)
        x = held[part]
        tail = x[:, :, 896:].reshape(rows, 128)
        tail = jnp.where((lane // 32) % 2 == 0, pltpu.roll(tail, 96, 1), pltpu.roll(tail, 32, 1))
        rows_ref[part] = jnp.where(lane < 64, x[:, :, :128].reshape(rows, 128), tail).reshape(CHUNK, lev, 128)
        high, low = split(x.reshape(rows, 1024))
        cols_ref[part] = (dot(high, pick) + dot(low, pick)).reshape(CHUNK, lev, 128)
        edge_ref[part] = jnp.where(slab == 0, x[:, lev - 1, :], x[:, 0, :])


def levels_of(ref, lev):
    at = lax.broadcasted_iota(jnp.int32, (lev, 128), 0)
    out = jnp.zeros((lev, 128), jnp.float32)
    for l in range(lev):
        out = jnp.where(at == l, ref[l], out)
    return out


def local_kernel(crow_ref, ccol_ref, mix_ref, state_ref, edge_ref, sten_ref, win_ref, base_ref, wins_ref):
    slab = lax.axis_index("slab")
    count, lev = state_ref.shape[0], state_ref.shape[1]
    a_row = levels_of(crow_ref, lev) * (1.0 / 12.0)
    a_col = levels_of(ccol_ref, lev) * (1.0 / 12.0)
    mix = levels_of(mix_ref, lev)
    rows = CHUNK * lev
    lane = lax.broadcasted_iota(jnp.int32, (rows, 128), 1)
    level = lax.broadcasted_iota(jnp.int32, (CHUNK, lev, 128), 1)
    zero = jnp.zeros((rows, 128), jnp.float32)

    def step(i, carry):
        blocks = pl.ds(pl.multiple_of(i * CHUNK, CHUNK), CHUNK)
        tiles = [state_ref[blocks, :, 128 * j : 128 * j + 128] for j in range(8)]
        flat = [t.reshape(rows, 128) for t in tiles]
        left = []
        for j in range(8):
            other = jnp.where(lane < 64, flat[j + 1] if j < 7 else zero, flat[j - 1] if j else zero)
            left.append(jnp.concatenate(split(flat[j]) + split(other), 1))
        diff = dot(jnp.concatenate(left, 0), sten_ref[...])
        done = []
        for j in range(8):
            lanes = slice(128 * j, 128 * j + 128)
            x = tiles[j]
            edge = edge_ref[blocks, lanes][:, None, :]
            below = jnp.where(level == 0, jnp.where(slab == 0, 0.0, edge), pltpu.roll(x, 1, 1))
            above = jnp.where(level == lev - 1, jnp.where(slab == 0, edge, 0.0), pltpu.roll(x, lev - 1, 1))
            vert = above - 2.0 * x + below
            d = diff[rows * j : rows * j + rows].reshape(CHUNK, lev, 256)
            out = x + a_row * d[:, :, :128] + a_col * d[:, :, 128:] + mix * vert
            base_ref[blocks, :, lanes] = out
            done.append(out.reshape(rows, 128))
        pairs = []
        for j in range(4):
            pairs.append(jnp.concatenate(split(jnp.concatenate(done[2 * j : 2 * j + 2], 1)), 1))
        w = dot(jnp.concatenate(pairs, 0), win_ref[...])
        for j in range(4):
            v = w[rows * j : rows * j + rows].reshape(CHUNK, lev, 256)
            wins_ref[blocks, 2 * j] = v[:, :, :128]
            wins_ref[blocks, 2 * j + 1] = v[:, :, 128:]
        return carry

    lax.fori_loop(0, count // CHUNK, step, 0)


def collect_strips(near_refs, near):
    for i, ref in enumerate(near_refs):
        near[i // 2, i % 2] = ref[...]


def gather_ghosts(i, code_ref, a_row, a_col, near, ghosts_ref):
    lev = near.shape[3]
    half = lax.broadcasted_iota(jnp.int32, (lev, 128), 1) // 64
    rows = CHUNK * lev
    for s in range(4):
        parts = []
        for n in range(CHUNK):
            code = code_ref[s, i * CHUNK + n]
            x = near[(code >> 3) & 3, (code >> 2) & 1, code >> 5]
            x = jnp.where((code & 2) == 0, x, pltpu.roll(x, 64, 1))
            parts.append(jnp.where(half == (code & 1), x, 0.0))
        x = jnp.stack(parts) * (a_row if s < 2 else a_col)
        high, low = split(x.reshape(rows, 128))
        ghosts_ref[:, s * 256 : s * 256 + 128] = high
        ghosts_ref[:, s * 256 + 128 : s * 256 + 256] = low


def pack_kernel(
    code_ref,
    send_ref,
    crow_ref,
    ccol_ref,
    base_ref,
    prev_rows,
    prev_cols,
    own_rows,
    own_cols,
    next_rows,
    next_cols,
    col0_ref,
    col1_ref,
    row0_ref,
    row1_ref,
    pay_ref,
    near,
    wins,
    *ghosts,
):
    count, lev = own_rows.shape[:2]
    half = lax.broadcasted_iota(jnp.int32, (lev, 128), 1) // 64
    collect_strips((prev_rows, prev_cols, own_rows, own_cols, next_rows, next_cols), near)
    a_row = levels_of(crow_ref, lev) * (1.0 / 12.0)
    a_col = levels_of(ccol_ref, lev) * (1.0 / 12.0)
    for i, held in enumerate(ghosts):
        gather_ghosts(i, code_ref, a_row, a_col, near, held)
        blocks = slice(i * CHUNK, i * CHUNK + CHUNK)
        row0 = dot(held[:, 0:256], row0_ref[...]).reshape(CHUNK, lev, 256)
        row1 = dot(held[:, 256:512], row1_ref[...]).reshape(CHUNK, lev, 256)
        for h, col_ref in enumerate((col0_ref, col1_ref)):
            c = dot(held[:, 512 + 256 * h : 768 + 256 * h], col_ref[...]).reshape(CHUNK, lev, 512)
            for j in range(4):
                v = base_ref[blocks, 2 * j + h] + c[:, :, 128 * j : 128 * j + 128]
                if j == 0:
                    v = v + row0[:, :, 128 * h : 128 * h + 128]
                if j == 3:
                    v = v + row1[:, :, 128 * h : 128 * h + 128]
                wins[blocks, 2 * j + h] = v

    def pack(d, carry):
        parts = []
        for k in range(2):
            w = send_ref[k, d]
            x = wins[w >> 4, (w >> 1) & 7]
            parts.append(jnp.where((w & 1) == k, x, pltpu.roll(x, 64, 1)))
        pay_ref[d] = jnp.where(half == 0, parts[0], parts[1])
        return carry

    lax.fori_loop(0, pay_ref.shape[0], pack, 0, unroll=PACK)


def finish_kernel(
    code_ref,
    crow_ref,
    ccol_ref,
    base_ref,
    prev_rows,
    prev_cols,
    own_rows,
    own_cols,
    next_rows,
    next_cols,
    col_ref,
    row0_ref,
    row1_ref,
    out_ref,
    near,
    held,
):
    lev = own_rows.shape[1]
    blocks = base_ref.shape[0]
    i = pl.program_id(0)

    @pl.when(i == 0)
    def _():
        collect_strips((prev_rows, prev_cols, own_rows, own_cols, next_rows, next_cols), near)

    a_row = levels_of(crow_ref, lev) * (1.0 / 12.0)
    a_col = levels_of(ccol_ref, lev) * (1.0 / 12.0)
    gather_ghosts(i, code_ref, a_row, a_col, near, held)
    c = dot(held[:, 512:1024], col_ref[...]).reshape(blocks, lev, 1024)
    out_ref[...] = base_ref[...] + c
    out_ref[:, :, :128] += dot(held[:, 0:256], row0_ref[...]).reshape(blocks, lev, 128)
    out_ref[:, :, 896:] += dot(held[:, 256:512], row1_ref[...]).reshape(blocks, lev, 128)


def refine_kernel(sizes, slot_ref, count_ref, recv_ref, table_ref, out_ref, held, sems, *parents):
    lev = recv_ref.shape[1]
    half = lax.broadcasted_iota(jnp.int32, (lev, 128), 1) // 64
    live = count_ref[0]
    copies, start = [], 0
    for i, size in enumerate(sizes):
        for n in range(size):
            slot = slot_ref[0, start + n]
            x = recv_ref[slot >> 1]
            x = jnp.where(half == (slot & 1), x, pltpu.roll(x, 64, 1))
            x = jnp.where(start + n < live, x, 0.0)
            high, low = split(x)
            parents[i][n * lev : (n + 1) * lev, :128] = high
            parents[i][n * lev : (n + 1) * lev, 128:] = low
        part = pl.ds(start, size)
        fine = dot(parents[i][...], table_ref[...])
        held[part] = fine.astype(jnp.bfloat16).reshape(size, lev, 1024)
        copies.append(pltpu.make_async_copy(held.at[part], out_ref.at[part], sems.at[i]))
        copies[i].start()
        start += size
    for copy in copies:
        copy.wait()


VMEM = pl.BlockSpec(memory_space=pltpu.VMEM)
SMEM = pl.BlockSpec(memory_space=pltpu.SMEM)
HBM = pl.BlockSpec(memory_space=pltpu.HBM)
PARAMS = pltpu.CompilerParams(vmem_limit_bytes=VMEM_LIMIT)


def cost(flops, size):
    return pl.CostEstimate(flops=flops, bytes_accessed=size, transcendentals=0)


def make_strips(state):
    count, lev = state.shape[:2]
    strip = jax.ShapeDtypeStruct((count, lev, 128), jnp.float32)
    return pl.pallas_call(
        strips_kernel,
        out_shape=(strip, strip, jax.ShapeDtypeStruct((count, 1024), jnp.float32)),
        in_specs=[HBM],
        out_specs=(VMEM, VMEM, VMEM),
        scratch_shapes=[pltpu.VMEM(state.shape, jnp.float32), pltpu.SemaphoreType.DMA((count // CHUNK,))],
        compiler_params=PARAMS,
        name="strips",
    )(pltpu.with_memory_space_constraint(state, pltpu.HBM))


def make_local(coefs, state, edge):
    count, lev = state.shape[:2]
    return pl.pallas_call(
        local_kernel,
        out_shape=(
            pltpu.HBM(state.shape, jnp.float32),
            jax.ShapeDtypeStruct((count, 8, lev, 128), jnp.float32),
        ),
        in_specs=[SMEM] * 3 + [VMEM] * 4,
        out_specs=(VMEM, VMEM),
        compiler_params=PARAMS,
        cost_estimate=cost(4 * 10**9, 8 * 10**6),
        name="local",
    )(*coefs, state, edge, jnp.asarray(stencil_map()), jnp.asarray(window_map()))


def make_payload(code, send, coefs, base, nearby):
    count, lev = base.shape[0], base.shape[2]
    sides = [window_order(ghost_map(s)) for s in range(4)]
    cols = [m.reshape(256, 4, 256)[:, :, 128 * h : 128 * h + 128].reshape(256, 512) for h, m in enumerate(sides[2:])]
    maps = cols + [sides[0][:, :256], sides[1][:, 768:]]
    return pl.pallas_call(
        pack_kernel,
        out_shape=jax.ShapeDtypeStruct((send.shape[1], lev, 128), jnp.float32),
        in_specs=[SMEM] * 4 + [VMEM] * 11,
        out_specs=VMEM,
        scratch_shapes=[
            pltpu.VMEM((3, 2, count, lev, 128), jnp.float32),
            pltpu.VMEM((count, 8, lev, 128), jnp.float32),
            *[pltpu.VMEM((CHUNK * lev, 1024), jnp.bfloat16)] * (count // CHUNK),
        ],
        compiler_params=PARAMS,
        cost_estimate=cost(10**9, 8 * 10**6),
        name="pack",
    )(code, send, *coefs[:2], base, *nearby, *[jnp.asarray(m) for m in maps])


def make_advanced(code, coefs, base, nearby):
    count, lev = base.shape[:2]
    maps = [np.concatenate([ghost_map(2), ghost_map(3)], 0), ghost_map(0)[:, :128], ghost_map(1)[:, 896:]]
    block = pl.BlockSpec((CHUNK, lev, 1024), lambda i: (i, 0, 0))
    return pl.pallas_call(
        finish_kernel,
        grid=(count // CHUNK,),
        out_shape=jax.ShapeDtypeStruct(base.shape, jnp.float32),
        in_specs=[SMEM] * 3 + [block] + [VMEM] * 9,
        out_specs=block,
        scratch_shapes=[
            pltpu.VMEM((3, 2, count, lev, 128), jnp.float32),
            pltpu.VMEM((CHUNK * lev, 1024), jnp.bfloat16),
        ],
        compiler_params=PARAMS,
        cost_estimate=cost(2 * 10**9, 8 * 10**6),
        name="finish",
    )(code, *coefs[:2], base, *nearby, *[jnp.asarray(m) for m in maps])


def make_refined(slots, live, received):
    fine = slots.shape[1]
    lev = received.shape[1]
    sizes = []
    for size in REFINE + (fine,) * fine:
        if sum(sizes) < fine:
            sizes.append(min(size, fine - sum(sizes)))
    return pl.pallas_call(
        functools.partial(refine_kernel, tuple(sizes)),
        out_shape=jax.ShapeDtypeStruct((fine, lev, 1024), jnp.bfloat16),
        in_specs=[SMEM, SMEM, VMEM, VMEM],
        out_specs=HBM,
        scratch_shapes=[
            pltpu.VMEM((fine, lev, 1024), jnp.bfloat16),
            pltpu.SemaphoreType.DMA((len(sizes),)),
            *[pltpu.VMEM((size * lev, 256), jnp.bfloat16) for size in sizes],
        ],
        compiler_params=PARAMS,
        name="refine",
    )(slots, live, received, jnp.asarray(refine_table()))


def ghost_codes(nbr_block, nbr_side, nbr_flip, count, peers, here):
    rel = (nbr_block // count - here + 1 + peers) % peers
    rel = jnp.where(here % 2 == 0, rel, 2 - rel)
    swap = (nbr_side % 2) ^ nbr_flip
    return nbr_block % count * 32 + rel * 8 + nbr_side // 2 * 4 + swap * 2 + nbr_flip


def body(
    state,
    courant_row,
    courant_col,
    mixing,
    nbr_block,
    nbr_side,
    nbr_flip,
    send_idx,
    fine_slot,
    fine_count,
):
    peers = lax.axis_size("blocks")
    here = lax.axis_index("blocks")
    rows, cols, edge = make_strips(state)
    first = [(i, (i + (1 if i % 2 else -1)) % peers) for i in range(peers)]
    second = [(i, i ^ 1) for i in range(peers)]
    other = [lax.ppermute(s, "blocks", first) for s in (rows, cols)]
    after = [lax.ppermute(s, "blocks", second) for s in (rows, cols)]
    nearby = (*other, rows, cols, *after)
    edge = lax.ppermute(edge, "slab", [(0, 1), (1, 0)])
    coefs = (courant_row, courant_col, mixing)
    base, wins = make_local(coefs, state, edge)
    code = ghost_codes(nbr_block.T, nbr_side.T, nbr_flip.T, state.shape[0], peers, here)
    payload = make_payload(code, send_idx[0].T, coefs, wins, nearby)
    received = lax.all_to_all(payload, "blocks", split_axis=0, concat_axis=0, tiled=True)
    advanced = make_advanced(code, coefs, base, nearby)
    return advanced, make_refined(fine_slot, fine_count, received)


def solution(mesh):
    in_specs = (
        P("blocks", "slab", None),
        P("slab"),
        P("slab"),
        P("slab"),
        P("blocks", None),
        P("blocks", None),
        P("blocks", None),
        P("blocks", None, None),
        P("blocks", None),
        P("blocks"),
    )
    out_specs = (P("blocks", "slab", None), P("blocks", "slab", None))
    return jax.shard_map(body, mesh=mesh, in_specs=in_specs, out_specs=out_specs, check_vma=False)
```

```python
import functools

import jax
import jax.numpy as jnp
import ml_dtypes
import numpy as np
from jax import lax
from jax.experimental import pallas as pl
from jax.experimental.pallas import tpu as pltpu
from jax.sharding import PartitionSpec as P

CHUNK = 8
REFINE = (32, 32, 32, 32, 32, 32)
VMEM_LIMIT = 24 * 1024 * 1024


def interp_1d():
    table = np.zeros((32, 8))
    for fine in range(32):
        x = (fine + 0.5) / 4.0
        start = min(max(int(np.floor(x - 0.5)) - 1, 0), 4)
        nodes = start + np.arange(4) + 0.5
        for a in range(4):
            weight = 1.0
            for b in range(4):
                if b != a:
                    weight *= (x - nodes[b]) / (nodes[a] - nodes[b])
            table[fine, start + a] = weight
    return table


def as_bf16(array):
    return np.asarray(array, np.float32).astype(ml_dtypes.bfloat16)


def refine_table():
    table = interp_1d()
    full = np.kron(table, table).T.astype(np.float32)
    high = as_bf16(full)
    low = as_bf16(full - high.astype(np.float32))
    return np.concatenate([high, low, high, low], 0)


def strip_cell(side, depth, t):
    line = depth if side in (0, 2) else 31 - depth
    return line * 32 + t if side < 2 else t * 32 + line


def ghost_map(side):
    first = side in (0, 2)
    out = np.zeros((128, 1024))
    for flip in range(2):
        for t in range(32):
            to = 31 - t if flip else t
            near = flip * 64 + t
            far = flip * 64 + 32 + t
            sign = 1.0 if first else -1.0
            out[near, strip_cell(side, 0, to)] += 8.0 * sign
            out[far, strip_cell(side, 0, to)] -= sign
            out[near, strip_cell(side, 1, to)] -= sign
    return as_bf16(np.concatenate([out, out], 0))


def window_order(table):
    out = np.zeros_like(table)
    for row in range(32):
        for col in range(32):
            to = (row // 8) * 256 + (col // 8) * 64 + (row % 8) * 8 + col % 8
            out[:, to] = table[:, row * 32 + col]
    return out


def stencil_map():
    own = np.zeros((128, 256))
    other = np.zeros((128, 256))
    weights = {-2: -1.0, -1: 8.0, 1: -8.0, 2: 1.0}
    for row in range(4):
        for col in range(32):
            lane = row * 32 + col
            for step, weight in weights.items():
                r = row + step
                if 0 <= r < 4:
                    own[r * 32 + col, lane] += weight
                else:
                    other[(r % 4) * 32 + col, lane] += weight
                c = col + step
                if 0 <= c < 32:
                    own[row * 32 + c, 128 + lane] += weight
    return as_bf16(np.concatenate([own, own, other, other], 0))


def window_map():
    pick = np.zeros((256, 256))
    for row in range(8):
        for col in range(32):
            pick[row * 32 + col, (col // 8) * 64 + row * 8 + col % 8] = 1.0
    return as_bf16(np.concatenate([pick, pick], 0))


def split(x):
    high = x.astype(jnp.bfloat16)
    low = (x - high.astype(jnp.float32)).astype(jnp.bfloat16)
    return high, low


def dot(a, b):
    return jnp.dot(a, b, preferred_element_type=jnp.float32)


def rows_kernel(state_ref, rows_ref, held, sems):
    count, lev = state_ref.shape[0], state_ref.shape[1]
    copies = []
    for i in range(4):
        part = pl.ds(i // 2 * (count // 2), count // 2)
        lanes = pl.ds(i % 2 * 896, 128)
        copies.append(pltpu.make_async_copy(state_ref.at[part, :, lanes], held.at[i % 2, part], sems.at[i]))
        copies[i].start()
    for copy in copies:
        copy.wait()
    lane = lax.broadcasted_iota(jnp.int32, (count * lev, 128), 1)
    tail = held[1].reshape(count * lev, 128)
    tail = jnp.where((lane // 32) % 2 == 0, pltpu.roll(tail, 96, 1), pltpu.roll(tail, 32, 1))
    rows_ref[...] = jnp.where(lane < 64, held[0].reshape(count * lev, 128), tail).reshape(count, lev, 128)


def cols_kernel(state_ref, cols_ref, edge_ref):
    slab = lax.axis_index("slab")
    count, lev = state_ref.shape[0], state_ref.shape[1]
    cell = lax.broadcasted_iota(jnp.int32, (1024, 128), 0)
    to = lax.broadcasted_iota(jnp.int32, (1024, 128), 1)
    line = to // 32
    line = jnp.where(line < 2, line, 33 - line)
    pick = jnp.where((cell // 32 == to % 32) & (cell % 32 == line), 1.0, 0.0).astype(jnp.bfloat16)
    size = 2 * CHUNK
    for i in range(count // size):
        part = slice(i * size, i * size + size)
        x = state_ref[part]
        high, low = split(x.reshape(size * lev, 1024))
        cols_ref[part] = (dot(high, pick) + dot(low, pick)).reshape(size, lev, 128)
        edge_ref[part] = jnp.where(slab == 0, x[:, lev - 1, :], x[:, 0, :])


def levels_of(ref, lev):
    at = lax.broadcasted_iota(jnp.int32, (lev, 128), 0)
    out = jnp.zeros((lev, 128), jnp.float32)
    for l in range(lev):
        out = jnp.where(at == l, ref[l], out)
    return out


def local_part(blocks, crow_ref, ccol_ref, mix_ref, state_ref, edge_ref, sten_ref):
    slab = lax.axis_index("slab")
    lev = state_ref.shape[1]
    a_row = levels_of(crow_ref, lev) * (1.0 / 12.0)
    a_col = levels_of(ccol_ref, lev) * (1.0 / 12.0)
    mix = levels_of(mix_ref, lev)
    rows = CHUNK * lev
    lane = lax.broadcasted_iota(jnp.int32, (rows, 128), 1)
    level = lax.broadcasted_iota(jnp.int32, (CHUNK, lev, 128), 1)
    zero = jnp.zeros((rows, 128), jnp.float32)
    tiles = [state_ref[blocks, :, 128 * j : 128 * j + 128] for j in range(8)]
    flat = [t.reshape(rows, 128) for t in tiles]
    left = []
    for j in range(8):
        other = jnp.where(lane < 64, flat[j + 1] if j < 7 else zero, flat[j - 1] if j else zero)
        left.append(jnp.concatenate(split(flat[j]) + split(other), 1))
    diff = dot(jnp.concatenate(left, 0), sten_ref[...])
    done = []
    for j in range(8):
        x = tiles[j]
        edge = edge_ref[blocks, 128 * j : 128 * j + 128][:, None, :]
        below = jnp.where(level == 0, jnp.where(slab == 0, 0.0, edge), pltpu.roll(x, 1, 1))
        above = jnp.where(level == lev - 1, jnp.where(slab == 0, edge, 0.0), pltpu.roll(x, lev - 1, 1))
        vert = above - 2.0 * x + below
        d = diff[rows * j : rows * j + rows].reshape(CHUNK, lev, 256)
        done.append(x + a_row * d[:, :, :128] + a_col * d[:, :, 128:] + mix * vert)
    return done


def local_kernel(
    crow_ref,
    ccol_ref,
    mix_ref,
    block_ref,
    side_ref,
    flip_ref,
    state_ref,
    edge_ref,
    sten_ref,
    win_ref,
    wins_ref,
    code_ref,
    base_ref,
    sten,
    win,
    kept,
    sems,
    base_sems,
):
    copies = []
    for i, (ref, held) in enumerate(((sten_ref, sten), (win_ref, win))):
        for n in range(2):
            part = pl.ds(n * 256, 256)
            copies.append(pltpu.make_async_copy(ref.at[part], held.at[part], sems.at[2 * i + n]))
            copies[-1].start()
    count, lev = state_ref.shape[0], state_ref.shape[1]
    here, peers = lax.axis_index("blocks"), lax.axis_size("blocks")
    block, side, flip = block_ref[...], side_ref[...], flip_ref[...]
    rel = (block >> 5) - here + 1
    rel = jnp.where(rel < 0, rel + peers, rel)
    rel = jnp.where(rel >= peers, rel - peers, rel)
    rel = jnp.where((here & 1) == 0, rel, 2 - rel)
    swap = (side & 1) ^ flip
    code_ref[...] = (block & 31) * 32 + rel * 8 + (side >> 1) * 4 + swap * 2 + flip
    for copy in copies:
        copy.wait()
    rows = CHUNK * lev

    def base_copy(i):
        blocks = pl.ds(i * CHUNK, CHUNK)
        return pltpu.make_async_copy(kept.at[blocks], base_ref.at[blocks], base_sems.at[i])

    def step(i, carry):
        blocks = pl.ds(pl.multiple_of(i * CHUNK, CHUNK), CHUNK)
        done = local_part(blocks, crow_ref, ccol_ref, mix_ref, state_ref, edge_ref, sten)
        for j in range(8):
            kept[blocks, :, 128 * j : 128 * j + 128] = done[j]
        base_copy(i).start()
        pairs = []
        for j in range(4):
            pair = [t.reshape(rows, 128) for t in done[2 * j : 2 * j + 2]]
            pairs.append(jnp.concatenate(split(jnp.concatenate(pair, 1)), 1))
        w = dot(jnp.concatenate(pairs, 0), win[...])
        for j in range(4):
            v = w[rows * j : rows * j + rows].reshape(CHUNK, lev, 256)
            wins_ref[blocks, 2 * j] = v[:, :, :128]
            wins_ref[blocks, 2 * j + 1] = v[:, :, 128:]
        return carry

    lax.fori_loop(0, count // CHUNK, step, 0)
    for i in range(count // CHUNK):
        base_copy(i).wait()


def collect_strips(near_refs, near):
    for i, ref in enumerate(near_refs):
        near[i // 2, i % 2] = ref[...]


def gather_ghosts(i, code_ref, a_row, a_col, near, ghosts_ref):
    lev = near.shape[3]
    half = lax.broadcasted_iota(jnp.int32, (lev, 128), 1) // 64
    rows = CHUNK * lev
    for s in range(4):
        parts = []
        for n in range(CHUNK):
            code = code_ref[s, i * CHUNK + n]
            x = near[(code >> 3) & 3, (code >> 2) & 1, code >> 5]
            x = jnp.where((code & 2) == 0, x, pltpu.roll(x, 64, 1))
            parts.append(jnp.where(half == (code & 1), x, 0.0))
        x = jnp.stack(parts) * (a_row if s < 2 else a_col)
        high, low = split(x.reshape(rows, 128))
        ghosts_ref[:, s * 256 : s * 256 + 128] = high
        ghosts_ref[:, s * 256 + 128 : s * 256 + 256] = low


def pack_kernel(
    code_ref,
    send_ref,
    crow_ref,
    ccol_ref,
    base_ref,
    prev_rows,
    prev_cols,
    own_rows,
    own_cols,
    next_rows,
    next_cols,
    col0_ref,
    col1_ref,
    row0_ref,
    row1_ref,
    pay_ref,
    ghosts_ref,
    near,
    wins,
    held_pay,
    pay_sems,
    ghost_sems,
    *ghosts,
):
    count, lev = own_rows.shape[:2]
    half = lax.broadcasted_iota(jnp.int32, (lev, 128), 1) // 64
    collect_strips((prev_rows, prev_cols, own_rows, own_cols, next_rows, next_cols), near)
    a_row = levels_of(crow_ref, lev) * (1.0 / 12.0)
    a_col = levels_of(ccol_ref, lev) * (1.0 / 12.0)
    copies = []
    for i, held in enumerate(ghosts):
        gather_ghosts(i, code_ref, a_row, a_col, near, held)
        rows = pl.ds(i * CHUNK * lev, CHUNK * lev)
        copies.append(pltpu.make_async_copy(held, ghosts_ref.at[rows], ghost_sems.at[i]))
        copies[i].start()
        blocks = slice(i * CHUNK, i * CHUNK + CHUNK)
        row0 = dot(held[:, 0:256], row0_ref[...]).reshape(CHUNK, lev, 256)
        row1 = dot(held[:, 256:512], row1_ref[...]).reshape(CHUNK, lev, 256)
        for h, col_ref in enumerate((col0_ref, col1_ref)):
            c = dot(held[:, 512 + 256 * h : 768 + 256 * h], col_ref[...]).reshape(CHUNK, lev, 512)
            for j in range(4):
                v = base_ref[blocks, 2 * j + h] + c[:, :, 128 * j : 128 * j + 128]
                if j == 0:
                    v = v + row0[:, :, 128 * h : 128 * h + 128]
                if j == 3:
                    v = v + row1[:, :, 128 * h : 128 * h + 128]
                wins[blocks, 2 * j + h] = v

    size = pay_ref.shape[0] // pay_sems.shape[0]
    for i in range(pay_sems.shape[0]):
        for d in range(i * size, i * size + size):
            parts = []
            for k in range(2):
                w = send_ref[k, d]
                x = wins[w >> 4, (w >> 1) & 7]
                parts.append(jnp.where((w & 1) == k, x, pltpu.roll(x, 64, 1)))
            held_pay[d] = jnp.where(half == 0, parts[0], parts[1])
        part = pl.ds(i * size, size)
        copies.append(pltpu.make_async_copy(held_pay.at[part], pay_ref.at[part], pay_sems.at[i]))
        copies[-1].start()
    for copy in copies:
        copy.wait()


def finish_kernel(base_ref, ghosts_ref, col_ref, row0_ref, row1_ref, out_ref):
    blocks, lev = base_ref.shape[:2]
    c = dot(ghosts_ref[:, 512:1024], col_ref[...])
    row0 = dot(ghosts_ref[:, 0:256], row0_ref[...])
    row1 = dot(ghosts_ref[:, 256:512], row1_ref[...])
    for j in range(8):
        v = c[:, 128 * j : 128 * j + 128]
        if j == 0:
            v = v + row0
        if j == 7:
            v = v + row1
        lanes = slice(128 * j, 128 * j + 128)
        out_ref[:, :, lanes] = base_ref[:, :, lanes] + v.reshape(blocks, lev, 128)


def refine_kernel(sizes, slot_ref, count_ref, recv_ref, table_ref, out_ref, held, sems, *parents):
    lev = recv_ref.shape[1]
    half = lax.broadcasted_iota(jnp.int32, (lev, 128), 1) // 64
    live = count_ref[0]
    copies, start = [], 0
    for i, size in enumerate(sizes):
        for n in range(size):
            slot = slot_ref[0, start + n]
            x = recv_ref[slot >> 1]
            x = jnp.where(half == (slot & 1), x, pltpu.roll(x, 64, 1))
            x = jnp.where(start + n < live, x, 0.0)
            high, low = split(x)
            parents[i][n * lev : (n + 1) * lev, :128] = high
            parents[i][n * lev : (n + 1) * lev, 128:] = low
        part = pl.ds(start, size)
        fine = dot(parents[i][...], table_ref[...])
        held[part] = fine.astype(jnp.bfloat16).reshape(size, lev, 1024)
        copies.append(pltpu.make_async_copy(held.at[part], out_ref.at[part], sems.at[i]))
        copies[i].start()
        start += size
    for copy in copies:
        copy.wait()


VMEM = pl.BlockSpec(memory_space=pltpu.VMEM)
SMEM = pl.BlockSpec(memory_space=pltpu.SMEM)
HBM = pl.BlockSpec(memory_space=pltpu.HBM)
PARAMS = pltpu.CompilerParams(vmem_limit_bytes=VMEM_LIMIT)


def cost(flops, size):
    return pl.CostEstimate(flops=flops, bytes_accessed=size, transcendentals=0)


def make_rows(state):
    count, lev = state.shape[:2]
    return pl.pallas_call(
        rows_kernel,
        out_shape=jax.ShapeDtypeStruct((count, lev, 128), jnp.float32),
        in_specs=[HBM],
        out_specs=VMEM,
        scratch_shapes=[pltpu.VMEM((2, count, lev, 128), jnp.float32), pltpu.SemaphoreType.DMA((4,))],
        compiler_params=PARAMS,
        name="rows",
    )(pltpu.with_memory_space_constraint(state, pltpu.HBM))


def make_cols(state):
    count, lev = state.shape[:2]
    return pl.pallas_call(
        cols_kernel,
        out_shape=(
            jax.ShapeDtypeStruct((count, lev, 128), jnp.float32),
            jax.ShapeDtypeStruct((count, 1024), jnp.float32),
        ),
        in_specs=[VMEM],
        out_specs=(VMEM, VMEM),
        compiler_params=PARAMS,
        name="cols",
    )(state)


def make_local(coefs, tables, state, edge):
    count, lev = state.shape[:2]
    maps = [pltpu.with_memory_space_constraint(jnp.asarray(m), pltpu.HBM) for m in (stencil_map(), window_map())]
    return pl.pallas_call(
        local_kernel,
        out_shape=(
            jax.ShapeDtypeStruct((count, 8, lev, 128), jnp.float32),
            jax.ShapeDtypeStruct(tables[0].shape, jnp.int32),
            pltpu.HBM(state.shape, jnp.float32),
        ),
        in_specs=[SMEM] * 3 + [VMEM] * 5 + [HBM] * 2,
        out_specs=(VMEM, VMEM, HBM),
        scratch_shapes=[
            pltpu.VMEM(maps[0].shape, jnp.bfloat16),
            pltpu.VMEM(maps[1].shape, jnp.bfloat16),
            pltpu.VMEM(state.shape, jnp.float32),
            pltpu.SemaphoreType.DMA((4,)),
            pltpu.SemaphoreType.DMA((count // CHUNK,)),
        ],
        compiler_params=PARAMS,
        cost_estimate=cost(10**3, 10**3),
        name="local",
    )(*coefs, *tables, state, edge, *maps)


def make_payload(code, send, coefs, base, nearby):
    count, lev, peers = base.shape[0], base.shape[2], send.shape[1]
    sides = [window_order(ghost_map(s)) for s in range(4)]
    cols = [m.reshape(256, 4, 256)[:, :, 128 * h : 128 * h + 128].reshape(256, 512) for h, m in enumerate(sides[2:])]
    maps = cols + [sides[0][:, :256], sides[1][:, 768:]]
    return pl.pallas_call(
        pack_kernel,
        out_shape=(
            pltpu.HBM((peers, lev, 128), jnp.float32),
            pltpu.HBM((count * lev, 1024), jnp.bfloat16),
        ),
        in_specs=[SMEM] * 4 + [VMEM] * 11,
        out_specs=(HBM, HBM),
        scratch_shapes=[
            pltpu.VMEM((3, 2, count, lev, 128), jnp.float32),
            pltpu.VMEM((count, 8, lev, 128), jnp.float32),
            pltpu.VMEM((peers, lev, 128), jnp.float32),
            pltpu.SemaphoreType.DMA((4,)),
            pltpu.SemaphoreType.DMA((count // CHUNK,)),
            *[pltpu.VMEM((CHUNK * lev, 1024), jnp.bfloat16)] * (count // CHUNK),
        ],
        compiler_params=PARAMS,
        cost_estimate=cost(10**9, 8 * 10**6),
        name="pack",
    )(code, send, *coefs[:2], base, *nearby, *[jnp.asarray(m) for m in maps])


def make_advanced(base, ghosts):
    count, lev = base.shape[:2]
    maps = [np.concatenate([ghost_map(2), ghost_map(3)], 0), ghost_map(0)[:, :128], ghost_map(1)[:, 896:]]
    block = pl.BlockSpec((CHUNK, lev, 1024), lambda i: (i, 0, 0))
    return pl.pallas_call(
        finish_kernel,
        grid=(count // CHUNK,),
        out_shape=jax.ShapeDtypeStruct(base.shape, jnp.float32),
        in_specs=[block, pl.BlockSpec((CHUNK * lev, 1024), lambda i: (i, 0))] + [VMEM] * 3,
        out_specs=block,
        compiler_params=PARAMS,
        cost_estimate=cost(2 * 10**9, 8 * 10**6),
        name="finish",
    )(
        pltpu.with_memory_space_constraint(base, pltpu.HBM),
        pltpu.with_memory_space_constraint(ghosts, pltpu.HBM),
        *[jnp.asarray(m) for m in maps],
    )


def make_refined(slots, live, received):
    fine = slots.shape[1]
    lev = received.shape[1]
    sizes = []
    for size in REFINE + (fine,) * fine:
        if sum(sizes) < fine:
            sizes.append(min(size, fine - sum(sizes)))
    return pl.pallas_call(
        functools.partial(refine_kernel, tuple(sizes)),
        out_shape=jax.ShapeDtypeStruct((fine, lev, 1024), jnp.bfloat16),
        in_specs=[SMEM, SMEM, VMEM, VMEM],
        out_specs=HBM,
        scratch_shapes=[
            pltpu.VMEM((fine, lev, 1024), jnp.bfloat16),
            pltpu.SemaphoreType.DMA((len(sizes),)),
            *[pltpu.VMEM((size * lev, 256), jnp.bfloat16) for size in sizes],
        ],
        compiler_params=PARAMS,
        name="refine",
    )(slots, live, received, jnp.asarray(refine_table()))


def body(
    state,
    courant_row,
    courant_col,
    mixing,
    nbr_block,
    nbr_side,
    nbr_flip,
    send_idx,
    fine_slot,
    fine_count,
):
    peers = lax.axis_size("blocks")
    first = [(i, (i + (1 if i % 2 else -1)) % peers) for i in range(peers)]
    second = [(i, i ^ 1) for i in range(peers)]
    rows = make_rows(state)
    cols, edge = make_cols(state)
    near_rows = lax.ppermute(rows, "blocks", second)
    near_cols = lax.ppermute(cols, "blocks", second)
    far_rows = lax.ppermute(rows, "blocks", first)
    far_cols = lax.ppermute(cols, "blocks", first)
    nearby = (far_rows, far_cols, rows, cols, near_rows, near_cols)
    edge = lax.ppermute(edge, "slab", [(0, 1), (1, 0)])
    coefs = (courant_row, courant_col, mixing)
    wins, code, base = make_local(coefs, (nbr_block.T, nbr_side.T, nbr_flip.T), state, edge)
    payload, ghosts = make_payload(code, send_idx[0].T, coefs, wins, nearby)
    received = lax.all_to_all(payload, "blocks", split_axis=0, concat_axis=0, tiled=True)
    advanced = make_advanced(base, ghosts)
    return advanced, make_refined(fine_slot, fine_count, received)


def solution(mesh):
    in_specs = (
        P("blocks", "slab", None),
        P("slab"),
        P("slab"),
        P("slab"),
        P("blocks", None),
        P("blocks", None),
        P("blocks", None),
        P("blocks", None, None),
        P("blocks", None),
        P("blocks"),
    )
    out_specs = (P("blocks", "slab", None), P("blocks", "slab", None))
    return jax.shard_map(body, mesh=mesh, in_specs=in_specs, out_specs=out_specs, check_vma=False)
```

```python
import functools

import jax
import jax.numpy as jnp
import ml_dtypes
import numpy as np
from jax import lax
from jax.experimental import pallas as pl
from jax.experimental.pallas import tpu as pltpu
from jax.sharding import PartitionSpec as P

CHUNK = 8
REFINE = (32, 32, 32, 32, 32, 32)
VMEM_LIMIT = 24 * 1024 * 1024


def interp_1d():
    table = np.zeros((32, 8))
    for fine in range(32):
        x = (fine + 0.5) / 4.0
        start = min(max(int(np.floor(x - 0.5)) - 1, 0), 4)
        nodes = start + np.arange(4) + 0.5
        for a in range(4):
            weight = 1.0
            for b in range(4):
                if b != a:
                    weight *= (x - nodes[b]) / (nodes[a] - nodes[b])
            table[fine, start + a] = weight
    return table


def as_bf16(array):
    return np.asarray(array, np.float32).astype(ml_dtypes.bfloat16)


def refine_table():
    table = interp_1d()
    full = np.kron(table, table).T.astype(np.float32)
    high = as_bf16(full)
    low = as_bf16(full - high.astype(np.float32))
    return np.concatenate([high, low, high, low], 0)


def strip_cell(side, depth, t):
    line = depth if side in (0, 2) else 31 - depth
    return line * 32 + t if side < 2 else t * 32 + line


def ghost_map(side):
    first = side in (0, 2)
    out = np.zeros((128, 1024))
    for flip in range(2):
        for t in range(32):
            to = 31 - t if flip else t
            near = flip * 64 + t
            far = flip * 64 + 32 + t
            sign = 1.0 if first else -1.0
            out[near, strip_cell(side, 0, to)] += 8.0 * sign
            out[far, strip_cell(side, 0, to)] -= sign
            out[near, strip_cell(side, 1, to)] -= sign
    return as_bf16(np.concatenate([out, out], 0))


def window_order(table):
    out = np.zeros_like(table)
    for row in range(32):
        for col in range(32):
            to = (row // 8) * 256 + (col // 8) * 64 + (row % 8) * 8 + col % 8
            out[:, to] = table[:, row * 32 + col]
    return out


def stencil_map():
    own = np.zeros((128, 256))
    other = np.zeros((128, 256))
    weights = {-2: -1.0, -1: 8.0, 1: -8.0, 2: 1.0}
    for row in range(4):
        for col in range(32):
            lane = row * 32 + col
            for step, weight in weights.items():
                r = row + step
                if 0 <= r < 4:
                    own[r * 32 + col, lane] += weight
                else:
                    other[(r % 4) * 32 + col, lane] += weight
                c = col + step
                if 0 <= c < 32:
                    own[row * 32 + c, 128 + lane] += weight
    return as_bf16(np.concatenate([own, own, other, other], 0))


def window_map():
    pick = np.zeros((256, 256))
    for row in range(8):
        for col in range(32):
            pick[row * 32 + col, (col // 8) * 64 + row * 8 + col % 8] = 1.0
    return as_bf16(np.concatenate([pick, pick], 0))


def split(x):
    high = x.astype(jnp.bfloat16)
    low = (x - high.astype(jnp.float32)).astype(jnp.bfloat16)
    return high, low


def dot(a, b):
    return jnp.dot(a, b, preferred_element_type=jnp.float32)


def strips_kernel(state_ref, strips_ref, edge_ref, held, sems):
    slab = lax.axis_index("slab")
    count, lev = state_ref.shape[0], state_ref.shape[1]
    size = count // sems.shape[0]
    copies = []
    for i in range(sems.shape[0]):
        part = pl.ds(i * size, size)
        copies.append(pltpu.make_async_copy(state_ref.at[part], held.at[part], sems.at[i]))
        copies[i].start()
    cell = lax.broadcasted_iota(jnp.int32, (1024, 128), 0)
    to = lax.broadcasted_iota(jnp.int32, (1024, 128), 1)
    line = to // 32
    line = jnp.where(line < 2, line, 33 - line)
    pick = jnp.where((cell // 32 == to % 32) & (cell % 32 == line), 1.0, 0.0).astype(jnp.bfloat16)
    rows = size * lev
    lane = lax.broadcasted_iota(jnp.int32, (rows, 128), 1)
    for i in range(sems.shape[0]):
        copies[i].wait()
        part = slice(i * size, i * size + size)
        x = held[part]
        tail = x[:, :, 896:].reshape(rows, 128)
        tail = jnp.where((lane // 32) % 2 == 0, pltpu.roll(tail, 96, 1), pltpu.roll(tail, 32, 1))
        strips_ref[part, 0] = jnp.where(lane < 64, x[:, :, :128].reshape(rows, 128), tail).reshape(size, lev, 128)
        high, low = split(x.reshape(rows, 1024))
        strips_ref[part, 1] = (dot(high, pick) + dot(low, pick)).reshape(size, lev, 128)
        edge_ref[part] = jnp.where(slab == 0, x[:, lev - 1, :], x[:, 0, :])


def levels_of(ref, lev):
    at = lax.broadcasted_iota(jnp.int32, (lev, 128), 0)
    out = jnp.zeros((lev, 128), jnp.float32)
    for l in range(lev):
        out = jnp.where(at == l, ref[l], out)
    return out


def local_part(blocks, crow_ref, ccol_ref, mix_ref, state_ref, edge_ref, sten_ref):
    slab = lax.axis_index("slab")
    lev = state_ref.shape[1]
    a_row = levels_of(crow_ref, lev) * (1.0 / 12.0)
    a_col = levels_of(ccol_ref, lev) * (1.0 / 12.0)
    mix = levels_of(mix_ref, lev)
    rows = CHUNK * lev
    lane = lax.broadcasted_iota(jnp.int32, (rows, 128), 1)
    level = lax.broadcasted_iota(jnp.int32, (CHUNK, lev, 128), 1)
    zero = jnp.zeros((rows, 128), jnp.float32)
    tiles = [state_ref[blocks, :, 128 * j : 128 * j + 128] for j in range(8)]
    flat = [t.reshape(rows, 128) for t in tiles]
    left = []
    for j in range(8):
        other = jnp.where(lane < 64, flat[j + 1] if j < 7 else zero, flat[j - 1] if j else zero)
        left.append(jnp.concatenate(split(flat[j]) + split(other), 1))
    diff = dot(jnp.concatenate(left, 0), sten_ref[...])
    done = []
    for j in range(8):
        x = tiles[j]
        edge = edge_ref[blocks, 128 * j : 128 * j + 128][:, None, :]
        below = jnp.where(level == 0, jnp.where(slab == 0, 0.0, edge), pltpu.roll(x, 1, 1))
        above = jnp.where(level == lev - 1, jnp.where(slab == 0, edge, 0.0), pltpu.roll(x, lev - 1, 1))
        vert = above - 2.0 * x + below
        d = diff[rows * j : rows * j + rows].reshape(CHUNK, lev, 256)
        done.append(x + a_row * d[:, :, :128] + a_col * d[:, :, 128:] + mix * vert)
    return done


def local_kernel(
    crow_ref,
    ccol_ref,
    mix_ref,
    block_ref,
    side_ref,
    flip_ref,
    strips_ref,
    state_ref,
    edge_ref,
    sten_ref,
    win_ref,
    wins_ref,
    code_ref,
    later_ref,
    base_ref,
    sten,
    win,
    kept,
    sems,
    base_sems,
):
    copies = []
    for i, (ref, held) in enumerate(((sten_ref, sten), (win_ref, win))):
        for n in range(2):
            part = pl.ds(n * 256, 256)
            copies.append(pltpu.make_async_copy(ref.at[part], held.at[part], sems.at[2 * i + n]))
            copies[-1].start()
    count, lev = state_ref.shape[0], state_ref.shape[1]
    here, peers = lax.axis_index("blocks"), lax.axis_size("blocks")
    block, side, flip = block_ref[...], side_ref[...], flip_ref[...]
    rel = (block >> 5) - here + 1
    rel = jnp.where(rel < 0, rel + peers, rel)
    rel = jnp.where(rel >= peers, rel - peers, rel)
    rel = jnp.where((here & 1) == 0, 2 - rel, rel)
    swap = (side & 1) ^ flip
    code_ref[...] = (block & 31) * 32 + rel * 8 + (side >> 1) * 4 + swap * 2 + flip
    later_ref[...] = strips_ref[...]
    for copy in copies:
        copy.wait()
    rows = CHUNK * lev

    def base_copy(i):
        blocks = pl.ds(i * CHUNK, CHUNK)
        return pltpu.make_async_copy(kept.at[blocks], base_ref.at[blocks], base_sems.at[i])

    def step(i, carry):
        blocks = pl.ds(pl.multiple_of(i * CHUNK, CHUNK), CHUNK)
        done = local_part(blocks, crow_ref, ccol_ref, mix_ref, state_ref, edge_ref, sten)
        for j in range(8):
            kept[blocks, :, 128 * j : 128 * j + 128] = done[j]
        base_copy(i).start()
        pairs = []
        for j in range(4):
            pair = [t.reshape(rows, 128) for t in done[2 * j : 2 * j + 2]]
            pairs.append(jnp.concatenate(split(jnp.concatenate(pair, 1)), 1))
        w = dot(jnp.concatenate(pairs, 0), win[...])
        for j in range(4):
            v = w[rows * j : rows * j + rows].reshape(CHUNK, lev, 256)
            wins_ref[blocks, 2 * j] = v[:, :, :128]
            wins_ref[blocks, 2 * j + 1] = v[:, :, 128:]
        return carry

    lax.fori_loop(0, count // CHUNK, step, 0)
    for i in range(count // CHUNK):
        base_copy(i).wait()


def collect_strips(near_refs, near):
    slab = lax.axis_index("slab")
    near[1] = near_refs[2][...]
    for owner, refs in ((0, near_refs[:2]), (2, near_refs[3:])):
        for which in range(2):

            @pl.when(slab == 1 - which)
            def _():
                near[owner] = refs[which][...]


def gather_ghosts(i, code_ref, a_row, a_col, near, ghosts_ref):
    lev = near.shape[3]
    half = lax.broadcasted_iota(jnp.int32, (lev, 128), 1) // 64
    rows = CHUNK * lev
    for s in range(4):
        parts = []
        for n in range(CHUNK):
            code = code_ref[s, i * CHUNK + n]
            x = near[(code >> 3) & 3, code >> 5, (code >> 2) & 1]
            x = jnp.where((code & 2) == 0, x, pltpu.roll(x, 64, 1))
            parts.append(jnp.where(half == (code & 1), x, 0.0))
        x = jnp.stack(parts) * (a_row if s < 2 else a_col)
        high, low = split(x.reshape(rows, 128))
        ghosts_ref[:, s * 256 : s * 256 + 128] = high
        ghosts_ref[:, s * 256 + 128 : s * 256 + 256] = low


def pack_kernel(
    code_ref,
    send_ref,
    crow_ref,
    ccol_ref,
    base_ref,
    near_early,
    near_late,
    own_ref,
    far_early,
    far_late,
    col0_ref,
    col1_ref,
    row0_ref,
    row1_ref,
    pay_ref,
    ghosts_ref,
    near,
    wins,
    held_pay,
    pay_sems,
    ghost_sems,
    *ghosts,
):
    lev = own_ref.shape[2]
    half = lax.broadcasted_iota(jnp.int32, (lev, 128), 1) // 64
    collect_strips((near_early, near_late, own_ref, far_early, far_late), near)
    a_row = levels_of(crow_ref, lev) * (1.0 / 12.0)
    a_col = levels_of(ccol_ref, lev) * (1.0 / 12.0)
    copies = []
    for i, held in enumerate(ghosts):
        gather_ghosts(i, code_ref, a_row, a_col, near, held)
        rows = pl.ds(i * CHUNK * lev, CHUNK * lev)
        copies.append(pltpu.make_async_copy(held, ghosts_ref.at[rows], ghost_sems.at[i]))
        copies[i].start()
        blocks = slice(i * CHUNK, i * CHUNK + CHUNK)
        row0 = dot(held[:, 0:256], row0_ref[...]).reshape(CHUNK, lev, 256)
        row1 = dot(held[:, 256:512], row1_ref[...]).reshape(CHUNK, lev, 256)
        for h, col_ref in enumerate((col0_ref, col1_ref)):
            c = dot(held[:, 512 + 256 * h : 768 + 256 * h], col_ref[...]).reshape(CHUNK, lev, 512)
            for j in range(4):
                v = base_ref[blocks, 2 * j + h] + c[:, :, 128 * j : 128 * j + 128]
                if j == 0:
                    v = v + row0[:, :, 128 * h : 128 * h + 128]
                if j == 3:
                    v = v + row1[:, :, 128 * h : 128 * h + 128]
                wins[blocks, 2 * j + h] = v

    size = pay_ref.shape[0] // pay_sems.shape[0]
    for i in range(pay_sems.shape[0]):
        for d in range(i * size, i * size + size):
            parts = []
            for k in range(2):
                w = send_ref[k, d]
                x = wins[w >> 4, (w >> 1) & 7]
                parts.append(jnp.where((w & 1) == k, x, pltpu.roll(x, 64, 1)))
            held_pay[d] = jnp.where(half == 0, parts[0], parts[1])
        part = pl.ds(i * size, size)
        copies.append(pltpu.make_async_copy(held_pay.at[part], pay_ref.at[part], pay_sems.at[i]))
        copies[-1].start()
    for copy in copies:
        copy.wait()


def finish_kernel(base_ref, ghosts_ref, col_ref, row0_ref, row1_ref, out_ref):
    blocks, lev = base_ref.shape[:2]
    c = dot(ghosts_ref[:, 512:1024], col_ref[...])
    row0 = dot(ghosts_ref[:, 0:256], row0_ref[...])
    row1 = dot(ghosts_ref[:, 256:512], row1_ref[...])
    for j in range(8):
        v = c[:, 128 * j : 128 * j + 128]
        if j == 0:
            v = v + row0
        if j == 7:
            v = v + row1
        lanes = slice(128 * j, 128 * j + 128)
        out_ref[:, :, lanes] = base_ref[:, :, lanes] + v.reshape(blocks, lev, 128)


def refine_kernel(sizes, slot_ref, count_ref, recv_ref, table_ref, out_ref, held, sems, *parents):
    lev = recv_ref.shape[1]
    half = lax.broadcasted_iota(jnp.int32, (lev, 128), 1) // 64
    live = count_ref[0]
    copies, start = [], 0
    for i, size in enumerate(sizes):
        for n in range(size):
            slot = slot_ref[0, start + n]
            x = recv_ref[slot >> 1]
            x = jnp.where(half == (slot & 1), x, pltpu.roll(x, 64, 1))
            x = jnp.where(start + n < live, x, 0.0)
            high, low = split(x)
            parents[i][n * lev : (n + 1) * lev, :128] = high
            parents[i][n * lev : (n + 1) * lev, 128:] = low
        part = pl.ds(start, size)
        fine = dot(parents[i][...], table_ref[...])
        held[part] = fine.astype(jnp.bfloat16).reshape(size, lev, 1024)
        copies.append(pltpu.make_async_copy(held.at[part], out_ref.at[part], sems.at[i]))
        copies[i].start()
        start += size
    for copy in copies:
        copy.wait()


VMEM = pl.BlockSpec(memory_space=pltpu.VMEM)
SMEM = pl.BlockSpec(memory_space=pltpu.SMEM)
HBM = pl.BlockSpec(memory_space=pltpu.HBM)
PARAMS = pltpu.CompilerParams(vmem_limit_bytes=VMEM_LIMIT)


def cost(flops, size):
    return pl.CostEstimate(flops=flops, bytes_accessed=size, transcendentals=0)


def make_strips(state):
    count, lev = state.shape[:2]
    return pl.pallas_call(
        strips_kernel,
        out_shape=(
            jax.ShapeDtypeStruct((count, 2, lev, 128), jnp.float32),
            jax.ShapeDtypeStruct((count, 1024), jnp.float32),
        ),
        in_specs=[HBM],
        out_specs=(VMEM, VMEM),
        scratch_shapes=[pltpu.VMEM(state.shape, jnp.float32), pltpu.SemaphoreType.DMA((2,))],
        compiler_params=PARAMS,
        name="strips",
    )(pltpu.with_memory_space_constraint(state, pltpu.HBM))


def make_local(coefs, tables, strips, state, edge):
    count, lev = state.shape[:2]
    maps = [pltpu.with_memory_space_constraint(jnp.asarray(m), pltpu.HBM) for m in (stencil_map(), window_map())]
    return pl.pallas_call(
        local_kernel,
        out_shape=(
            jax.ShapeDtypeStruct((count, 8, lev, 128), jnp.float32),
            jax.ShapeDtypeStruct(tables[0].shape, jnp.int32),
            jax.ShapeDtypeStruct(strips.shape, jnp.float32),
            pltpu.HBM(state.shape, jnp.float32),
        ),
        in_specs=[SMEM] * 3 + [VMEM] * 6 + [HBM] * 2,
        out_specs=(VMEM, VMEM, VMEM, HBM),
        scratch_shapes=[
            pltpu.VMEM(maps[0].shape, jnp.bfloat16),
            pltpu.VMEM(maps[1].shape, jnp.bfloat16),
            pltpu.VMEM(state.shape, jnp.float32),
            pltpu.SemaphoreType.DMA((4,)),
            pltpu.SemaphoreType.DMA((count // CHUNK,)),
        ],
        compiler_params=PARAMS,
        cost_estimate=cost(10**3, 10**3),
        name="local",
    )(*coefs, *tables, strips, state, edge, *maps)


def make_payload(code, send, coefs, base, nearby):
    count, lev, peers = base.shape[0], base.shape[2], send.shape[1]
    sides = [window_order(ghost_map(s)) for s in range(4)]
    cols = [m.reshape(256, 4, 256)[:, :, 128 * h : 128 * h + 128].reshape(256, 512) for h, m in enumerate(sides[2:])]
    maps = cols + [sides[0][:, :256], sides[1][:, 768:]]
    return pl.pallas_call(
        pack_kernel,
        out_shape=(
            pltpu.HBM((peers, lev, 128), jnp.float32),
            pltpu.HBM((count * lev, 1024), jnp.bfloat16),
        ),
        in_specs=[SMEM] * 4 + [VMEM] * 10,
        out_specs=(HBM, HBM),
        scratch_shapes=[
            pltpu.VMEM((3, count, 2, lev, 128), jnp.float32),
            pltpu.VMEM((count, 8, lev, 128), jnp.float32),
            pltpu.VMEM((peers, lev, 128), jnp.float32),
            pltpu.SemaphoreType.DMA((4,)),
            pltpu.SemaphoreType.DMA((count // CHUNK,)),
            *[pltpu.VMEM((CHUNK * lev, 1024), jnp.bfloat16)] * (count // CHUNK),
        ],
        compiler_params=PARAMS,
        cost_estimate=cost(10**9, 8 * 10**6),
        name="pack",
    )(code, send, *coefs[:2], base, *nearby, *[jnp.asarray(m) for m in maps])


def make_advanced(base, ghosts):
    count, lev = base.shape[:2]
    maps = [np.concatenate([ghost_map(2), ghost_map(3)], 0), ghost_map(0)[:, :128], ghost_map(1)[:, 896:]]
    block = pl.BlockSpec((CHUNK, lev, 1024), lambda i: (i, 0, 0))
    return pl.pallas_call(
        finish_kernel,
        grid=(count // CHUNK,),
        out_shape=jax.ShapeDtypeStruct(base.shape, jnp.float32),
        in_specs=[block, pl.BlockSpec((CHUNK * lev, 1024), lambda i: (i, 0))] + [VMEM] * 3,
        out_specs=block,
        compiler_params=PARAMS,
        cost_estimate=cost(2 * 10**9, 8 * 10**6),
        name="finish",
    )(
        pltpu.with_memory_space_constraint(base, pltpu.HBM),
        pltpu.with_memory_space_constraint(ghosts, pltpu.HBM),
        *[jnp.asarray(m) for m in maps],
    )


def make_refined(slots, live, received):
    fine = slots.shape[1]
    lev = received.shape[1]
    sizes = []
    for size in REFINE + (fine,) * fine:
        if sum(sizes) < fine:
            sizes.append(min(size, fine - sum(sizes)))
    return pl.pallas_call(
        functools.partial(refine_kernel, tuple(sizes)),
        out_shape=jax.ShapeDtypeStruct((fine, lev, 1024), jnp.bfloat16),
        in_specs=[SMEM, SMEM, VMEM, VMEM],
        out_specs=HBM,
        scratch_shapes=[
            pltpu.VMEM((fine, lev, 1024), jnp.bfloat16),
            pltpu.SemaphoreType.DMA((len(sizes),)),
            *[pltpu.VMEM((size * lev, 256), jnp.bfloat16) for size in sizes],
        ],
        compiler_params=PARAMS,
        name="refine",
    )(slots, live, received, jnp.asarray(refine_table()))


def body(
    state,
    courant_row,
    courant_col,
    mixing,
    nbr_block,
    nbr_side,
    nbr_flip,
    send_idx,
    fine_slot,
    fine_count,
):
    peers = lax.axis_size("blocks")
    far = [(i, (i + (1 if i % 2 else -1)) % peers) for i in range(peers)]
    near = [(i, i ^ 1) for i in range(peers)]

    def exchange(x, pairs, slab):
        return lax.ppermute(x, ("blocks", "slab"), [(2 * i + slab, 2 * j + slab) for i, j in pairs])

    strips, edge = make_strips(state)
    edge = lax.ppermute(edge, "slab", [(0, 1), (1, 0)])
    coefs = (courant_row, courant_col, mixing)
    wins, code, later, base = make_local(coefs, (nbr_block.T, nbr_side.T, nbr_flip.T), strips, state, edge)
    nearby = (
        exchange(strips, near, 1),
        exchange(later, near, 0),
        strips,
        exchange(strips, far, 1),
        exchange(later, far, 0),
    )
    payload, ghosts = make_payload(code, send_idx[0].T, coefs, wins, nearby)
    received = lax.all_to_all(payload, "blocks", split_axis=0, concat_axis=0, tiled=True)
    advanced = make_advanced(base, ghosts)
    return advanced, make_refined(fine_slot, fine_count, received)


def solution(mesh):
    in_specs = (
        P("blocks", "slab", None),
        P("slab"),
        P("slab"),
        P("slab"),
        P("blocks", None),
        P("blocks", None),
        P("blocks", None),
        P("blocks", None, None),
        P("blocks", None),
        P("blocks"),
    )
    out_specs = (P("blocks", "slab", None), P("blocks", "slab", None))
    return jax.shard_map(body, mesh=mesh, in_specs=in_specs, out_specs=out_specs, check_vma=False)
```

```python
import functools

import jax
import jax.numpy as jnp
import ml_dtypes
import numpy as np
from jax import lax
from jax.experimental import pallas as pl
from jax.experimental.pallas import tpu as pltpu
from jax.sharding import PartitionSpec as P

CHUNK = 8
REFINE = (32, 32, 32, 32, 32, 32)
VMEM_LIMIT = 24 * 1024 * 1024


def interp_1d():
    table = np.zeros((32, 8))
    for fine in range(32):
        x = (fine + 0.5) / 4.0
        start = min(max(int(np.floor(x - 0.5)) - 1, 0), 4)
        nodes = start + np.arange(4) + 0.5
        for a in range(4):
            weight = 1.0
            for b in range(4):
                if b != a:
                    weight *= (x - nodes[b]) / (nodes[a] - nodes[b])
            table[fine, start + a] = weight
    return table


def as_bf16(array):
    return np.asarray(array, np.float32).astype(ml_dtypes.bfloat16)


def refine_table():
    table = interp_1d()
    full = np.kron(table, table).T.astype(np.float32)
    high = as_bf16(full)
    low = as_bf16(full - high.astype(np.float32))
    return np.concatenate([high, low, high, low], 0)


def strip_cell(side, depth, t):
    line = depth if side in (0, 2) else 31 - depth
    return line * 32 + t if side < 2 else t * 32 + line


def ghost_map(side):
    first = side in (0, 2)
    out = np.zeros((128, 1024))
    for flip in range(2):
        for t in range(32):
            to = 31 - t if flip else t
            near = flip * 64 + t
            far = flip * 64 + 32 + t
            sign = 1.0 if first else -1.0
            out[near, strip_cell(side, 0, to)] += 8.0 * sign
            out[far, strip_cell(side, 0, to)] -= sign
            out[near, strip_cell(side, 1, to)] -= sign
    return as_bf16(np.concatenate([out, out], 0))


def window_order(table):
    out = np.zeros_like(table)
    for row in range(32):
        for col in range(32):
            to = (row // 8) * 256 + (col // 8) * 64 + (row % 8) * 8 + col % 8
            out[:, to] = table[:, row * 32 + col]
    return out


def stencil_map():
    own = np.zeros((128, 256))
    other = np.zeros((128, 256))
    weights = {-2: -1.0, -1: 8.0, 1: -8.0, 2: 1.0}
    for row in range(4):
        for col in range(32):
            lane = row * 32 + col
            for step, weight in weights.items():
                r = row + step
                if 0 <= r < 4:
                    own[r * 32 + col, lane] += weight
                else:
                    other[(r % 4) * 32 + col, lane] += weight
                c = col + step
                if 0 <= c < 32:
                    own[row * 32 + c, 128 + lane] += weight
    return as_bf16(np.concatenate([own, own, other, other], 0))


def window_map():
    pick = np.zeros((256, 256))
    for row in range(8):
        for col in range(32):
            pick[row * 32 + col, (col // 8) * 64 + row * 8 + col % 8] = 1.0
    return as_bf16(np.concatenate([pick, pick], 0))


def split(x):
    high = x.astype(jnp.bfloat16)
    low = (x - high.astype(jnp.float32)).astype(jnp.bfloat16)
    return high, low


def dot(a, b):
    return jnp.dot(a, b, preferred_element_type=jnp.float32)


def strips_kernel(state_ref, strips_ref, edge_ref, held, sems):
    slab = lax.axis_index("slab")
    count, lev = state_ref.shape[0], state_ref.shape[1]
    size = count // sems.shape[0]
    copies = []
    for i in range(sems.shape[0]):
        part = pl.ds(i * size, size)
        copies.append(pltpu.make_async_copy(state_ref.at[part], held.at[part], sems.at[i]))
        copies[i].start()
    cell = lax.broadcasted_iota(jnp.int32, (1024, 128), 0)
    to = lax.broadcasted_iota(jnp.int32, (1024, 128), 1)
    line = to // 32
    line = jnp.where(line < 2, line, 33 - line)
    pick = jnp.where((cell // 32 == to % 32) & (cell % 32 == line), 1.0, 0.0).astype(jnp.bfloat16)
    rows = size * lev
    lane = lax.broadcasted_iota(jnp.int32, (rows, 128), 1)
    for i in range(sems.shape[0]):
        copies[i].wait()
        part = slice(i * size, i * size + size)
        x = held[part]
        tail = x[:, :, 896:].reshape(rows, 128)
        tail = jnp.where((lane // 32) % 2 == 0, pltpu.roll(tail, 96, 1), pltpu.roll(tail, 32, 1))
        strips_ref[part, 0] = jnp.where(lane < 64, x[:, :, :128].reshape(rows, 128), tail).reshape(size, lev, 128)
        high, low = split(x.reshape(rows, 1024))
        strips_ref[part, 1] = (dot(high, pick) + dot(low, pick)).reshape(size, lev, 128)
        edge_ref[part] = jnp.where(slab == 0, x[:, lev - 1, :], x[:, 0, :])


def levels_of(ref, lev):
    at = lax.broadcasted_iota(jnp.int32, (lev, 128), 0)
    out = jnp.zeros((lev, 128), jnp.float32)
    for l in range(lev):
        out = jnp.where(at == l, ref[l], out)
    return out


def local_part(blocks, crow_ref, ccol_ref, mix_ref, state_ref, edge_ref, sten_ref):
    slab = lax.axis_index("slab")
    lev = state_ref.shape[1]
    a_row = levels_of(crow_ref, lev) * (1.0 / 12.0)
    a_col = levels_of(ccol_ref, lev) * (1.0 / 12.0)
    mix = levels_of(mix_ref, lev)
    rows = CHUNK * lev
    lane = lax.broadcasted_iota(jnp.int32, (rows, 128), 1)
    level = lax.broadcasted_iota(jnp.int32, (CHUNK, lev, 128), 1)
    zero = jnp.zeros((rows, 128), jnp.float32)
    tiles = [state_ref[blocks, :, 128 * j : 128 * j + 128] for j in range(8)]
    flat = [t.reshape(rows, 128) for t in tiles]
    left = []
    for j in range(8):
        other = jnp.where(lane < 64, flat[j + 1] if j < 7 else zero, flat[j - 1] if j else zero)
        left.append(jnp.concatenate(split(flat[j]) + split(other), 1))
    diff = dot(jnp.concatenate(left, 0), sten_ref[...])
    done = []
    for j in range(8):
        x = tiles[j]
        edge = edge_ref[blocks, 128 * j : 128 * j + 128][:, None, :]
        below = jnp.where(level == 0, jnp.where(slab == 0, 0.0, edge), pltpu.roll(x, 1, 1))
        above = jnp.where(level == lev - 1, jnp.where(slab == 0, edge, 0.0), pltpu.roll(x, lev - 1, 1))
        vert = above - 2.0 * x + below
        d = diff[rows * j : rows * j + rows].reshape(CHUNK, lev, 256)
        done.append(x + a_row * d[:, :, :128] + a_col * d[:, :, 128:] + mix * vert)
    return done


def ghost_codes(block, side, flip):
    here, peers = lax.axis_index("blocks"), lax.axis_size("blocks")
    rel = (block >> 5) - here + 1
    rel = jnp.where(rel < 0, rel + peers, rel)
    rel = jnp.where(rel >= peers, rel - peers, rel)
    rel = jnp.where((here & 1) == 0, 2 - rel, rel)
    swap = (side & 1) ^ flip
    return (block & 31) * 32 + rel * 8 + (side >> 1) * 4 + swap * 2 + flip


def local_kernel(
    start,
    crow_ref,
    ccol_ref,
    mix_ref,
    state_ref,
    edge_ref,
    sten_ref,
    win_ref,
    wins_ref,
    base_ref,
    sten,
    win,
    kept,
    sems,
    base_sems,
):
    copies = []
    for i, (ref, held) in enumerate(((sten_ref, sten), (win_ref, win))):
        for n in range(2):
            part = pl.ds(n * 256, 256)
            copies.append(pltpu.make_async_copy(ref.at[part], held.at[part], sems.at[2 * i + n]))
            copies[-1].start()
    count, lev = kept.shape[0], kept.shape[1]
    rows = CHUNK * lev
    for copy in copies:
        copy.wait()

    def base_copy(i):
        here = pl.ds(i * CHUNK, CHUNK)
        there = pl.ds(start + i * CHUNK, CHUNK)
        return pltpu.make_async_copy(kept.at[here], base_ref.at[there], base_sems.at[i])

    for i in range(count // CHUNK):
        here = slice(i * CHUNK, i * CHUNK + CHUNK)
        there = slice(start + i * CHUNK, start + i * CHUNK + CHUNK)
        done = local_part(there, crow_ref, ccol_ref, mix_ref, state_ref, edge_ref, sten)
        for j in range(8):
            kept[here, :, 128 * j : 128 * j + 128] = done[j]
        base_copy(i).start()
        pairs = []
        for j in range(4):
            pair = [t.reshape(rows, 128) for t in done[2 * j : 2 * j + 2]]
            pairs.append(jnp.concatenate(split(jnp.concatenate(pair, 1)), 1))
        w = dot(jnp.concatenate(pairs, 0), win[...])
        for j in range(4):
            v = w[rows * j : rows * j + rows].reshape(CHUNK, lev, 256)
            wins_ref[here, 2 * j] = v[:, :, :128]
            wins_ref[here, 2 * j + 1] = v[:, :, 128:]
    for i in range(count // CHUNK):
        base_copy(i).wait()


def first_local_kernel(
    crow_ref,
    ccol_ref,
    mix_ref,
    block_ref,
    side_ref,
    flip_ref,
    strips_ref,
    state_ref,
    edge_ref,
    sten_ref,
    win_ref,
    wins_ref,
    base_ref,
    code_ref,
    later_ref,
    *scratch,
):
    code_ref[...] = ghost_codes(block_ref[...], side_ref[...], flip_ref[...])
    later_ref[...] = strips_ref[...]
    refs = (crow_ref, ccol_ref, mix_ref, state_ref, edge_ref, sten_ref, win_ref, wins_ref, base_ref)
    local_kernel(0, *refs, *scratch)


def second_local_kernel(crow_ref, ccol_ref, mix_ref, state_ref, edge_ref, sten_ref, win_ref, kept_ref, *refs):
    half = state_ref.shape[0] // 2
    local_kernel(half, crow_ref, ccol_ref, mix_ref, state_ref, edge_ref, sten_ref, win_ref, *refs)


def collect_strips(near_refs, near):
    slab = lax.axis_index("slab")
    near[1] = near_refs[2][...]
    for owner, refs in ((0, near_refs[:2]), (2, near_refs[3:])):
        for which in range(2):

            @pl.when(slab == 1 - which)
            def _():
                near[owner] = refs[which][...]


def gather_ghosts(i, code_ref, a_row, a_col, near, ghosts_ref):
    lev = near.shape[3]
    half = lax.broadcasted_iota(jnp.int32, (lev, 128), 1) // 64
    rows = CHUNK * lev
    for s in range(4):
        parts = []
        for n in range(CHUNK):
            code = code_ref[s, i * CHUNK + n]
            x = near[(code >> 3) & 3, code >> 5, (code >> 2) & 1]
            x = jnp.where((code & 2) == 0, x, pltpu.roll(x, 64, 1))
            parts.append(jnp.where(half == (code & 1), x, 0.0))
        x = jnp.stack(parts) * (a_row if s < 2 else a_col)
        high, low = split(x.reshape(rows, 128))
        ghosts_ref[:, s * 256 : s * 256 + 128] = high
        ghosts_ref[:, s * 256 + 128 : s * 256 + 256] = low


def pack_kernel(
    code_ref,
    send_ref,
    crow_ref,
    ccol_ref,
    base0_ref,
    base1_ref,
    near_early,
    near_late,
    own_ref,
    far_early,
    far_late,
    col0_ref,
    col1_ref,
    row0_ref,
    row1_ref,
    pay_ref,
    ghosts_ref,
    near,
    wins,
    held_pay,
    pay_sems,
    ghost_sems,
    *ghosts,
):
    lev = own_ref.shape[2]
    half = lax.broadcasted_iota(jnp.int32, (lev, 128), 1) // 64
    collect_strips((near_early, near_late, own_ref, far_early, far_late), near)
    a_row = levels_of(crow_ref, lev) * (1.0 / 12.0)
    a_col = levels_of(ccol_ref, lev) * (1.0 / 12.0)
    copies = []
    for i, held in enumerate(ghosts):
        gather_ghosts(i, code_ref, a_row, a_col, near, held)
        rows = pl.ds(i * CHUNK * lev, CHUNK * lev)
        copies.append(pltpu.make_async_copy(held, ghosts_ref.at[rows], ghost_sems.at[i]))
        copies[i].start()
        blocks = slice(i * CHUNK, i * CHUNK + CHUNK)
        base = (base0_ref, base1_ref)[2 * i // len(ghosts)]
        mine = slice(blocks.start % base.shape[0], blocks.start % base.shape[0] + CHUNK)
        row0 = dot(held[:, 0:256], row0_ref[...]).reshape(CHUNK, lev, 256)
        row1 = dot(held[:, 256:512], row1_ref[...]).reshape(CHUNK, lev, 256)
        for h, col_ref in enumerate((col0_ref, col1_ref)):
            c = dot(held[:, 512 + 256 * h : 768 + 256 * h], col_ref[...]).reshape(CHUNK, lev, 512)
            for j in range(4):
                v = base[mine, 2 * j + h] + c[:, :, 128 * j : 128 * j + 128]
                if j == 0:
                    v = v + row0[:, :, 128 * h : 128 * h + 128]
                if j == 3:
                    v = v + row1[:, :, 128 * h : 128 * h + 128]
                wins[blocks, 2 * j + h] = v

    size = max(pay_ref.shape[0] // pay_sems.shape[0], 1)
    for i in range(pay_ref.shape[0] // size):
        for d in range(i * size, i * size + size):
            parts = []
            for k in range(2):
                w = send_ref[k, d]
                x = wins[w >> 4, (w >> 1) & 7]
                parts.append(jnp.where((w & 1) == k, x, pltpu.roll(x, 64, 1)))
            held_pay[d] = jnp.where(half == 0, parts[0], parts[1])
        part = pl.ds(i * size, size)
        copies.append(pltpu.make_async_copy(held_pay.at[part], pay_ref.at[part], pay_sems.at[i]))
        copies[-1].start()
    for copy in copies:
        copy.wait()


def finish_kernel(base_ref, ghosts_ref, col_ref, row0_ref, row1_ref, out_ref):
    blocks, lev = base_ref.shape[:2]
    c = dot(ghosts_ref[:, 512:1024], col_ref[...])
    row0 = dot(ghosts_ref[:, 0:256], row0_ref[...])
    row1 = dot(ghosts_ref[:, 256:512], row1_ref[...])
    for j in range(8):
        v = c[:, 128 * j : 128 * j + 128]
        if j == 0:
            v = v + row0
        if j == 7:
            v = v + row1
        lanes = slice(128 * j, 128 * j + 128)
        out_ref[:, :, lanes] = base_ref[:, :, lanes] + v.reshape(blocks, lev, 128)


def refine_kernel(sizes, slot_ref, count_ref, recv_ref, table_ref, out_ref, held, sems, *parents):
    lev = recv_ref.shape[1]
    half = lax.broadcasted_iota(jnp.int32, (lev, 128), 1) // 64
    live = count_ref[0]
    copies, start = [], 0
    for i, size in enumerate(sizes):
        for n in range(size):
            slot = slot_ref[0, start + n]
            x = recv_ref[slot >> 1]
            x = jnp.where(half == (slot & 1), x, pltpu.roll(x, 64, 1))
            x = jnp.where(start + n < live, x, 0.0)
            high, low = split(x)
            parents[i][n * lev : (n + 1) * lev, :128] = high
            parents[i][n * lev : (n + 1) * lev, 128:] = low
        part = pl.ds(start, size)
        fine = dot(parents[i][...], table_ref[...])
        held[part] = fine.astype(jnp.bfloat16).reshape(size, lev, 1024)
        copies.append(pltpu.make_async_copy(held.at[part], out_ref.at[part], sems.at[i]))
        copies[i].start()
        start += size
    for copy in copies:
        copy.wait()


VMEM = pl.BlockSpec(memory_space=pltpu.VMEM)
SMEM = pl.BlockSpec(memory_space=pltpu.SMEM)
HBM = pl.BlockSpec(memory_space=pltpu.HBM)
PARAMS = pltpu.CompilerParams(vmem_limit_bytes=VMEM_LIMIT)


def cost(flops, size):
    return pl.CostEstimate(flops=flops, bytes_accessed=size, transcendentals=0)


def make_strips(state):
    count, lev = state.shape[:2]
    return pl.pallas_call(
        strips_kernel,
        out_shape=(
            jax.ShapeDtypeStruct((count, 2, lev, 128), jnp.float32),
            jax.ShapeDtypeStruct((count, 1024), jnp.float32),
        ),
        in_specs=[HBM],
        out_specs=(VMEM, VMEM),
        scratch_shapes=[pltpu.VMEM(state.shape, jnp.float32), pltpu.SemaphoreType.DMA((2,))],
        compiler_params=PARAMS,
        name="strips",
    )(pltpu.with_memory_space_constraint(state, pltpu.HBM))


def make_local(coefs, state, edge, tables=(), strips=None, base=None):
    count, lev = state.shape[0] // 2, state.shape[1]
    maps = [pltpu.with_memory_space_constraint(jnp.asarray(m), pltpu.HBM) for m in (stencil_map(), window_map())]
    out_shape = [jax.ShapeDtypeStruct((count, 8, lev, 128), jnp.float32), pltpu.HBM(state.shape, jnp.float32)]
    in_specs, out_specs = [SMEM] * 3, [VMEM, HBM]
    args = [*coefs]
    aliases = {}
    if base is None:
        out_shape += [
            jax.ShapeDtypeStruct(tables[0].shape, jnp.int32),
            jax.ShapeDtypeStruct(strips.shape, jnp.float32),
        ]
        out_specs += [VMEM, VMEM]
        in_specs += [VMEM] * 4
        args += [*tables, strips]
    in_specs += [VMEM] * 2 + [HBM] * 2
    args += [state, edge, *maps]
    if base is not None:
        aliases = {len(args): 1}
        in_specs += [HBM]
        args += [base]
    return pl.pallas_call(
        first_local_kernel if base is None else second_local_kernel,
        out_shape=tuple(out_shape),
        in_specs=in_specs,
        out_specs=tuple(out_specs),
        scratch_shapes=[
            pltpu.VMEM(maps[0].shape, jnp.bfloat16),
            pltpu.VMEM(maps[1].shape, jnp.bfloat16),
            pltpu.VMEM((count, *state.shape[1:]), jnp.float32),
            pltpu.SemaphoreType.DMA((4,)),
            pltpu.SemaphoreType.DMA((count // CHUNK,)),
        ],
        input_output_aliases=aliases,
        compiler_params=PARAMS,
        cost_estimate=cost(10**3, 10**3),
        name="local",
    )(*args)


def make_payload(code, send, coefs, bases, nearby):
    count, lev, peers = 2 * bases[0].shape[0], bases[0].shape[2], send.shape[1]
    sides = [window_order(ghost_map(s)) for s in range(4)]
    cols = [m.reshape(256, 4, 256)[:, :, 128 * h : 128 * h + 128].reshape(256, 512) for h, m in enumerate(sides[2:])]
    maps = cols + [sides[0][:, :256], sides[1][:, 768:]]
    return pl.pallas_call(
        pack_kernel,
        out_shape=(
            pltpu.HBM((peers, lev, 128), jnp.float32),
            pltpu.HBM((count * lev, 1024), jnp.bfloat16),
        ),
        in_specs=[SMEM] * 4 + [VMEM] * 11,
        out_specs=(HBM, HBM),
        scratch_shapes=[
            pltpu.VMEM((3, count, 2, lev, 128), jnp.float32),
            pltpu.VMEM((count, 8, lev, 128), jnp.float32),
            pltpu.VMEM((peers, lev, 128), jnp.float32),
            pltpu.SemaphoreType.DMA((8,)),
            pltpu.SemaphoreType.DMA((count // CHUNK,)),
            *[pltpu.VMEM((CHUNK * lev, 1024), jnp.bfloat16)] * (count // CHUNK),
        ],
        compiler_params=PARAMS,
        cost_estimate=cost(10**9, 8 * 10**6),
        name="pack",
    )(code, send, *coefs[:2], *bases, *nearby, *[jnp.asarray(m) for m in maps])


def make_advanced(base, ghosts):
    count, lev = base.shape[:2]
    maps = [np.concatenate([ghost_map(2), ghost_map(3)], 0), ghost_map(0)[:, :128], ghost_map(1)[:, 896:]]
    block = pl.BlockSpec((CHUNK, lev, 1024), lambda i: (i, 0, 0))
    return pl.pallas_call(
        finish_kernel,
        grid=(count // CHUNK,),
        out_shape=jax.ShapeDtypeStruct(base.shape, jnp.float32),
        in_specs=[block, pl.BlockSpec((CHUNK * lev, 1024), lambda i: (i, 0))] + [VMEM] * 3,
        out_specs=block,
        compiler_params=PARAMS,
        cost_estimate=cost(2 * 10**9, 8 * 10**6),
        name="finish",
    )(
        pltpu.with_memory_space_constraint(base, pltpu.HBM),
        pltpu.with_memory_space_constraint(ghosts, pltpu.HBM),
        *[jnp.asarray(m) for m in maps],
    )


def make_refined(slots, live, received):
    fine = slots.shape[1]
    lev = received.shape[1]
    sizes = []
    for size in REFINE + (fine,) * fine:
        if sum(sizes) < fine:
            sizes.append(min(size, fine - sum(sizes)))
    return pl.pallas_call(
        functools.partial(refine_kernel, tuple(sizes)),
        out_shape=jax.ShapeDtypeStruct((fine, lev, 1024), jnp.bfloat16),
        in_specs=[SMEM, SMEM, VMEM, VMEM],
        out_specs=HBM,
        scratch_shapes=[
            pltpu.VMEM((fine, lev, 1024), jnp.bfloat16),
            pltpu.SemaphoreType.DMA((len(sizes),)),
            *[pltpu.VMEM((size * lev, 256), jnp.bfloat16) for size in sizes],
        ],
        compiler_params=PARAMS,
        name="refine",
    )(slots, live, received, jnp.asarray(refine_table()))


def body(
    state,
    courant_row,
    courant_col,
    mixing,
    nbr_block,
    nbr_side,
    nbr_flip,
    send_idx,
    fine_slot,
    fine_count,
):
    peers = lax.axis_size("blocks")
    far = [(i, (i + (1 if i % 2 else -1)) % peers) for i in range(peers)]
    near = [(i, i ^ 1) for i in range(peers)]

    def exchange(x, pairs, slab):
        own = [(2 * i + 1 - slab,) * 2 for i in range(peers)]
        return lax.ppermute(x, ("blocks", "slab"), [(2 * i + slab, 2 * j + slab) for i, j in pairs] + own)

    strips, edge = make_strips(state)
    edge = lax.ppermute(edge, "slab", [(0, 1), (1, 0)])
    coefs = (courant_row, courant_col, mixing)
    tables = (nbr_block.T, nbr_side.T, nbr_flip.T)
    wins0, base, code, later = make_local(coefs, state, edge, tables, strips)
    wins1, base = make_local(coefs, state, edge, base=base)
    nearby = (
        exchange(strips, near, 1),
        exchange(later, near, 0),
        strips,
        exchange(strips, far, 1),
        exchange(later, far, 0),
    )
    payload, ghosts = make_payload(code, send_idx[0].T, coefs, (wins0, wins1), nearby)
    received = lax.all_to_all(payload, "blocks", split_axis=0, concat_axis=0, tiled=True)
    advanced = make_advanced(base, ghosts)
    return advanced, make_refined(fine_slot, fine_count, received)


def solution(mesh):
    in_specs = (
        P("blocks", "slab", None),
        P("slab"),
        P("slab"),
        P("slab"),
        P("blocks", None),
        P("blocks", None),
        P("blocks", None),
        P("blocks", None, None),
        P("blocks", None),
        P("blocks"),
    )
    out_specs = (P("blocks", "slab", None), P("blocks", "slab", None))
    return jax.shard_map(body, mesh=mesh, in_specs=in_specs, out_specs=out_specs, check_vma=False)
```

```python
import functools

import jax
import jax.numpy as jnp
import ml_dtypes
import numpy as np
from jax import lax
from jax.experimental import pallas as pl
from jax.experimental.pallas import tpu as pltpu
from jax.sharding import PartitionSpec as P

CHUNK = 8
REFINE = (32, 32, 32, 32, 32, 32)
VMEM_LIMIT = 24 * 1024 * 1024


def interp_1d():
    table = np.zeros((32, 8))
    for fine in range(32):
        x = (fine + 0.5) / 4.0
        start = min(max(int(np.floor(x - 0.5)) - 1, 0), 4)
        nodes = start + np.arange(4) + 0.5
        for a in range(4):
            weight = 1.0
            for b in range(4):
                if b != a:
                    weight *= (x - nodes[b]) / (nodes[a] - nodes[b])
            table[fine, start + a] = weight
    return table


def as_bf16(array):
    return np.asarray(array, np.float32).astype(ml_dtypes.bfloat16)


def refine_table():
    table = interp_1d()
    full = np.kron(table, table).T.astype(np.float32)
    high = as_bf16(full)
    low = as_bf16(full - high.astype(np.float32))
    return np.concatenate([high, low, high, low], 0)


def strip_cell(side, depth, t):
    line = depth if side in (0, 2) else 31 - depth
    return line * 32 + t if side < 2 else t * 32 + line


def ghost_map(side):
    first = side in (0, 2)
    out = np.zeros((128, 1024))
    for flip in range(2):
        for t in range(32):
            to = 31 - t if flip else t
            near = flip * 64 + t
            far = flip * 64 + 32 + t
            sign = 1.0 if first else -1.0
            out[near, strip_cell(side, 0, to)] += 8.0 * sign
            out[far, strip_cell(side, 0, to)] -= sign
            out[near, strip_cell(side, 1, to)] -= sign
    return as_bf16(np.concatenate([out, out], 0))


def window_order(table):
    out = np.zeros_like(table)
    for row in range(32):
        for col in range(32):
            to = (row // 8) * 256 + (col // 8) * 64 + (row % 8) * 8 + col % 8
            out[:, to] = table[:, row * 32 + col]
    return out


def stencil_map():
    own = np.zeros((128, 256))
    other = np.zeros((128, 256))
    weights = {-2: -1.0, -1: 8.0, 1: -8.0, 2: 1.0}
    for row in range(4):
        for col in range(32):
            lane = row * 32 + col
            for step, weight in weights.items():
                r = row + step
                if 0 <= r < 4:
                    own[r * 32 + col, lane] += weight
                else:
                    other[(r % 4) * 32 + col, lane] += weight
                c = col + step
                if 0 <= c < 32:
                    own[row * 32 + c, 128 + lane] += weight
    return as_bf16(np.concatenate([own, own, other, other], 0))


def window_map():
    pick = np.zeros((256, 256))
    for row in range(8):
        for col in range(32):
            pick[row * 32 + col, (col // 8) * 64 + row * 8 + col % 8] = 1.0
    return as_bf16(np.concatenate([pick, pick], 0))


def split(x):
    high = x.astype(jnp.bfloat16)
    low = (x - high.astype(jnp.float32)).astype(jnp.bfloat16)
    return high, low


def dot(a, b):
    return jnp.dot(a, b, preferred_element_type=jnp.float32)


def strips_kernel(state_ref, strips_ref, edge_ref, held, sems):
    slab = lax.axis_index("slab")
    count, lev = state_ref.shape[0], state_ref.shape[1]
    size = count // sems.shape[0]
    copies = []
    for i in range(sems.shape[0]):
        part = pl.ds(i * size, size)
        copies.append(pltpu.make_async_copy(state_ref.at[part], held.at[part], sems.at[i]))
        copies[i].start()
    cell = lax.broadcasted_iota(jnp.int32, (1024, 128), 0)
    to = lax.broadcasted_iota(jnp.int32, (1024, 128), 1)
    line = to // 32
    line = jnp.where(line < 2, line, 33 - line)
    pick = jnp.where((cell // 32 == to % 32) & (cell % 32 == line), 1.0, 0.0).astype(jnp.bfloat16)
    rows = size * lev
    lane = lax.broadcasted_iota(jnp.int32, (rows, 128), 1)
    for i in range(sems.shape[0]):
        copies[i].wait()
        part = slice(i * size, i * size + size)
        x = held[part]
        tail = x[:, :, 896:].reshape(rows, 128)
        tail = jnp.where((lane // 32) % 2 == 0, pltpu.roll(tail, 96, 1), pltpu.roll(tail, 32, 1))
        strips_ref[part, 0] = jnp.where(lane < 64, x[:, :, :128].reshape(rows, 128), tail).reshape(size, lev, 128)
        high, low = split(x.reshape(rows, 1024))
        strips_ref[part, 1] = (dot(high, pick) + dot(low, pick)).reshape(size, lev, 128)
        edge_ref[part] = jnp.where(slab == 0, x[:, lev - 1, :], x[:, 0, :])


def levels_of(ref, lev):
    at = lax.broadcasted_iota(jnp.int32, (lev, 128), 0)
    out = jnp.zeros((lev, 128), jnp.float32)
    for l in range(lev):
        out = jnp.where(at == l, ref[l], out)
    return out


def local_part(blocks, crow_ref, ccol_ref, mix_ref, state_ref, sten_ref):
    lev = state_ref.shape[1]
    a_row = levels_of(crow_ref, lev) * (1.0 / 12.0)
    a_col = levels_of(ccol_ref, lev) * (1.0 / 12.0)
    mix = levels_of(mix_ref, lev)
    rows = CHUNK * lev
    lane = lax.broadcasted_iota(jnp.int32, (rows, 128), 1)
    level = lax.broadcasted_iota(jnp.int32, (CHUNK, lev, 128), 1)
    zero = jnp.zeros((rows, 128), jnp.float32)
    tiles = [state_ref[blocks, :, 128 * j : 128 * j + 128] for j in range(8)]
    flat = [t.reshape(rows, 128) for t in tiles]
    left = []
    for j in range(8):
        other = jnp.where(lane < 64, flat[j + 1] if j < 7 else zero, flat[j - 1] if j else zero)
        left.append(jnp.concatenate(split(flat[j]) + split(other), 1))
    diff = dot(jnp.concatenate(left, 0), sten_ref[...])
    done = []
    for j in range(8):
        x = tiles[j]
        below = jnp.where(level == 0, 0.0, pltpu.roll(x, 1, 1))
        above = jnp.where(level == lev - 1, 0.0, pltpu.roll(x, lev - 1, 1))
        vert = above - 2.0 * x + below
        d = diff[rows * j : rows * j + rows].reshape(CHUNK, lev, 256)
        done.append(x + a_row * d[:, :, :128] + a_col * d[:, :, 128:] + mix * vert)
    return done


def ghost_codes(block, side, flip):
    here, peers = lax.axis_index("blocks"), lax.axis_size("blocks")
    rel = (block >> 5) - here + 1
    rel = jnp.where(rel < 0, rel + peers, rel)
    rel = jnp.where(rel >= peers, rel - peers, rel)
    rel = jnp.where((here & 1) == 0, 2 - rel, rel)
    swap = (side & 1) ^ flip
    return (block & 31) * 32 + rel * 8 + (side >> 1) * 4 + swap * 2 + flip


def window_tiles(bands, win):
    pairs = [jnp.concatenate(split(band), 1) for band in bands]
    w = dot(jnp.concatenate(pairs, 0), win[...])
    rows = bands[0].shape[0]
    return [w[rows * (t // 2) : rows * (t // 2) + rows, 128 * (t % 2) : 128 * (t % 2) + 128] for t in range(8)]


def load_maps(sten_ref, win_ref, sten, win, sems):
    copies = []
    for i, (ref, held) in enumerate(((sten_ref, sten), (win_ref, win))):
        for n in range(2):
            part = pl.ds(n * 256, 256)
            copies.append(pltpu.make_async_copy(ref.at[part], held.at[part], sems.at[2 * i + n]))
            copies[-1].start()
    for copy in copies:
        copy.wait()


def local_blocks(crow_ref, ccol_ref, mix_ref, state_ref, wins_ref, base_ref, sten, win, kept, base_sems):
    count, lev = state_ref.shape[0], state_ref.shape[1]
    rows = CHUNK * lev

    def base_copy(i):
        blocks = pl.ds(i * CHUNK, CHUNK)
        return pltpu.make_async_copy(kept.at[blocks], base_ref.at[blocks], base_sems.at[i])

    def stencil(i, carry):
        blocks = pl.ds(pl.multiple_of(i * CHUNK, CHUNK), CHUNK)
        done = local_part(blocks, crow_ref, ccol_ref, mix_ref, state_ref, sten)
        for j in range(8):
            kept[blocks, :, 128 * j : 128 * j + 128] = done[j]
        base_copy(i).start()
        bands = [jnp.concatenate([t.reshape(rows, 128) for t in done[2 * j : 2 * j + 2]], 1) for j in range(4)]
        for t, tile in enumerate(window_tiles(bands, win)):
            wins_ref[blocks, t] = tile.reshape(CHUNK, lev, 128)
        return carry

    lax.fori_loop(0, count // CHUNK, stencil, 0)
    for i in range(count // CHUNK):
        base_copy(i).wait()


def first_kernel(
    crow_ref,
    ccol_ref,
    mix_ref,
    block_ref,
    side_ref,
    flip_ref,
    strips_ref,
    state_ref,
    sten_ref,
    win_ref,
    wins_ref,
    base_ref,
    code_ref,
    ready_ref,
    sten,
    win,
    kept,
    sems,
    base_sems,
):
    code_ref[...] = ghost_codes(block_ref[...], side_ref[...], flip_ref[...])
    ready_ref[...] = strips_ref[...]

    @pl.when(lax.axis_index("slab") == 0)
    def _():
        load_maps(sten_ref, win_ref, sten, win, sems)
        local_blocks(crow_ref, ccol_ref, mix_ref, state_ref, wins_ref, base_ref, sten, win, kept, base_sems)


def second_kernel(
    crow_ref,
    ccol_ref,
    mix_ref,
    edge_ref,
    state_ref,
    sten_ref,
    win_ref,
    done_ref,
    base_in_ref,
    wins_ref,
    base_ref,
    fix_ref,
    sten,
    win,
    kept,
    fix,
    sems,
    base_sems,
    fix_sem,
):
    slab = lax.axis_index("slab")
    count, lev = state_ref.shape[0], state_ref.shape[1]
    fix[...] = edge_ref[...] * jnp.where(slab == 0, mix_ref[lev - 1], mix_ref[0])
    fix_copy = pltpu.make_async_copy(fix, fix_ref, fix_sem.at[0])
    fix_copy.start()
    load_maps(sten_ref, win_ref, sten, win, sems)
    edge = window_tiles([fix[:, 256 * j : 256 * j + 256] for j in range(4)], win)

    @pl.when(slab == 1)
    def _():
        local_blocks(crow_ref, ccol_ref, mix_ref, state_ref, wins_ref, base_ref, sten, win, kept, base_sems)
        for t in range(8):
            wins_ref[:, t, 0, :] += edge[t]

    @pl.when(slab == 0)
    def _():
        wins_ref[...] = done_ref[...]
        for t in range(8):
            wins_ref[:, t, lev - 1, :] += edge[t]

    fix_copy.wait()


def collect_strips(near_refs, near):
    for i, ref in enumerate(near_refs):
        near[i] = ref[...]


def gather_ghosts(i, code_ref, a_row, a_col, near, ghosts_ref):
    lev = near.shape[3]
    half = lax.broadcasted_iota(jnp.int32, (lev, 128), 1) // 64
    rows = CHUNK * lev
    for s in range(4):
        parts = []
        for n in range(CHUNK):
            code = code_ref[s, i * CHUNK + n]
            x = near[(code >> 3) & 3, code >> 5, (code >> 2) & 1]
            x = jnp.where((code & 2) == 0, x, pltpu.roll(x, 64, 1))
            parts.append(jnp.where(half == (code & 1), x, 0.0))
        x = jnp.stack(parts) * (a_row if s < 2 else a_col)
        high, low = split(x.reshape(rows, 128))
        ghosts_ref[:, s * 256 : s * 256 + 128] = high
        ghosts_ref[:, s * 256 + 128 : s * 256 + 256] = low


def pack_kernel(
    code_ref,
    send_ref,
    crow_ref,
    ccol_ref,
    base_ref,
    near_ref,
    own_ref,
    far_ref,
    col0_ref,
    col1_ref,
    row0_ref,
    row1_ref,
    pay_ref,
    ghosts_ref,
    near,
    wins,
    held_pay,
    pay_sems,
    ghost_sems,
    *ghosts,
):
    lev = own_ref.shape[2]
    half = lax.broadcasted_iota(jnp.int32, (lev, 128), 1) // 64
    collect_strips((near_ref, own_ref, far_ref), near)
    a_row = levels_of(crow_ref, lev) * (1.0 / 12.0)
    a_col = levels_of(ccol_ref, lev) * (1.0 / 12.0)
    copies = []
    for i, held in enumerate(ghosts):
        gather_ghosts(i, code_ref, a_row, a_col, near, held)
        rows = pl.ds(i * CHUNK * lev, CHUNK * lev)
        copies.append(pltpu.make_async_copy(held, ghosts_ref.at[rows], ghost_sems.at[i]))
        copies[i].start()
        blocks = slice(i * CHUNK, i * CHUNK + CHUNK)
        row0 = dot(held[:, 0:256], row0_ref[...]).reshape(CHUNK, lev, 256)
        row1 = dot(held[:, 256:512], row1_ref[...]).reshape(CHUNK, lev, 256)
        for h, col_ref in enumerate((col0_ref, col1_ref)):
            c = dot(held[:, 512 + 256 * h : 768 + 256 * h], col_ref[...]).reshape(CHUNK, lev, 512)
            for j in range(4):
                v = base_ref[blocks, 2 * j + h] + c[:, :, 128 * j : 128 * j + 128]
                if j == 0:
                    v = v + row0[:, :, 128 * h : 128 * h + 128]
                if j == 3:
                    v = v + row1[:, :, 128 * h : 128 * h + 128]
                wins[blocks, 2 * j + h] = v

    size = pay_ref.shape[0] // pay_sems.shape[0]
    for i in range(pay_sems.shape[0]):
        for d in range(i * size, i * size + size):
            parts = []
            for k in range(2):
                w = send_ref[k, d]
                x = wins[w >> 4, (w >> 1) & 7]
                parts.append(jnp.where((w & 1) == k, x, pltpu.roll(x, 64, 1)))
            held_pay[d] = jnp.where(half == 0, parts[0], parts[1])
        part = pl.ds(i * size, size)
        copies.append(pltpu.make_async_copy(held_pay.at[part], pay_ref.at[part], pay_sems.at[i]))
        copies[-1].start()
    for copy in copies:
        copy.wait()


def finish_kernel(base_ref, ghosts_ref, fix_ref, col_ref, row0_ref, row1_ref, out_ref):
    blocks, lev = base_ref.shape[:2]
    level = lax.broadcasted_iota(jnp.int32, (blocks, lev, 128), 1)
    edge_level = jnp.where(lax.axis_index("slab") == 0, lev - 1, 0)
    c = dot(ghosts_ref[:, 512:1024], col_ref[...])
    row0 = dot(ghosts_ref[:, 0:256], row0_ref[...])
    row1 = dot(ghosts_ref[:, 256:512], row1_ref[...])
    for j in range(8):
        v = c[:, 128 * j : 128 * j + 128]
        if j == 0:
            v = v + row0
        if j == 7:
            v = v + row1
        lanes = slice(128 * j, 128 * j + 128)
        fix = jnp.where(level == edge_level, fix_ref[:, lanes][:, None, :], 0.0)
        out_ref[:, :, lanes] = base_ref[:, :, lanes] + fix + v.reshape(blocks, lev, 128)


def refine_kernel(sizes, slot_ref, count_ref, recv_ref, table_ref, out_ref, held, sems, *parents):
    lev = recv_ref.shape[1]
    half = lax.broadcasted_iota(jnp.int32, (lev, 128), 1) // 64
    live = count_ref[0]
    copies, start = [], 0
    for i, size in enumerate(sizes):
        for n in range(size):
            slot = slot_ref[0, start + n]
            x = recv_ref[slot >> 1]
            x = jnp.where(half == (slot & 1), x, pltpu.roll(x, 64, 1))
            x = jnp.where(start + n < live, x, 0.0)
            high, low = split(x)
            parents[i][n * lev : (n + 1) * lev, :128] = high
            parents[i][n * lev : (n + 1) * lev, 128:] = low
        part = pl.ds(start, size)
        fine = dot(parents[i][...], table_ref[...])
        held[part] = fine.astype(jnp.bfloat16).reshape(size, lev, 1024)
        copies.append(pltpu.make_async_copy(held.at[part], out_ref.at[part], sems.at[i]))
        copies[i].start()
        start += size
    for copy in copies:
        copy.wait()


VMEM = pl.BlockSpec(memory_space=pltpu.VMEM)
SMEM = pl.BlockSpec(memory_space=pltpu.SMEM)
HBM = pl.BlockSpec(memory_space=pltpu.HBM)
PARAMS = pltpu.CompilerParams(vmem_limit_bytes=VMEM_LIMIT)


def cost(flops, size):
    return pl.CostEstimate(flops=flops, bytes_accessed=size, transcendentals=0)


def make_strips(state):
    count, lev = state.shape[:2]
    return pl.pallas_call(
        strips_kernel,
        out_shape=(
            jax.ShapeDtypeStruct((count, 2, lev, 128), jnp.float32),
            jax.ShapeDtypeStruct((count, 1024), jnp.float32),
        ),
        in_specs=[HBM],
        out_specs=(VMEM, VMEM),
        scratch_shapes=[pltpu.VMEM(state.shape, jnp.float32), pltpu.SemaphoreType.DMA((2,))],
        compiler_params=PARAMS,
        name="strips",
    )(pltpu.with_memory_space_constraint(state, pltpu.HBM))


def local_maps():
    return [pltpu.with_memory_space_constraint(jnp.asarray(m), pltpu.HBM) for m in (stencil_map(), window_map())]


def local_scratch(state):
    return [
        pltpu.VMEM((512, 256), jnp.bfloat16),
        pltpu.VMEM((512, 256), jnp.bfloat16),
        pltpu.VMEM(state.shape, jnp.float32),
    ]


def make_first(coefs, tables, strips, state):
    count, lev = state.shape[:2]
    return pl.pallas_call(
        first_kernel,
        out_shape=(
            jax.ShapeDtypeStruct((count, 8, lev, 128), jnp.float32),
            pltpu.HBM(state.shape, jnp.float32),
            jax.ShapeDtypeStruct(tables[0].shape, jnp.int32),
            jax.ShapeDtypeStruct(strips.shape, jnp.float32),
        ),
        in_specs=[SMEM] * 3 + [VMEM] * 5 + [HBM] * 2,
        out_specs=(VMEM, HBM, VMEM, VMEM),
        scratch_shapes=local_scratch(state)
        + [pltpu.SemaphoreType.DMA((4,)), pltpu.SemaphoreType.DMA((count // CHUNK,))],
        compiler_params=PARAMS,
        name="first",
    )(*coefs, *tables, strips, state, *local_maps())


def make_second(coefs, edge, state, wins, base):
    count, lev = state.shape[:2]
    return pl.pallas_call(
        second_kernel,
        out_shape=(
            jax.ShapeDtypeStruct(wins.shape, jnp.float32),
            pltpu.HBM(state.shape, jnp.float32),
            pltpu.HBM(edge.shape, jnp.float32),
        ),
        in_specs=[SMEM] * 3 + [VMEM] * 2 + [HBM] * 2 + [VMEM, HBM],
        out_specs=(VMEM, HBM, HBM),
        scratch_shapes=local_scratch(state)
        + [
            pltpu.VMEM(edge.shape, jnp.float32),
            pltpu.SemaphoreType.DMA((4,)),
            pltpu.SemaphoreType.DMA((count // CHUNK,)),
            pltpu.SemaphoreType.DMA((1,)),
        ],
        input_output_aliases={8: 1},
        compiler_params=PARAMS,
        cost_estimate=cost(10**3, 10**3),
        name="second",
    )(*coefs, edge, state, *local_maps(), wins, base)


def make_payload(code, send, coefs, base, nearby):
    count, lev, peers = base.shape[0], base.shape[2], send.shape[1]
    sides = [window_order(ghost_map(s)) for s in range(4)]
    cols = [m.reshape(256, 4, 256)[:, :, 128 * h : 128 * h + 128].reshape(256, 512) for h, m in enumerate(sides[2:])]
    maps = cols + [sides[0][:, :256], sides[1][:, 768:]]
    return pl.pallas_call(
        pack_kernel,
        out_shape=(
            pltpu.HBM((peers, lev, 128), jnp.float32),
            pltpu.HBM((count * lev, 1024), jnp.bfloat16),
        ),
        in_specs=[SMEM] * 4 + [VMEM] * 8,
        out_specs=(HBM, HBM),
        scratch_shapes=[
            pltpu.VMEM((3, count, 2, lev, 128), jnp.float32),
            pltpu.VMEM((count, 8, lev, 128), jnp.float32),
            pltpu.VMEM((peers, lev, 128), jnp.float32),
            pltpu.SemaphoreType.DMA((4,)),
            pltpu.SemaphoreType.DMA((count // CHUNK,)),
            *[pltpu.VMEM((CHUNK * lev, 1024), jnp.bfloat16)] * (count // CHUNK),
        ],
        compiler_params=PARAMS,
        cost_estimate=cost(10**9, 8 * 10**6),
        name="pack",
    )(code, send, *coefs[:2], base, *nearby, *[jnp.asarray(m) for m in maps])


def make_advanced(base, ghosts, fix):
    count, lev = base.shape[:2]
    maps = [np.concatenate([ghost_map(2), ghost_map(3)], 0), ghost_map(0)[:, :128], ghost_map(1)[:, 896:]]
    block = pl.BlockSpec((CHUNK, lev, 1024), lambda i: (i, 0, 0))
    return pl.pallas_call(
        finish_kernel,
        grid=(count // CHUNK,),
        out_shape=jax.ShapeDtypeStruct(base.shape, jnp.float32),
        in_specs=[block, pl.BlockSpec((CHUNK * lev, 1024), lambda i: (i, 0)), pl.BlockSpec((CHUNK, 1024), lambda i: (i, 0))]
        + [VMEM] * 3,
        out_specs=block,
        compiler_params=PARAMS,
        cost_estimate=cost(2 * 10**9, 8 * 10**6),
        name="finish",
    )(
        pltpu.with_memory_space_constraint(base, pltpu.HBM),
        pltpu.with_memory_space_constraint(ghosts, pltpu.HBM),
        pltpu.with_memory_space_constraint(fix, pltpu.HBM),
        *[jnp.asarray(m) for m in maps],
    )


def make_refined(slots, live, received):
    fine = slots.shape[1]
    lev = received.shape[1]
    sizes = []
    for size in REFINE + (fine,) * fine:
        if sum(sizes) < fine:
            sizes.append(min(size, fine - sum(sizes)))
    return pl.pallas_call(
        functools.partial(refine_kernel, tuple(sizes)),
        out_shape=jax.ShapeDtypeStruct((fine, lev, 1024), jnp.bfloat16),
        in_specs=[SMEM, SMEM, VMEM, VMEM],
        out_specs=HBM,
        scratch_shapes=[
            pltpu.VMEM((fine, lev, 1024), jnp.bfloat16),
            pltpu.SemaphoreType.DMA((len(sizes),)),
            *[pltpu.VMEM((size * lev, 256), jnp.bfloat16) for size in sizes],
        ],
        compiler_params=PARAMS,
        name="refine",
    )(slots, live, received, jnp.asarray(refine_table()))


def body(
    state,
    courant_row,
    courant_col,
    mixing,
    nbr_block,
    nbr_side,
    nbr_flip,
    send_idx,
    fine_slot,
    fine_count,
):
    peers = lax.axis_size("blocks")
    far = [(i, (i + (1 if i % 2 else -1)) % peers) for i in range(peers)]
    near = [(i, i ^ 1) for i in range(peers)]
    coefs = (courant_row, courant_col, mixing)
    strips, edge = make_strips(state)
    wins, base, code, strips = make_first(coefs, (nbr_block.T, nbr_side.T, nbr_flip.T), strips, state)
    nearby = (lax.ppermute(strips, "blocks", near), strips, lax.ppermute(strips, "blocks", far))
    edge = lax.ppermute(edge, "slab", [(0, 1), (1, 0)])
    wins, base, fix = make_second(coefs, edge, state, wins, base)
    payload, ghosts = make_payload(code, send_idx[0].T, coefs, wins, nearby)
    received = lax.all_to_all(payload, "blocks", split_axis=0, concat_axis=0, tiled=True)
    advanced = make_advanced(base, ghosts, fix)
    return advanced, make_refined(fine_slot, fine_count, received)


def solution(mesh):
    in_specs = (
        P("blocks", "slab", None),
        P("slab"),
        P("slab"),
        P("slab"),
        P("blocks", None),
        P("blocks", None),
        P("blocks", None),
        P("blocks", None, None),
        P("blocks", None),
        P("blocks"),
    )
    out_specs = (P("blocks", "slab", None), P("blocks", "slab", None))
    return jax.shard_map(body, mesh=mesh, in_specs=in_specs, out_specs=out_specs, check_vma=False)
```

```python
import functools

import jax
import jax.numpy as jnp
import ml_dtypes
import numpy as np
from jax import lax
from jax.experimental import pallas as pl
from jax.experimental.pallas import tpu as pltpu
from jax.sharding import PartitionSpec as P

CHUNK = 8
REFINE = (32, 32, 32, 32, 32, 32)
VMEM_LIMIT = 24 * 1024 * 1024


def interp_1d():
    table = np.zeros((32, 8))
    for fine in range(32):
        x = (fine + 0.5) / 4.0
        start = min(max(int(np.floor(x - 0.5)) - 1, 0), 4)
        nodes = start + np.arange(4) + 0.5
        for a in range(4):
            weight = 1.0
            for b in range(4):
                if b != a:
                    weight *= (x - nodes[b]) / (nodes[a] - nodes[b])
            table[fine, start + a] = weight
    return table


def as_bf16(array):
    return np.asarray(array, np.float32).astype(ml_dtypes.bfloat16)


def refine_table():
    table = interp_1d()
    full = np.kron(table, table).T.astype(np.float32)
    high = as_bf16(full)
    low = as_bf16(full - high.astype(np.float32))
    return np.concatenate([high, low, high, low], 0)


def strip_cell(side, depth, t):
    line = depth if side in (0, 2) else 31 - depth
    return line * 32 + t if side < 2 else t * 32 + line


def ghost_map(side):
    first = side in (0, 2)
    out = np.zeros((128, 1024))
    for flip in range(2):
        for t in range(32):
            to = 31 - t if flip else t
            near = flip * 64 + t
            far = flip * 64 + 32 + t
            sign = 1.0 if first else -1.0
            out[near, strip_cell(side, 0, to)] += 8.0 * sign
            out[far, strip_cell(side, 0, to)] -= sign
            out[near, strip_cell(side, 1, to)] -= sign
    return as_bf16(np.concatenate([out, out], 0))


def window_order(table):
    out = np.zeros_like(table)
    for row in range(32):
        for col in range(32):
            to = (row // 8) * 256 + (col // 8) * 64 + (row % 8) * 8 + col % 8
            out[:, to] = table[:, row * 32 + col]
    return out


def stencil_map():
    own = np.zeros((128, 256))
    other = np.zeros((128, 256))
    weights = {-2: -1.0, -1: 8.0, 1: -8.0, 2: 1.0}
    for row in range(4):
        for col in range(32):
            lane = row * 32 + col
            for step, weight in weights.items():
                r = row + step
                if 0 <= r < 4:
                    own[r * 32 + col, lane] += weight
                else:
                    other[(r % 4) * 32 + col, lane] += weight
                c = col + step
                if 0 <= c < 32:
                    own[row * 32 + c, 128 + lane] += weight
    return as_bf16(np.concatenate([own, own, other, other], 0))


def window_map():
    pick = np.zeros((256, 256))
    for row in range(8):
        for col in range(32):
            pick[row * 32 + col, (col // 8) * 64 + row * 8 + col % 8] = 1.0
    return as_bf16(np.concatenate([pick, pick], 0))


def split(x):
    high = x.astype(jnp.bfloat16)
    low = (x - high.astype(jnp.float32)).astype(jnp.bfloat16)
    return high, low


def dot(a, b):
    return jnp.dot(a, b, preferred_element_type=jnp.float32)


def strips_kernel(state_ref, strips_ref, edge_ref, held, sems):
    slab = lax.axis_index("slab")
    count, lev = state_ref.shape[0], state_ref.shape[1]
    size = count // sems.shape[0]
    copies = []
    for i in range(sems.shape[0]):
        part = pl.ds(i * size, size)
        copies.append(pltpu.make_async_copy(state_ref.at[part], held.at[part], sems.at[i]))
        copies[i].start()
    cell = lax.broadcasted_iota(jnp.int32, (1024, 128), 0)
    to = lax.broadcasted_iota(jnp.int32, (1024, 128), 1)
    line = to // 32
    line = jnp.where(line < 2, line, 33 - line)
    pick = jnp.where((cell // 32 == to % 32) & (cell % 32 == line), 1.0, 0.0).astype(jnp.bfloat16)
    rows = size * lev
    lane = lax.broadcasted_iota(jnp.int32, (rows, 128), 1)
    for i in range(sems.shape[0]):
        copies[i].wait()
        part = slice(i * size, i * size + size)
        x = held[part]
        tail = x[:, :, 896:].reshape(rows, 128)
        tail = jnp.where((lane // 32) % 2 == 0, pltpu.roll(tail, 96, 1), pltpu.roll(tail, 32, 1))
        strips_ref[part, 0] = jnp.where(lane < 64, x[:, :, :128].reshape(rows, 128), tail).reshape(size, lev, 128)
        high, low = split(x.reshape(rows, 1024))
        strips_ref[part, 1] = (dot(high, pick) + dot(low, pick)).reshape(size, lev, 128)
        edge_ref[part] = jnp.where(slab == 0, x[:, lev - 1, :], x[:, 0, :])


def levels_of(ref, lev):
    at = lax.broadcasted_iota(jnp.int32, (lev, 128), 0)
    out = jnp.zeros((lev, 128), jnp.float32)
    for l in range(lev):
        out = jnp.where(at == l, ref[l], out)
    return out


def local_part(blocks, crow_ref, ccol_ref, mix_ref, state_ref, sten_ref):
    lev = state_ref.shape[1]
    a_row = levels_of(crow_ref, lev) * (1.0 / 12.0)
    a_col = levels_of(ccol_ref, lev) * (1.0 / 12.0)
    mix = levels_of(mix_ref, lev)
    rows = CHUNK * lev
    lane = lax.broadcasted_iota(jnp.int32, (rows, 128), 1)
    level = lax.broadcasted_iota(jnp.int32, (CHUNK, lev, 128), 1)
    zero = jnp.zeros((rows, 128), jnp.float32)
    tiles = [state_ref[blocks, :, 128 * j : 128 * j + 128] for j in range(8)]
    flat = [t.reshape(rows, 128) for t in tiles]
    left = []
    for j in range(8):
        other = jnp.where(lane < 64, flat[j + 1] if j < 7 else zero, flat[j - 1] if j else zero)
        left.append(jnp.concatenate(split(flat[j]) + split(other), 1))
    diff = dot(jnp.concatenate(left, 0), sten_ref[...])
    done = []
    for j in range(8):
        x = tiles[j]
        below = jnp.where(level == 0, 0.0, pltpu.roll(x, 1, 1))
        above = jnp.where(level == lev - 1, 0.0, pltpu.roll(x, lev - 1, 1))
        vert = above - 2.0 * x + below
        d = diff[rows * j : rows * j + rows].reshape(CHUNK, lev, 256)
        done.append(x + a_row * d[:, :, :128] + a_col * d[:, :, 128:] + mix * vert)
    return done


def ghost_codes(block, side, flip):
    here, peers = lax.axis_index("blocks"), lax.axis_size("blocks")
    rel = (block >> 5) - here + 1
    rel = jnp.where(rel < 0, rel + peers, rel)
    rel = jnp.where(rel >= peers, rel - peers, rel)
    rel = jnp.where((here & 1) == 0, rel, 2 - rel)
    swap = (side & 1) ^ flip
    return (block & 31) * 32 + rel * 8 + (side >> 1) * 4 + swap * 2 + flip


def window_tiles(bands, win):
    pairs = [jnp.concatenate(split(band), 1) for band in bands]
    w = dot(jnp.concatenate(pairs, 0), win[...])
    rows = bands[0].shape[0]
    return [w[rows * (t // 2) : rows * (t // 2) + rows, 128 * (t % 2) : 128 * (t % 2) + 128] for t in range(8)]


def load_maps(sten_ref, win_ref, sten, win, sems):
    copies = []
    for i, (ref, held) in enumerate(((sten_ref, sten), (win_ref, win))):
        for n in range(2):
            part = pl.ds(n * 256, 256)
            copies.append(pltpu.make_async_copy(ref.at[part], held.at[part], sems.at[2 * i + n]))
            copies[-1].start()
    for copy in copies:
        copy.wait()


def local_blocks(crow_ref, ccol_ref, mix_ref, state_ref, wins_ref, base_ref, sten, win, kept, base_sems):
    count, lev = state_ref.shape[0], state_ref.shape[1]
    rows = CHUNK * lev

    def base_copy(i):
        blocks = pl.ds(i * CHUNK, CHUNK)
        return pltpu.make_async_copy(kept.at[blocks], base_ref.at[blocks], base_sems.at[i])

    def stencil(i, carry):
        blocks = pl.ds(pl.multiple_of(i * CHUNK, CHUNK), CHUNK)
        done = local_part(blocks, crow_ref, ccol_ref, mix_ref, state_ref, sten)
        for j in range(8):
            kept[blocks, :, 128 * j : 128 * j + 128] = done[j]
        base_copy(i).start()
        bands = [jnp.concatenate([t.reshape(rows, 128) for t in done[2 * j : 2 * j + 2]], 1) for j in range(4)]
        for t, tile in enumerate(window_tiles(bands, win)):
            wins_ref[blocks, t] = tile.reshape(CHUNK, lev, 128)
        return carry

    lax.fori_loop(0, count // CHUNK, stencil, 0)
    for i in range(count // CHUNK):
        base_copy(i).wait()


def first_kernel(
    crow_ref,
    ccol_ref,
    mix_ref,
    block_ref,
    side_ref,
    flip_ref,
    strips_ref,
    state_ref,
    sten_ref,
    win_ref,
    wins_ref,
    base_ref,
    code_ref,
    ready_ref,
    sten,
    win,
    kept,
    sems,
    base_sems,
):
    code_ref[...] = ghost_codes(block_ref[...], side_ref[...], flip_ref[...])
    ready_ref[...] = strips_ref[...]

    @pl.when(lax.axis_index("slab") == 0)
    def _():
        load_maps(sten_ref, win_ref, sten, win, sems)
        local_blocks(crow_ref, ccol_ref, mix_ref, state_ref, wins_ref, base_ref, sten, win, kept, base_sems)


def second_kernel(
    crow_ref,
    ccol_ref,
    mix_ref,
    edge_ref,
    state_ref,
    sten_ref,
    win_ref,
    base_in_ref,
    wins_ref,
    base_ref,
    ready_ref,
    sten,
    win,
    kept,
    sems,
    base_sems,
):
    ready_ref[...] = edge_ref[...]

    @pl.when(lax.axis_index("slab") == 1)
    def _():
        load_maps(sten_ref, win_ref, sten, win, sems)
        local_blocks(crow_ref, ccol_ref, mix_ref, state_ref, wins_ref, base_ref, sten, win, kept, base_sems)


def edge_kernel(mix_ref, edge_ref, win_ref, first_ref, second_ref, wins_ref, fix_ref, fix, sem):
    slab = lax.axis_index("slab")
    lev = wins_ref.shape[2]
    fix[...] = edge_ref[...] * jnp.where(slab == 0, mix_ref[lev - 1], mix_ref[0])
    fix_copy = pltpu.make_async_copy(fix, fix_ref, sem.at[0])
    fix_copy.start()
    edge = window_tiles([fix[:, 256 * j : 256 * j + 256] for j in range(4)], win_ref)
    for which, done_ref, level in ((0, first_ref, lev - 1), (1, second_ref, 0)):

        @pl.when(slab == which)
        def _():
            wins_ref[...] = done_ref[...]
            for t in range(8):
                wins_ref[:, t, level, :] += edge[t]

    fix_copy.wait()


def collect_strips(near_refs, near):
    for i, ref in enumerate(near_refs):
        near[i] = ref[...]


def gather_ghosts(i, code_ref, a_row, a_col, near, ghosts_ref):
    lev = near.shape[3]
    half = lax.broadcasted_iota(jnp.int32, (lev, 128), 1) // 64
    rows = CHUNK * lev
    for s in range(4):
        parts = []
        for n in range(CHUNK):
            code = code_ref[s, i * CHUNK + n]
            x = near[(code >> 3) & 3, code >> 5, (code >> 2) & 1]
            x = jnp.where((code & 2) == 0, x, pltpu.roll(x, 64, 1))
            parts.append(jnp.where(half == (code & 1), x, 0.0))
        x = jnp.stack(parts) * (a_row if s < 2 else a_col)
        high, low = split(x.reshape(rows, 128))
        ghosts_ref[:, s * 256 : s * 256 + 128] = high
        ghosts_ref[:, s * 256 + 128 : s * 256 + 256] = low


def pack_kernel(
    code_ref,
    send_ref,
    crow_ref,
    ccol_ref,
    base_ref,
    far_ref,
    own_ref,
    near_ref,
    col0_ref,
    col1_ref,
    row0_ref,
    row1_ref,
    pay_ref,
    ghosts_ref,
    near,
    wins,
    held_pay,
    pay_sems,
    ghost_sems,
    *ghosts,
):
    lev = own_ref.shape[2]
    half = lax.broadcasted_iota(jnp.int32, (lev, 128), 1) // 64
    collect_strips((far_ref, own_ref, near_ref), near)
    a_row = levels_of(crow_ref, lev) * (1.0 / 12.0)
    a_col = levels_of(ccol_ref, lev) * (1.0 / 12.0)
    copies = []
    for i, held in enumerate(ghosts):
        gather_ghosts(i, code_ref, a_row, a_col, near, held)
        rows = pl.ds(i * CHUNK * lev, CHUNK * lev)
        copies.append(pltpu.make_async_copy(held, ghosts_ref.at[rows], ghost_sems.at[i]))
        copies[i].start()
        blocks = slice(i * CHUNK, i * CHUNK + CHUNK)
        row0 = dot(held[:, 0:256], row0_ref[...]).reshape(CHUNK, lev, 256)
        row1 = dot(held[:, 256:512], row1_ref[...]).reshape(CHUNK, lev, 256)
        for h, col_ref in enumerate((col0_ref, col1_ref)):
            c = dot(held[:, 512 + 256 * h : 768 + 256 * h], col_ref[...]).reshape(CHUNK, lev, 512)
            for j in range(4):
                v = base_ref[blocks, 2 * j + h] + c[:, :, 128 * j : 128 * j + 128]
                if j == 0:
                    v = v + row0[:, :, 128 * h : 128 * h + 128]
                if j == 3:
                    v = v + row1[:, :, 128 * h : 128 * h + 128]
                wins[blocks, 2 * j + h] = v

    size = pay_ref.shape[0] // pay_sems.shape[0]
    for i in range(pay_sems.shape[0]):
        for d in range(i * size, i * size + size):
            parts = []
            for k in range(2):
                w = send_ref[k, d]
                x = wins[w >> 4, (w >> 1) & 7]
                parts.append(jnp.where((w & 1) == k, x, pltpu.roll(x, 64, 1)))
            held_pay[d] = jnp.where(half == 0, parts[0], parts[1])
        part = pl.ds(i * size, size)
        copies.append(pltpu.make_async_copy(held_pay.at[part], pay_ref.at[part], pay_sems.at[i]))
        copies[-1].start()
    for copy in copies:
        copy.wait()


def finish_kernel(base_ref, ghosts_ref, fix_ref, col_ref, row0_ref, row1_ref, out_ref):
    blocks, lev = base_ref.shape[:2]
    level = lax.broadcasted_iota(jnp.int32, (blocks, lev, 128), 1)
    edge_level = jnp.where(lax.axis_index("slab") == 0, lev - 1, 0)
    c = dot(ghosts_ref[:, 512:1024], col_ref[...])
    row0 = dot(ghosts_ref[:, 0:256], row0_ref[...])
    row1 = dot(ghosts_ref[:, 256:512], row1_ref[...])
    for j in range(8):
        v = c[:, 128 * j : 128 * j + 128]
        if j == 0:
            v = v + row0
        if j == 7:
            v = v + row1
        lanes = slice(128 * j, 128 * j + 128)
        fix = jnp.where(level == edge_level, fix_ref[:, lanes][:, None, :], 0.0)
        out_ref[:, :, lanes] = base_ref[:, :, lanes] + fix + v.reshape(blocks, lev, 128)


def refine_kernel(sizes, slot_ref, count_ref, recv_ref, table_ref, out_ref, held, sems, *parents):
    lev = recv_ref.shape[1]
    half = lax.broadcasted_iota(jnp.int32, (lev, 128), 1) // 64
    live = count_ref[0]
    copies, start = [], 0
    for i, size in enumerate(sizes):
        for n in range(size):
            slot = slot_ref[0, start + n]
            x = recv_ref[slot >> 1]
            x = jnp.where(half == (slot & 1), x, pltpu.roll(x, 64, 1))
            x = jnp.where(start + n < live, x, 0.0)
            high, low = split(x)
            parents[i][n * lev : (n + 1) * lev, :128] = high
            parents[i][n * lev : (n + 1) * lev, 128:] = low
        part = pl.ds(start, size)
        fine = dot(parents[i][...], table_ref[...])
        held[part] = fine.astype(jnp.bfloat16).reshape(size, lev, 1024)
        copies.append(pltpu.make_async_copy(held.at[part], out_ref.at[part], sems.at[i]))
        copies[i].start()
        start += size
    for copy in copies:
        copy.wait()


VMEM = pl.BlockSpec(memory_space=pltpu.VMEM)
SMEM = pl.BlockSpec(memory_space=pltpu.SMEM)
HBM = pl.BlockSpec(memory_space=pltpu.HBM)
PARAMS = pltpu.CompilerParams(vmem_limit_bytes=VMEM_LIMIT)


def cost(flops, size):
    return pl.CostEstimate(flops=flops, bytes_accessed=size, transcendentals=0)


def make_strips(state):
    count, lev = state.shape[:2]
    return pl.pallas_call(
        strips_kernel,
        out_shape=(
            jax.ShapeDtypeStruct((count, 2, lev, 128), jnp.float32),
            jax.ShapeDtypeStruct((count, 1024), jnp.float32),
        ),
        in_specs=[HBM],
        out_specs=(VMEM, VMEM),
        scratch_shapes=[pltpu.VMEM(state.shape, jnp.float32), pltpu.SemaphoreType.DMA((2,))],
        compiler_params=PARAMS,
        name="strips",
    )(pltpu.with_memory_space_constraint(state, pltpu.HBM))


def local_maps():
    return [pltpu.with_memory_space_constraint(jnp.asarray(m), pltpu.HBM) for m in (stencil_map(), window_map())]


def local_scratch(state):
    return [
        pltpu.VMEM((512, 256), jnp.bfloat16),
        pltpu.VMEM((512, 256), jnp.bfloat16),
        pltpu.VMEM(state.shape, jnp.float32),
    ]


def make_first(coefs, tables, strips, state):
    count, lev = state.shape[:2]
    return pl.pallas_call(
        first_kernel,
        out_shape=(
            jax.ShapeDtypeStruct((count, 8, lev, 128), jnp.float32),
            pltpu.HBM(state.shape, jnp.float32),
            jax.ShapeDtypeStruct(tables[0].shape, jnp.int32),
            jax.ShapeDtypeStruct(strips.shape, jnp.float32),
        ),
        in_specs=[SMEM] * 3 + [VMEM] * 5 + [HBM] * 2,
        out_specs=(VMEM, HBM, VMEM, VMEM),
        scratch_shapes=local_scratch(state)
        + [pltpu.SemaphoreType.DMA((4,)), pltpu.SemaphoreType.DMA((count // CHUNK,))],
        compiler_params=PARAMS,
        name="first",
    )(*coefs, *tables, strips, state, *local_maps())


def make_second(coefs, edge, state, base):
    count, lev = state.shape[:2]
    return pl.pallas_call(
        second_kernel,
        out_shape=(
            jax.ShapeDtypeStruct((count, 8, lev, 128), jnp.float32),
            pltpu.HBM(state.shape, jnp.float32),
            jax.ShapeDtypeStruct(edge.shape, jnp.float32),
        ),
        in_specs=[SMEM] * 3 + [VMEM] * 2 + [HBM] * 3,
        out_specs=(VMEM, HBM, VMEM),
        scratch_shapes=local_scratch(state)
        + [pltpu.SemaphoreType.DMA((4,)), pltpu.SemaphoreType.DMA((count // CHUNK,))],
        input_output_aliases={7: 1},
        compiler_params=PARAMS,
        cost_estimate=cost(10**3, 10**3),
        name="second",
    )(*coefs, edge, state, *local_maps(), base)


def add_edge(mixing, edge, first, second):
    return pl.pallas_call(
        edge_kernel,
        out_shape=(jax.ShapeDtypeStruct(first.shape, jnp.float32), pltpu.HBM(edge.shape, jnp.float32)),
        in_specs=[SMEM] + [VMEM] * 4,
        out_specs=(VMEM, HBM),
        scratch_shapes=[pltpu.VMEM(edge.shape, jnp.float32), pltpu.SemaphoreType.DMA((1,))],
        compiler_params=PARAMS,
        cost_estimate=cost(10**3, 10**3),
        name="edge",
    )(mixing, edge, jnp.asarray(window_map()), first, second)


def make_payload(code, send, coefs, base, nearby):
    count, lev, peers = base.shape[0], base.shape[2], send.shape[1]
    sides = [window_order(ghost_map(s)) for s in range(4)]
    cols = [m.reshape(256, 4, 256)[:, :, 128 * h : 128 * h + 128].reshape(256, 512) for h, m in enumerate(sides[2:])]
    maps = cols + [sides[0][:, :256], sides[1][:, 768:]]
    return pl.pallas_call(
        pack_kernel,
        out_shape=(
            pltpu.HBM((peers, lev, 128), jnp.float32),
            pltpu.HBM((count * lev, 1024), jnp.bfloat16),
        ),
        in_specs=[SMEM] * 4 + [VMEM] * 8,
        out_specs=(HBM, HBM),
        scratch_shapes=[
            pltpu.VMEM((3, count, 2, lev, 128), jnp.float32),
            pltpu.VMEM((count, 8, lev, 128), jnp.float32),
            pltpu.VMEM((peers, lev, 128), jnp.float32),
            pltpu.SemaphoreType.DMA((4,)),
            pltpu.SemaphoreType.DMA((count // CHUNK,)),
            *[pltpu.VMEM((CHUNK * lev, 1024), jnp.bfloat16)] * (count // CHUNK),
        ],
        compiler_params=PARAMS,
        cost_estimate=cost(10**9, 8 * 10**6),
        name="pack",
    )(code, send, *coefs[:2], base, *nearby, *[jnp.asarray(m) for m in maps])


def make_advanced(base, ghosts, fix):
    count, lev = base.shape[:2]
    maps = [np.concatenate([ghost_map(2), ghost_map(3)], 0), ghost_map(0)[:, :128], ghost_map(1)[:, 896:]]
    block = pl.BlockSpec((CHUNK, lev, 1024), lambda i: (i, 0, 0))
    return pl.pallas_call(
        finish_kernel,
        grid=(count // CHUNK,),
        out_shape=jax.ShapeDtypeStruct(base.shape, jnp.float32),
        in_specs=[block, pl.BlockSpec((CHUNK * lev, 1024), lambda i: (i, 0)), pl.BlockSpec((CHUNK, 1024), lambda i: (i, 0))]
        + [VMEM] * 3,
        out_specs=block,
        compiler_params=PARAMS,
        cost_estimate=cost(2 * 10**9, 8 * 10**6),
        name="finish",
    )(
        pltpu.with_memory_space_constraint(base, pltpu.HBM),
        pltpu.with_memory_space_constraint(ghosts, pltpu.HBM),
        pltpu.with_memory_space_constraint(fix, pltpu.HBM),
        *[jnp.asarray(m) for m in maps],
    )


def make_refined(slots, live, received):
    fine = slots.shape[1]
    lev = received.shape[1]
    sizes = []
    for size in REFINE + (fine,) * fine:
        if sum(sizes) < fine:
            sizes.append(min(size, fine - sum(sizes)))
    return pl.pallas_call(
        functools.partial(refine_kernel, tuple(sizes)),
        out_shape=jax.ShapeDtypeStruct((fine, lev, 1024), jnp.bfloat16),
        in_specs=[SMEM, SMEM, VMEM, VMEM],
        out_specs=HBM,
        scratch_shapes=[
            pltpu.VMEM((fine, lev, 1024), jnp.bfloat16),
            pltpu.SemaphoreType.DMA((len(sizes),)),
            *[pltpu.VMEM((size * lev, 256), jnp.bfloat16) for size in sizes],
        ],
        compiler_params=PARAMS,
        name="refine",
    )(slots, live, received, jnp.asarray(refine_table()))


def body(
    state,
    courant_row,
    courant_col,
    mixing,
    nbr_block,
    nbr_side,
    nbr_flip,
    send_idx,
    fine_slot,
    fine_count,
):
    peers = lax.axis_size("blocks")
    far = [(i, (i + (1 if i % 2 else -1)) % peers) for i in range(peers)]
    near = [(i, i ^ 1) for i in range(peers)]
    coefs = (courant_row, courant_col, mixing)
    strips, edge = make_strips(state)
    first, base, code, strips = make_first(coefs, (nbr_block.T, nbr_side.T, nbr_flip.T), strips, state)
    nearby = (lax.ppermute(strips, "blocks", far), strips, lax.ppermute(strips, "blocks", near))
    second, base, edge = make_second(coefs, edge, state, base)
    edge = lax.ppermute(edge, "slab", [(0, 1), (1, 0)])
    wins, fix = add_edge(mixing, edge, first, second)
    payload, ghosts = make_payload(code, send_idx[0].T, coefs, wins, nearby)
    received = lax.all_to_all(payload, "blocks", split_axis=0, concat_axis=0, tiled=True)
    advanced = make_advanced(base, ghosts, fix)
    return advanced, make_refined(fine_slot, fine_count, received)


def solution(mesh):
    in_specs = (
        P("blocks", "slab", None),
        P("slab"),
        P("slab"),
        P("slab"),
        P("blocks", None),
        P("blocks", None),
        P("blocks", None),
        P("blocks", None, None),
        P("blocks", None),
        P("blocks"),
    )
    out_specs = (P("blocks", "slab", None), P("blocks", "slab", None))
    return jax.shard_map(body, mesh=mesh, in_specs=in_specs, out_specs=out_specs, check_vma=False)
```

```python
import functools

import jax
import jax.numpy as jnp
import ml_dtypes
import numpy as np
from jax import lax
from jax.experimental import pallas as pl
from jax.experimental.pallas import tpu as pltpu
from jax.sharding import PartitionSpec as P

CHUNK = 8
REFINE = (32, 32, 32, 32, 32, 32)
VMEM_LIMIT = 24 * 1024 * 1024


def interp_1d():
    table = np.zeros((32, 8))
    for fine in range(32):
        x = (fine + 0.5) / 4.0
        start = min(max(int(np.floor(x - 0.5)) - 1, 0), 4)
        nodes = start + np.arange(4) + 0.5
        for a in range(4):
            weight = 1.0
            for b in range(4):
                if b != a:
                    weight *= (x - nodes[b]) / (nodes[a] - nodes[b])
            table[fine, start + a] = weight
    return table


def as_bf16(array):
    return np.asarray(array, np.float32).astype(ml_dtypes.bfloat16)


def refine_table():
    table = interp_1d()
    full = np.kron(table, table).T.astype(np.float32)
    high = as_bf16(full)
    low = as_bf16(full - high.astype(np.float32))
    return np.concatenate([high, low, high, low], 0)


def strip_cell(side, depth, t):
    line = depth if side in (0, 2) else 31 - depth
    return line * 32 + t if side < 2 else t * 32 + line


def ghost_map(side):
    first = side in (0, 2)
    out = np.zeros((128, 1024))
    for flip in range(2):
        for t in range(32):
            to = 31 - t if flip else t
            near = flip * 64 + t
            far = flip * 64 + 32 + t
            sign = 1.0 if first else -1.0
            out[near, strip_cell(side, 0, to)] += 8.0 * sign
            out[far, strip_cell(side, 0, to)] -= sign
            out[near, strip_cell(side, 1, to)] -= sign
    return as_bf16(np.concatenate([out, out], 0))


def window_order(table):
    out = np.zeros_like(table)
    for row in range(32):
        for col in range(32):
            to = (row // 8) * 256 + (col // 8) * 64 + (row % 8) * 8 + col % 8
            out[:, to] = table[:, row * 32 + col]
    return out


def stencil_map():
    own = np.zeros((128, 256))
    other = np.zeros((128, 256))
    weights = {-2: -1.0, -1: 8.0, 1: -8.0, 2: 1.0}
    for row in range(4):
        for col in range(32):
            lane = row * 32 + col
            for step, weight in weights.items():
                r = row + step
                if 0 <= r < 4:
                    own[r * 32 + col, lane] += weight
                else:
                    other[(r % 4) * 32 + col, lane] += weight
                c = col + step
                if 0 <= c < 32:
                    own[row * 32 + c, 128 + lane] += weight
    return as_bf16(np.concatenate([own, own, other, other], 0))


def window_map():
    pick = np.zeros((256, 256))
    for row in range(8):
        for col in range(32):
            pick[row * 32 + col, (col // 8) * 64 + row * 8 + col % 8] = 1.0
    return as_bf16(np.concatenate([pick, pick], 0))


def plane_size(peers):
    return max(peers // 8, 1)


def send_order(peers):
    size = plane_size(peers)
    planes = peers // size
    fold = [p // 2 if p % 2 == 0 else planes - 1 - p // 2 for p in range(planes)]
    return [plane * size + i for plane in fold for i in range(size)]


def split(x):
    high = x.astype(jnp.bfloat16)
    low = (x - high.astype(jnp.float32)).astype(jnp.bfloat16)
    return high, low


def dot(a, b):
    return jnp.dot(a, b, preferred_element_type=jnp.float32)


def strips_kernel(state_ref, strips_ref, edge_ref, held, sems):
    slab = lax.axis_index("slab")
    count, lev = state_ref.shape[0], state_ref.shape[1]
    size = count // sems.shape[0]
    copies = []
    for i in range(sems.shape[0]):
        part = pl.ds(i * size, size)
        copies.append(pltpu.make_async_copy(state_ref.at[part], held.at[part], sems.at[i]))
        copies[i].start()
    cell = lax.broadcasted_iota(jnp.int32, (1024, 128), 0)
    to = lax.broadcasted_iota(jnp.int32, (1024, 128), 1)
    line = to // 32
    line = jnp.where(line < 2, line, 33 - line)
    pick = jnp.where((cell // 32 == to % 32) & (cell % 32 == line), 1.0, 0.0).astype(jnp.bfloat16)
    rows = size * lev
    lane = lax.broadcasted_iota(jnp.int32, (rows, 128), 1)
    for i in range(sems.shape[0]):
        copies[i].wait()
        part = slice(i * size, i * size + size)
        x = held[part]
        tail = x[:, :, 896:].reshape(rows, 128)
        tail = jnp.where((lane // 32) % 2 == 0, pltpu.roll(tail, 96, 1), pltpu.roll(tail, 32, 1))
        strips_ref[part, 0] = jnp.where(lane < 64, x[:, :, :128].reshape(rows, 128), tail).reshape(size, lev, 128)
        high, low = split(x.reshape(rows, 1024))
        strips_ref[part, 1] = (dot(high, pick) + dot(low, pick)).reshape(size, lev, 128)
        edge_ref[part] = jnp.where(slab == 0, x[:, lev - 1, :], x[:, 0, :])


def levels_of(ref, lev):
    at = lax.broadcasted_iota(jnp.int32, (lev, 128), 0)
    out = jnp.zeros((lev, 128), jnp.float32)
    for l in range(lev):
        out = jnp.where(at == l, ref[l], out)
    return out


def local_part(blocks, crow_ref, ccol_ref, mix_ref, state_ref, sten_ref):
    lev = state_ref.shape[1]
    a_row = levels_of(crow_ref, lev) * (1.0 / 12.0)
    a_col = levels_of(ccol_ref, lev) * (1.0 / 12.0)
    mix = levels_of(mix_ref, lev)
    rows = CHUNK * lev
    lane = lax.broadcasted_iota(jnp.int32, (rows, 128), 1)
    level = lax.broadcasted_iota(jnp.int32, (CHUNK, lev, 128), 1)
    zero = jnp.zeros((rows, 128), jnp.float32)
    tiles = [state_ref[blocks, :, 128 * j : 128 * j + 128] for j in range(8)]
    flat = [t.reshape(rows, 128) for t in tiles]
    left = []
    for j in range(8):
        other = jnp.where(lane < 64, flat[j + 1] if j < 7 else zero, flat[j - 1] if j else zero)
        left.append(jnp.concatenate(split(flat[j]) + split(other), 1))
    diff = dot(jnp.concatenate(left, 0), sten_ref[...])
    done = []
    for j in range(8):
        x = tiles[j]
        below = jnp.where(level == 0, 0.0, pltpu.roll(x, 1, 1))
        above = jnp.where(level == lev - 1, 0.0, pltpu.roll(x, lev - 1, 1))
        vert = above - 2.0 * x + below
        d = diff[rows * j : rows * j + rows].reshape(CHUNK, lev, 256)
        done.append(x + a_row * d[:, :, :128] + a_col * d[:, :, 128:] + mix * vert)
    return done


def ghost_codes(block, side, flip):
    here, peers = lax.axis_index("blocks"), lax.axis_size("blocks")
    rel = (block >> 5) - here + 1
    rel = jnp.where(rel < 0, rel + peers, rel)
    rel = jnp.where(rel >= peers, rel - peers, rel)
    rel = jnp.where((here & 1) == 0, rel, 2 - rel)
    swap = (side & 1) ^ flip
    return (block & 31) * 32 + rel * 8 + (side >> 1) * 4 + swap * 2 + flip


def window_tiles(bands, win):
    pairs = [jnp.concatenate(split(band), 1) for band in bands]
    w = dot(jnp.concatenate(pairs, 0), win[...])
    rows = bands[0].shape[0]
    return [w[rows * (t // 2) : rows * (t // 2) + rows, 128 * (t % 2) : 128 * (t % 2) + 128] for t in range(8)]


def load_maps(sten_ref, win_ref, sten, win, sems):
    copies = []
    for i, (ref, held) in enumerate(((sten_ref, sten), (win_ref, win))):
        for n in range(2):
            part = pl.ds(n * 256, 256)
            copies.append(pltpu.make_async_copy(ref.at[part], held.at[part], sems.at[2 * i + n]))
            copies[-1].start()
    for copy in copies:
        copy.wait()


def local_blocks(crow_ref, ccol_ref, mix_ref, state_ref, wins_ref, base_ref, sten, win, kept, base_sems):
    count, lev = state_ref.shape[0], state_ref.shape[1]
    rows = CHUNK * lev

    def base_copy(i):
        blocks = pl.ds(i * CHUNK, CHUNK)
        return pltpu.make_async_copy(kept.at[blocks], base_ref.at[blocks], base_sems.at[i])

    def stencil(i, carry):
        blocks = pl.ds(pl.multiple_of(i * CHUNK, CHUNK), CHUNK)
        done = local_part(blocks, crow_ref, ccol_ref, mix_ref, state_ref, sten)
        for j in range(8):
            kept[blocks, :, 128 * j : 128 * j + 128] = done[j]
        base_copy(i).start()
        bands = [jnp.concatenate([t.reshape(rows, 128) for t in done[2 * j : 2 * j + 2]], 1) for j in range(4)]
        for t, tile in enumerate(window_tiles(bands, win)):
            wins_ref[blocks, t] = tile.reshape(CHUNK, lev, 128)
        return carry

    lax.fori_loop(0, count // CHUNK, stencil, 0)
    for i in range(count // CHUNK):
        base_copy(i).wait()


def first_kernel(
    crow_ref,
    ccol_ref,
    mix_ref,
    block_ref,
    side_ref,
    flip_ref,
    strips_ref,
    state_ref,
    sten_ref,
    win_ref,
    wins_ref,
    base_ref,
    code_ref,
    ready_ref,
    sten,
    win,
    kept,
    sems,
    base_sems,
):
    code_ref[...] = ghost_codes(block_ref[...], side_ref[...], flip_ref[...])
    ready_ref[...] = strips_ref[...]

    @pl.when(lax.axis_index("slab") == 0)
    def _():
        load_maps(sten_ref, win_ref, sten, win, sems)
        local_blocks(crow_ref, ccol_ref, mix_ref, state_ref, wins_ref, base_ref, sten, win, kept, base_sems)


def second_kernel(
    crow_ref,
    ccol_ref,
    mix_ref,
    edge_ref,
    state_ref,
    sten_ref,
    win_ref,
    base_in_ref,
    wins_ref,
    base_ref,
    ready_ref,
    sten,
    win,
    kept,
    sems,
    base_sems,
):
    ready_ref[...] = edge_ref[...]

    @pl.when(lax.axis_index("slab") == 1)
    def _():
        load_maps(sten_ref, win_ref, sten, win, sems)
        local_blocks(crow_ref, ccol_ref, mix_ref, state_ref, wins_ref, base_ref, sten, win, kept, base_sems)


def edge_kernel(mix_ref, edge_ref, win_ref, first_ref, second_ref, wins_ref, fix_ref, fix, sem):
    slab = lax.axis_index("slab")
    lev = wins_ref.shape[2]
    fix[...] = edge_ref[...] * jnp.where(slab == 0, mix_ref[lev - 1], mix_ref[0])
    fix_copy = pltpu.make_async_copy(fix, fix_ref, sem.at[0])
    fix_copy.start()
    edge = window_tiles([fix[:, 256 * j : 256 * j + 256] for j in range(4)], win_ref)
    for which, done_ref, level in ((0, first_ref, lev - 1), (1, second_ref, 0)):

        @pl.when(slab == which)
        def _():
            wins_ref[...] = done_ref[...]
            for t in range(8):
                wins_ref[:, t, level, :] += edge[t]

    fix_copy.wait()


def collect_strips(near_refs, near):
    for i, ref in enumerate(near_refs):
        near[i] = ref[...]


def gather_ghosts(i, code_ref, a_row, a_col, near, ghosts_ref):
    lev = near.shape[3]
    half = lax.broadcasted_iota(jnp.int32, (lev, 128), 1) // 64
    rows = CHUNK * lev
    for s in range(4):
        parts = []
        for n in range(CHUNK):
            code = code_ref[s, i * CHUNK + n]
            x = near[(code >> 3) & 3, code >> 5, (code >> 2) & 1]
            x = jnp.where((code & 2) == 0, x, pltpu.roll(x, 64, 1))
            parts.append(jnp.where(half == (code & 1), x, 0.0))
        x = jnp.stack(parts) * (a_row if s < 2 else a_col)
        high, low = split(x.reshape(rows, 128))
        ghosts_ref[:, s * 256 : s * 256 + 128] = high
        ghosts_ref[:, s * 256 + 128 : s * 256 + 256] = low


def pack_kernel(
    code_ref,
    send_ref,
    crow_ref,
    ccol_ref,
    base_ref,
    far_ref,
    own_ref,
    near_ref,
    col0_ref,
    col1_ref,
    row0_ref,
    row1_ref,
    pay_ref,
    ghosts_ref,
    near,
    wins,
    held_pay,
    pay_sems,
    ghost_sems,
    *ghosts,
):
    lev = own_ref.shape[2]
    half = lax.broadcasted_iota(jnp.int32, (lev, 128), 1) // 64
    collect_strips((far_ref, own_ref, near_ref), near)
    a_row = levels_of(crow_ref, lev) * (1.0 / 12.0)
    a_col = levels_of(ccol_ref, lev) * (1.0 / 12.0)
    copies = []
    for i, held in enumerate(ghosts):
        gather_ghosts(i, code_ref, a_row, a_col, near, held)
        rows = pl.ds(i * CHUNK * lev, CHUNK * lev)
        copies.append(pltpu.make_async_copy(held, ghosts_ref.at[rows], ghost_sems.at[i]))
        copies[i].start()
        blocks = slice(i * CHUNK, i * CHUNK + CHUNK)
        row0 = dot(held[:, 0:256], row0_ref[...]).reshape(CHUNK, lev, 256)
        row1 = dot(held[:, 256:512], row1_ref[...]).reshape(CHUNK, lev, 256)
        for h, col_ref in enumerate((col0_ref, col1_ref)):
            c = dot(held[:, 512 + 256 * h : 768 + 256 * h], col_ref[...]).reshape(CHUNK, lev, 512)
            for j in range(4):
                v = base_ref[blocks, 2 * j + h] + c[:, :, 128 * j : 128 * j + 128]
                if j == 0:
                    v = v + row0[:, :, 128 * h : 128 * h + 128]
                if j == 3:
                    v = v + row1[:, :, 128 * h : 128 * h + 128]
                wins[blocks, 2 * j + h] = v

    order = send_order(pay_ref.shape[0])
    size = pay_ref.shape[0] // pay_sems.shape[0]
    for i in range(pay_sems.shape[0]):
        for d in range(i * size, i * size + size):
            parts = []
            for k in range(2):
                w = send_ref[k, order[d]]
                x = wins[w >> 4, (w >> 1) & 7]
                parts.append(jnp.where((w & 1) == k, x, pltpu.roll(x, 64, 1)))
            held_pay[d] = jnp.where(half == 0, parts[0], parts[1])
        part = pl.ds(i * size, size)
        copies.append(pltpu.make_async_copy(held_pay.at[part], pay_ref.at[part], pay_sems.at[i]))
        copies[-1].start()
    for copy in copies:
        copy.wait()


def finish_kernel(base_ref, ghosts_ref, fix_ref, col_ref, row0_ref, row1_ref, out_ref):
    blocks, lev = base_ref.shape[:2]
    level = lax.broadcasted_iota(jnp.int32, (blocks, lev, 128), 1)
    edge_level = jnp.where(lax.axis_index("slab") == 0, lev - 1, 0)
    c = dot(ghosts_ref[:, 512:1024], col_ref[...])
    row0 = dot(ghosts_ref[:, 0:256], row0_ref[...])
    row1 = dot(ghosts_ref[:, 256:512], row1_ref[...])
    for j in range(8):
        v = c[:, 128 * j : 128 * j + 128]
        if j == 0:
            v = v + row0
        if j == 7:
            v = v + row1
        lanes = slice(128 * j, 128 * j + 128)
        fix = jnp.where(level == edge_level, fix_ref[:, lanes][:, None, :], 0.0)
        out_ref[:, :, lanes] = base_ref[:, :, lanes] + fix + v.reshape(blocks, lev, 128)


def refine_kernel(sizes, slot_ref, count_ref, recv_ref, table_ref, out_ref, held, sems, *parents):
    lev = recv_ref.shape[1]
    half = lax.broadcasted_iota(jnp.int32, (lev, 128), 1) // 64
    live = count_ref[0]
    size_in = plane_size(recv_ref.shape[0])
    planes = recv_ref.shape[0] // size_in
    shift = size_in.bit_length() - 1
    copies, start = [], 0
    for i, size in enumerate(sizes):
        for n in range(size):
            slot = slot_ref[0, start + n]
            src = slot >> 1
            plane = src >> shift
            place = jnp.where(plane < (planes + 1) // 2, 2 * plane, 2 * planes - 1 - 2 * plane)
            x = recv_ref[(place << shift) + (src & (size_in - 1))]
            x = jnp.where(half == (slot & 1), x, pltpu.roll(x, 64, 1))
            x = jnp.where(start + n < live, x, 0.0)
            high, low = split(x)
            parents[i][n * lev : (n + 1) * lev, :128] = high
            parents[i][n * lev : (n + 1) * lev, 128:] = low
        part = pl.ds(start, size)
        fine = dot(parents[i][...], table_ref[...])
        held[part] = fine.astype(jnp.bfloat16).reshape(size, lev, 1024)
        copies.append(pltpu.make_async_copy(held.at[part], out_ref.at[part], sems.at[i]))
        copies[i].start()
        start += size
    for copy in copies:
        copy.wait()


VMEM = pl.BlockSpec(memory_space=pltpu.VMEM)
SMEM = pl.BlockSpec(memory_space=pltpu.SMEM)
HBM = pl.BlockSpec(memory_space=pltpu.HBM)
PARAMS = pltpu.CompilerParams(vmem_limit_bytes=VMEM_LIMIT)


def cost(flops, size):
    return pl.CostEstimate(flops=flops, bytes_accessed=size, transcendentals=0)


def make_strips(state):
    count, lev = state.shape[:2]
    return pl.pallas_call(
        strips_kernel,
        out_shape=(
            jax.ShapeDtypeStruct((count, 2, lev, 128), jnp.float32),
            jax.ShapeDtypeStruct((count, 1024), jnp.float32),
        ),
        in_specs=[HBM],
        out_specs=(VMEM, VMEM),
        scratch_shapes=[pltpu.VMEM(state.shape, jnp.float32), pltpu.SemaphoreType.DMA((2,))],
        compiler_params=PARAMS,
        name="strips",
    )(pltpu.with_memory_space_constraint(state, pltpu.HBM))


def local_maps():
    return [pltpu.with_memory_space_constraint(jnp.asarray(m), pltpu.HBM) for m in (stencil_map(), window_map())]


def local_scratch(state):
    return [
        pltpu.VMEM((512, 256), jnp.bfloat16),
        pltpu.VMEM((512, 256), jnp.bfloat16),
        pltpu.VMEM(state.shape, jnp.float32),
    ]


def make_first(coefs, tables, strips, state):
    count, lev = state.shape[:2]
    return pl.pallas_call(
        first_kernel,
        out_shape=(
            jax.ShapeDtypeStruct((count, 8, lev, 128), jnp.float32),
            pltpu.HBM(state.shape, jnp.float32),
            jax.ShapeDtypeStruct(tables[0].shape, jnp.int32),
            jax.ShapeDtypeStruct(strips.shape, jnp.float32),
        ),
        in_specs=[SMEM] * 3 + [VMEM] * 5 + [HBM] * 2,
        out_specs=(VMEM, HBM, VMEM, VMEM),
        scratch_shapes=local_scratch(state)
        + [pltpu.SemaphoreType.DMA((4,)), pltpu.SemaphoreType.DMA((count // CHUNK,))],
        compiler_params=PARAMS,
        name="first",
    )(*coefs, *tables, strips, state, *local_maps())


def make_second(coefs, edge, state, base):
    count, lev = state.shape[:2]
    return pl.pallas_call(
        second_kernel,
        out_shape=(
            jax.ShapeDtypeStruct((count, 8, lev, 128), jnp.float32),
            pltpu.HBM(state.shape, jnp.float32),
            jax.ShapeDtypeStruct(edge.shape, jnp.float32),
        ),
        in_specs=[SMEM] * 3 + [VMEM] * 2 + [HBM] * 3,
        out_specs=(VMEM, HBM, VMEM),
        scratch_shapes=local_scratch(state)
        + [pltpu.SemaphoreType.DMA((4,)), pltpu.SemaphoreType.DMA((count // CHUNK,))],
        input_output_aliases={7: 1},
        compiler_params=PARAMS,
        cost_estimate=cost(10**3, 10**3),
        name="second",
    )(*coefs, edge, state, *local_maps(), base)


def add_edge(mixing, edge, first, second):
    return pl.pallas_call(
        edge_kernel,
        out_shape=(jax.ShapeDtypeStruct(first.shape, jnp.float32), pltpu.HBM(edge.shape, jnp.float32)),
        in_specs=[SMEM] + [VMEM] * 4,
        out_specs=(VMEM, HBM),
        scratch_shapes=[pltpu.VMEM(edge.shape, jnp.float32), pltpu.SemaphoreType.DMA((1,))],
        compiler_params=PARAMS,
        cost_estimate=cost(10**3, 10**3),
        name="edge",
    )(mixing, edge, jnp.asarray(window_map()), first, second)


def make_payload(code, send, coefs, base, nearby):
    count, lev, peers = base.shape[0], base.shape[2], send.shape[1]
    sides = [window_order(ghost_map(s)) for s in range(4)]
    cols = [m.reshape(256, 4, 256)[:, :, 128 * h : 128 * h + 128].reshape(256, 512) for h, m in enumerate(sides[2:])]
    maps = cols + [sides[0][:, :256], sides[1][:, 768:]]
    return pl.pallas_call(
        pack_kernel,
        out_shape=(
            pltpu.HBM((peers, lev, 128), jnp.float32),
            pltpu.HBM((count * lev, 1024), jnp.bfloat16),
        ),
        in_specs=[SMEM] * 4 + [VMEM] * 8,
        out_specs=(HBM, HBM),
        scratch_shapes=[
            pltpu.VMEM((3, count, 2, lev, 128), jnp.float32),
            pltpu.VMEM((count, 8, lev, 128), jnp.float32),
            pltpu.VMEM((peers, lev, 128), jnp.float32),
            pltpu.SemaphoreType.DMA((4,)),
            pltpu.SemaphoreType.DMA((count // CHUNK,)),
            *[pltpu.VMEM((CHUNK * lev, 1024), jnp.bfloat16)] * (count // CHUNK),
        ],
        compiler_params=PARAMS,
        cost_estimate=cost(10**9, 8 * 10**6),
        name="pack",
    )(code, send, *coefs[:2], base, *nearby, *[jnp.asarray(m) for m in maps])


def make_advanced(base, ghosts, fix):
    count, lev = base.shape[:2]
    maps = [np.concatenate([ghost_map(2), ghost_map(3)], 0), ghost_map(0)[:, :128], ghost_map(1)[:, 896:]]
    block = pl.BlockSpec((CHUNK, lev, 1024), lambda i: (i, 0, 0))
    return pl.pallas_call(
        finish_kernel,
        grid=(count // CHUNK,),
        out_shape=jax.ShapeDtypeStruct(base.shape, jnp.float32),
        in_specs=[block, pl.BlockSpec((CHUNK * lev, 1024), lambda i: (i, 0)), pl.BlockSpec((CHUNK, 1024), lambda i: (i, 0))]
        + [VMEM] * 3,
        out_specs=block,
        compiler_params=PARAMS,
        cost_estimate=cost(2 * 10**9, 8 * 10**6),
        name="finish",
    )(
        pltpu.with_memory_space_constraint(base, pltpu.HBM),
        pltpu.with_memory_space_constraint(ghosts, pltpu.HBM),
        pltpu.with_memory_space_constraint(fix, pltpu.HBM),
        *[jnp.asarray(m) for m in maps],
    )


def make_refined(slots, live, received):
    fine = slots.shape[1]
    lev = received.shape[1]
    sizes = []
    for size in REFINE + (fine,) * fine:
        if sum(sizes) < fine:
            sizes.append(min(size, fine - sum(sizes)))
    return pl.pallas_call(
        functools.partial(refine_kernel, tuple(sizes)),
        out_shape=jax.ShapeDtypeStruct((fine, lev, 1024), jnp.bfloat16),
        in_specs=[SMEM, SMEM, VMEM, VMEM],
        out_specs=HBM,
        scratch_shapes=[
            pltpu.VMEM((fine, lev, 1024), jnp.bfloat16),
            pltpu.SemaphoreType.DMA((len(sizes),)),
            *[pltpu.VMEM((size * lev, 256), jnp.bfloat16) for size in sizes],
        ],
        compiler_params=PARAMS,
        name="refine",
    )(slots, live, received, jnp.asarray(refine_table()))


def body(
    state,
    courant_row,
    courant_col,
    mixing,
    nbr_block,
    nbr_side,
    nbr_flip,
    send_idx,
    fine_slot,
    fine_count,
):
    peers = lax.axis_size("blocks")
    far = [(i, (i + (1 if i % 2 else -1)) % peers) for i in range(peers)]
    near = [(i, i ^ 1) for i in range(peers)]
    coefs = (courant_row, courant_col, mixing)
    strips, edge = make_strips(state)
    first, base, code, strips = make_first(coefs, (nbr_block.T, nbr_side.T, nbr_flip.T), strips, state)
    nearby = (lax.ppermute(strips, "blocks", far), strips, lax.ppermute(strips, "blocks", near))
    second, base, edge = make_second(coefs, edge, state, base)
    edge = lax.ppermute(edge, "slab", [(0, 1), (1, 0)])
    wins, fix = add_edge(mixing, edge, first, second)
    payload, ghosts = make_payload(code, send_idx[0].T, coefs, wins, nearby)
    received = lax.all_to_all(
        payload, "blocks", split_axis=0, concat_axis=0, axis_index_groups=[send_order(peers)], tiled=True
    )
    advanced = make_advanced(base, ghosts, fix)
    return advanced, make_refined(fine_slot, fine_count, received)


def solution(mesh):
    in_specs = (
        P("blocks", "slab", None),
        P("slab"),
        P("slab"),
        P("slab"),
        P("blocks", None),
        P("blocks", None),
        P("blocks", None),
        P("blocks", None, None),
        P("blocks", None),
        P("blocks"),
    )
    out_specs = (P("blocks", "slab", None), P("blocks", "slab", None))
    return jax.shard_map(body, mesh=mesh, in_specs=in_specs, out_specs=out_specs, check_vma=False)
```

```python
import functools

import jax
import jax.numpy as jnp
import ml_dtypes
import numpy as np
from jax import lax
from jax.experimental import pallas as pl
from jax.experimental.pallas import tpu as pltpu
from jax.sharding import PartitionSpec as P

CHUNK = 8
REFINE = (32, 32, 32, 32, 32, 32)
VMEM_LIMIT = 24 * 1024 * 1024


def interp_1d():
    table = np.zeros((32, 8))
    for fine in range(32):
        x = (fine + 0.5) / 4.0
        start = min(max(int(np.floor(x - 0.5)) - 1, 0), 4)
        nodes = start + np.arange(4) + 0.5
        for a in range(4):
            weight = 1.0
            for b in range(4):
                if b != a:
                    weight *= (x - nodes[b]) / (nodes[a] - nodes[b])
            table[fine, start + a] = weight
    return table


def as_bf16(array):
    return np.asarray(array, np.float32).astype(ml_dtypes.bfloat16)


def refine_table():
    table = interp_1d()
    full = np.kron(table, table).T.astype(np.float32)
    high = as_bf16(full)
    low = as_bf16(full - high.astype(np.float32))
    return np.concatenate([high, low, high, low], 0)


def strip_cell(side, depth, t):
    line = depth if side in (0, 2) else 31 - depth
    return line * 32 + t if side < 2 else t * 32 + line


def ghost_map(side):
    first = side in (0, 2)
    out = np.zeros((128, 1024))
    for flip in range(2):
        for t in range(32):
            to = 31 - t if flip else t
            near = flip * 64 + t
            far = flip * 64 + 32 + t
            sign = 1.0 if first else -1.0
            out[near, strip_cell(side, 0, to)] += 8.0 * sign
            out[far, strip_cell(side, 0, to)] -= sign
            out[near, strip_cell(side, 1, to)] -= sign
    return as_bf16(np.concatenate([out, out], 0))


def window_order(table):
    out = np.zeros_like(table)
    for row in range(32):
        for col in range(32):
            to = (row // 8) * 256 + (col // 8) * 64 + (row % 8) * 8 + col % 8
            out[:, to] = table[:, row * 32 + col]
    return out


def stencil_map():
    own = np.zeros((128, 256))
    other = np.zeros((128, 256))
    weights = {-2: -1.0, -1: 8.0, 1: -8.0, 2: 1.0}
    for row in range(4):
        for col in range(32):
            lane = row * 32 + col
            for step, weight in weights.items():
                r = row + step
                if 0 <= r < 4:
                    own[r * 32 + col, lane] += weight
                else:
                    other[(r % 4) * 32 + col, lane] += weight
                c = col + step
                if 0 <= c < 32:
                    own[row * 32 + c, 128 + lane] += weight
    return as_bf16(np.concatenate([own, own, other, other], 0))


def window_map():
    pick = np.zeros((256, 256))
    for row in range(8):
        for col in range(32):
            pick[row * 32 + col, (col // 8) * 64 + row * 8 + col % 8] = 1.0
    return as_bf16(np.concatenate([pick, pick], 0))


def plane_size(peers):
    return max(peers // 8, 1)


def send_order(peers):
    size = plane_size(peers)
    planes = peers // size
    fold = [p // 2 if p % 2 == 0 else planes - 1 - p // 2 for p in range(planes)]
    return [plane * size + i for plane in fold for i in range(size)]


def split(x):
    high = x.astype(jnp.bfloat16)
    low = (x - high.astype(jnp.float32)).astype(jnp.bfloat16)
    return high, low


def dot(a, b):
    return jnp.dot(a, b, preferred_element_type=jnp.float32)


def strips_kernel(state_ref, strips_ref, edge_ref, held, sems):
    slab = lax.axis_index("slab")
    count, lev = state_ref.shape[0], state_ref.shape[1]
    size = count // sems.shape[0]
    copies = []
    for i in range(sems.shape[0]):
        part = pl.ds(i * size, size)
        copies.append(pltpu.make_async_copy(state_ref.at[part], held.at[part], sems.at[i]))
        copies[i].start()
    cell = lax.broadcasted_iota(jnp.int32, (1024, 128), 0)
    to = lax.broadcasted_iota(jnp.int32, (1024, 128), 1)
    line = to // 32
    line = jnp.where(line < 2, line, 33 - line)
    pick = jnp.where((cell // 32 == to % 32) & (cell % 32 == line), 1.0, 0.0).astype(jnp.bfloat16)
    rows = size * lev
    lane = lax.broadcasted_iota(jnp.int32, (rows, 128), 1)
    for i in range(sems.shape[0]):
        copies[i].wait()
        part = slice(i * size, i * size + size)
        x = held[part]
        tail = x[:, :, 896:].reshape(rows, 128)
        tail = jnp.where((lane // 32) % 2 == 0, pltpu.roll(tail, 96, 1), pltpu.roll(tail, 32, 1))
        strips_ref[part, 0] = jnp.where(lane < 64, x[:, :, :128].reshape(rows, 128), tail).reshape(size, lev, 128)
        high, low = split(x.reshape(rows, 1024))
        strips_ref[part, 1] = (dot(high, pick) + dot(low, pick)).reshape(size, lev, 128)
        edge_ref[part] = jnp.where(slab == 0, x[:, lev - 1, :], x[:, 0, :])


def levels_of(ref, lev):
    at = lax.broadcasted_iota(jnp.int32, (lev, 128), 0)
    out = jnp.zeros((lev, 128), jnp.float32)
    for l in range(lev):
        out = jnp.where(at == l, ref[l], out)
    return out


def local_part(blocks, crow_ref, ccol_ref, mix_ref, state_ref, sten_ref):
    lev = state_ref.shape[1]
    a_row = levels_of(crow_ref, lev) * (1.0 / 12.0)
    a_col = levels_of(ccol_ref, lev) * (1.0 / 12.0)
    mix = levels_of(mix_ref, lev)
    rows = CHUNK * lev
    lane = lax.broadcasted_iota(jnp.int32, (rows, 128), 1)
    level = lax.broadcasted_iota(jnp.int32, (CHUNK, lev, 128), 1)
    zero = jnp.zeros((rows, 128), jnp.float32)
    tiles = [state_ref[blocks, :, 128 * j : 128 * j + 128] for j in range(8)]
    flat = [t.reshape(rows, 128) for t in tiles]
    left = []
    for j in range(8):
        other = jnp.where(lane < 64, flat[j + 1] if j < 7 else zero, flat[j - 1] if j else zero)
        left.append(jnp.concatenate(split(flat[j]) + split(other), 1))
    diff = dot(jnp.concatenate(left, 0), sten_ref[...])
    done = []
    for j in range(8):
        x = tiles[j]
        below = jnp.where(level == 0, 0.0, pltpu.roll(x, 1, 1))
        above = jnp.where(level == lev - 1, 0.0, pltpu.roll(x, lev - 1, 1))
        vert = above - 2.0 * x + below
        d = diff[rows * j : rows * j + rows].reshape(CHUNK, lev, 256)
        done.append(x + a_row * d[:, :, :128] + a_col * d[:, :, 128:] + mix * vert)
    return done


def ghost_codes(block, side, flip):
    here, peers = lax.axis_index("blocks"), lax.axis_size("blocks")
    rel = (block >> 5) - here + 1
    rel = jnp.where(rel < 0, rel + peers, rel)
    rel = jnp.where(rel >= peers, rel - peers, rel)
    rel = jnp.where((here & 1) == 0, rel, 2 - rel)
    swap = (side & 1) ^ flip
    return (block & 31) * 32 + rel * 8 + (side >> 1) * 4 + swap * 2 + flip


def window_tiles(bands, win):
    pairs = [jnp.concatenate(split(band), 1) for band in bands]
    w = dot(jnp.concatenate(pairs, 0), win[...])
    rows = bands[0].shape[0]
    return [w[rows * (t // 2) : rows * (t // 2) + rows, 128 * (t % 2) : 128 * (t % 2) + 128] for t in range(8)]


def load_maps(sten_ref, win_ref, sten, win, sems):
    copies = []
    for i, (ref, held) in enumerate(((sten_ref, sten), (win_ref, win))):
        for n in range(2):
            part = pl.ds(n * 256, 256)
            copies.append(pltpu.make_async_copy(ref.at[part], held.at[part], sems.at[2 * i + n]))
            copies[-1].start()
    for copy in copies:
        copy.wait()


def local_blocks(crow_ref, ccol_ref, mix_ref, state_ref, wins_ref, base_ref, sten, win, kept, base_sems):
    count, lev = state_ref.shape[0], state_ref.shape[1]
    rows = CHUNK * lev

    def base_copy(i):
        blocks = pl.ds(i * CHUNK, CHUNK)
        return pltpu.make_async_copy(kept.at[blocks], base_ref.at[blocks], base_sems.at[i])

    def stencil(i, carry):
        blocks = pl.ds(pl.multiple_of(i * CHUNK, CHUNK), CHUNK)
        done = local_part(blocks, crow_ref, ccol_ref, mix_ref, state_ref, sten)
        for j in range(8):
            kept[blocks, :, 128 * j : 128 * j + 128] = done[j]
        base_copy(i).start()
        bands = [jnp.concatenate([t.reshape(rows, 128) for t in done[2 * j : 2 * j + 2]], 1) for j in range(4)]
        for t, tile in enumerate(window_tiles(bands, win)):
            wins_ref[blocks, t] = tile.reshape(CHUNK, lev, 128)
        return carry

    lax.fori_loop(0, count // CHUNK, stencil, 0)
    for i in range(count // CHUNK):
        base_copy(i).wait()


def first_kernel(
    crow_ref,
    ccol_ref,
    mix_ref,
    block_ref,
    side_ref,
    flip_ref,
    strips_ref,
    state_ref,
    sten_ref,
    win_ref,
    wins_ref,
    base_ref,
    code_ref,
    ready_ref,
    sten,
    win,
    kept,
    sems,
    base_sems,
):
    code_ref[...] = ghost_codes(block_ref[...], side_ref[...], flip_ref[...])
    ready_ref[...] = strips_ref[...]

    @pl.when(lax.axis_index("slab") == 0)
    def _():
        load_maps(sten_ref, win_ref, sten, win, sems)
        local_blocks(crow_ref, ccol_ref, mix_ref, state_ref, wins_ref, base_ref, sten, win, kept, base_sems)


def second_kernel(
    crow_ref,
    ccol_ref,
    mix_ref,
    edge_ref,
    state_ref,
    sten_ref,
    win_ref,
    base_in_ref,
    wins_ref,
    base_ref,
    ready_ref,
    sten,
    win,
    kept,
    sems,
    base_sems,
):
    ready_ref[...] = edge_ref[...]

    @pl.when(lax.axis_index("slab") == 1)
    def _():
        load_maps(sten_ref, win_ref, sten, win, sems)
        local_blocks(crow_ref, ccol_ref, mix_ref, state_ref, wins_ref, base_ref, sten, win, kept, base_sems)


def edge_kernel(mix_ref, edge_ref, win_ref, first_ref, second_ref, wins_ref, fix_ref, fix, sem):
    slab = lax.axis_index("slab")
    lev = wins_ref.shape[2]
    fix[...] = edge_ref[...] * jnp.where(slab == 0, mix_ref[lev - 1], mix_ref[0])
    fix_copy = pltpu.make_async_copy(fix, fix_ref, sem.at[0])
    fix_copy.start()
    edge = window_tiles([fix[:, 256 * j : 256 * j + 256] for j in range(4)], win_ref)
    for which, done_ref, level in ((0, first_ref, lev - 1), (1, second_ref, 0)):

        @pl.when(slab == which)
        def _():
            wins_ref[...] = done_ref[...]
            for t in range(8):
                wins_ref[:, t, level, :] += edge[t]

    fix_copy.wait()


def gather_ghosts(i, code_ref, a_row, a_col, near, ghosts_ref):
    lev = near[0].shape[2]
    half = lax.broadcasted_iota(jnp.int32, (lev, 128), 1) // 64
    rows = CHUNK * lev
    for s in range(4):
        parts = []
        for n in range(CHUNK):
            code = code_ref[s, i * CHUNK + n]
            owner = (code >> 3) & 3
            x, middle, last = (ref[code >> 5, (code >> 2) & 1] for ref in near)
            x = jnp.where(owner == 0, x, jnp.where(owner == 1, middle, last))
            x = jnp.where((code & 2) == 0, x, pltpu.roll(x, 64, 1))
            parts.append(jnp.where(half == (code & 1), x, 0.0))
        x = jnp.stack(parts) * (a_row if s < 2 else a_col)
        high, low = split(x.reshape(rows, 128))
        ghosts_ref[:, s * 256 : s * 256 + 128] = high
        ghosts_ref[:, s * 256 + 128 : s * 256 + 256] = low


def pack_kernel(
    code_ref,
    send_ref,
    crow_ref,
    ccol_ref,
    base_ref,
    far_ref,
    own_ref,
    near_ref,
    col0_ref,
    col1_ref,
    row0_ref,
    row1_ref,
    pay_ref,
    ghosts_ref,
    wins,
    held_pay,
    pay_sems,
    ghost_sems,
    *ghosts,
):
    lev = own_ref.shape[2]
    half = lax.broadcasted_iota(jnp.int32, (lev, 128), 1) // 64
    near = (far_ref, own_ref, near_ref)
    a_row = levels_of(crow_ref, lev) * (1.0 / 12.0)
    a_col = levels_of(ccol_ref, lev) * (1.0 / 12.0)
    copies = []
    for i, held in enumerate(ghosts):
        gather_ghosts(i, code_ref, a_row, a_col, near, held)
        rows = pl.ds(i * CHUNK * lev, CHUNK * lev)
        copies.append(pltpu.make_async_copy(held, ghosts_ref.at[rows], ghost_sems.at[i]))
        copies[i].start()
        blocks = slice(i * CHUNK, i * CHUNK + CHUNK)
        row0 = dot(held[:, 0:256], row0_ref[...]).reshape(CHUNK, lev, 256)
        row1 = dot(held[:, 256:512], row1_ref[...]).reshape(CHUNK, lev, 256)
        for h, col_ref in enumerate((col0_ref, col1_ref)):
            c = dot(held[:, 512 + 256 * h : 768 + 256 * h], col_ref[...]).reshape(CHUNK, lev, 512)
            for j in range(4):
                v = base_ref[blocks, 2 * j + h] + c[:, :, 128 * j : 128 * j + 128]
                if j == 0:
                    v = v + row0[:, :, 128 * h : 128 * h + 128]
                if j == 3:
                    v = v + row1[:, :, 128 * h : 128 * h + 128]
                wins[blocks, 2 * j + h] = v

    order = send_order(pay_ref.shape[0])
    size = pay_ref.shape[0] // pay_sems.shape[0]
    for i in range(pay_sems.shape[0]):
        for d in range(i * size, i * size + size):
            parts = []
            for k in range(2):
                w = send_ref[k, order[d]]
                x = wins[w >> 4, (w >> 1) & 7]
                parts.append(jnp.where((w & 1) == k, x, pltpu.roll(x, 64, 1)))
            held_pay[d] = jnp.where(half == 0, parts[0], parts[1])
        part = pl.ds(i * size, size)
        copies.append(pltpu.make_async_copy(held_pay.at[part], pay_ref.at[part], pay_sems.at[i]))
        copies[-1].start()
    for copy in copies:
        copy.wait()


def finish_kernel(base_ref, ghosts_ref, fix_ref, col_ref, row0_ref, row1_ref, out_ref):
    blocks, lev = base_ref.shape[:2]
    level = lax.broadcasted_iota(jnp.int32, (blocks, lev, 128), 1)
    edge_level = jnp.where(lax.axis_index("slab") == 0, lev - 1, 0)
    c = dot(ghosts_ref[:, 512:1024], col_ref[...])
    row0 = dot(ghosts_ref[:, 0:256], row0_ref[...])
    row1 = dot(ghosts_ref[:, 256:512], row1_ref[...])
    for j in range(8):
        v = c[:, 128 * j : 128 * j + 128]
        if j == 0:
            v = v + row0
        if j == 7:
            v = v + row1
        lanes = slice(128 * j, 128 * j + 128)
        fix = jnp.where(level == edge_level, fix_ref[:, lanes][:, None, :], 0.0)
        out_ref[:, :, lanes] = base_ref[:, :, lanes] + fix + v.reshape(blocks, lev, 128)


def refine_kernel(sizes, slot_ref, count_ref, recv_ref, table_ref, out_ref, held, sems, *parents):
    lev = recv_ref.shape[1]
    half = lax.broadcasted_iota(jnp.int32, (lev, 128), 1) // 64
    live = count_ref[0]
    size_in = plane_size(recv_ref.shape[0])
    planes = recv_ref.shape[0] // size_in
    shift = size_in.bit_length() - 1
    copies, start = [], 0
    for i, size in enumerate(sizes):
        for n in range(size):
            slot = slot_ref[0, start + n]
            src = slot >> 1
            plane = src >> shift
            place = jnp.where(plane < (planes + 1) // 2, 2 * plane, 2 * planes - 1 - 2 * plane)
            x = recv_ref[(place << shift) + (src & (size_in - 1))]
            x = jnp.where(half == (slot & 1), x, pltpu.roll(x, 64, 1))
            x = jnp.where(start + n < live, x, 0.0)
            high, low = split(x)
            parents[i][n * lev : (n + 1) * lev, :128] = high
            parents[i][n * lev : (n + 1) * lev, 128:] = low
        part = pl.ds(start, size)
        fine = dot(parents[i][...], table_ref[...])
        held[part] = fine.astype(jnp.bfloat16).reshape(size, lev, 1024)
        copies.append(pltpu.make_async_copy(held.at[part], out_ref.at[part], sems.at[i]))
        copies[i].start()
        start += size
    for copy in copies:
        copy.wait()


VMEM = pl.BlockSpec(memory_space=pltpu.VMEM)
SMEM = pl.BlockSpec(memory_space=pltpu.SMEM)
HBM = pl.BlockSpec(memory_space=pltpu.HBM)
PARAMS = pltpu.CompilerParams(vmem_limit_bytes=VMEM_LIMIT)


def cost(flops, size):
    return pl.CostEstimate(flops=flops, bytes_accessed=size, transcendentals=0)


def make_strips(state):
    count, lev = state.shape[:2]
    return pl.pallas_call(
        strips_kernel,
        out_shape=(
            jax.ShapeDtypeStruct((count, 2, lev, 128), jnp.float32),
            jax.ShapeDtypeStruct((count, 1024), jnp.float32),
        ),
        in_specs=[HBM],
        out_specs=(VMEM, VMEM),
        scratch_shapes=[pltpu.VMEM(state.shape, jnp.float32), pltpu.SemaphoreType.DMA((2,))],
        compiler_params=PARAMS,
        name="strips",
    )(pltpu.with_memory_space_constraint(state, pltpu.HBM))


def local_maps():
    return [pltpu.with_memory_space_constraint(jnp.asarray(m), pltpu.HBM) for m in (stencil_map(), window_map())]


def local_scratch(state):
    return [
        pltpu.VMEM((512, 256), jnp.bfloat16),
        pltpu.VMEM((512, 256), jnp.bfloat16),
        pltpu.VMEM(state.shape, jnp.float32),
    ]


def make_first(coefs, tables, strips, state):
    count, lev = state.shape[:2]
    return pl.pallas_call(
        first_kernel,
        out_shape=(
            jax.ShapeDtypeStruct((count, 8, lev, 128), jnp.float32),
            pltpu.HBM(state.shape, jnp.float32),
            jax.ShapeDtypeStruct(tables[0].shape, jnp.int32),
            jax.ShapeDtypeStruct(strips.shape, jnp.float32),
        ),
        in_specs=[SMEM] * 3 + [VMEM] * 5 + [HBM] * 2,
        out_specs=(VMEM, HBM, VMEM, VMEM),
        scratch_shapes=local_scratch(state)
        + [pltpu.SemaphoreType.DMA((4,)), pltpu.SemaphoreType.DMA((count // CHUNK,))],
        compiler_params=PARAMS,
        name="first",
    )(*coefs, *tables, strips, state, *local_maps())


def make_second(coefs, edge, state, base):
    count, lev = state.shape[:2]
    return pl.pallas_call(
        second_kernel,
        out_shape=(
            jax.ShapeDtypeStruct((count, 8, lev, 128), jnp.float32),
            pltpu.HBM(state.shape, jnp.float32),
            jax.ShapeDtypeStruct(edge.shape, jnp.float32),
        ),
        in_specs=[SMEM] * 3 + [VMEM] * 2 + [HBM] * 3,
        out_specs=(VMEM, HBM, VMEM),
        scratch_shapes=local_scratch(state)
        + [pltpu.SemaphoreType.DMA((4,)), pltpu.SemaphoreType.DMA((count // CHUNK,))],
        input_output_aliases={7: 1},
        compiler_params=PARAMS,
        cost_estimate=cost(10**3, 10**3),
        name="second",
    )(*coefs, edge, state, *local_maps(), base)


def add_edge(mixing, edge, first, second):
    return pl.pallas_call(
        edge_kernel,
        out_shape=(jax.ShapeDtypeStruct(first.shape, jnp.float32), pltpu.HBM(edge.shape, jnp.float32)),
        in_specs=[SMEM] + [VMEM] * 4,
        out_specs=(VMEM, HBM),
        scratch_shapes=[pltpu.VMEM(edge.shape, jnp.float32), pltpu.SemaphoreType.DMA((1,))],
        compiler_params=PARAMS,
        cost_estimate=cost(10**3, 10**3),
        name="edge",
    )(mixing, edge, jnp.asarray(window_map()), first, second)


def make_payload(code, send, coefs, base, nearby):
    count, lev, peers = base.shape[0], base.shape[2], send.shape[1]
    sides = [window_order(ghost_map(s)) for s in range(4)]
    cols = [m.reshape(256, 4, 256)[:, :, 128 * h : 128 * h + 128].reshape(256, 512) for h, m in enumerate(sides[2:])]
    maps = cols + [sides[0][:, :256], sides[1][:, 768:]]
    return pl.pallas_call(
        pack_kernel,
        out_shape=(
            pltpu.HBM((peers, lev, 128), jnp.float32),
            pltpu.HBM((count * lev, 1024), jnp.bfloat16),
        ),
        in_specs=[SMEM] * 4 + [VMEM] * 8,
        out_specs=(HBM, HBM),
        scratch_shapes=[
            pltpu.VMEM((count, 8, lev, 128), jnp.float32),
            pltpu.VMEM((peers, lev, 128), jnp.float32),
            pltpu.SemaphoreType.DMA((4,)),
            pltpu.SemaphoreType.DMA((count // CHUNK,)),
            *[pltpu.VMEM((CHUNK * lev, 1024), jnp.bfloat16)] * (count // CHUNK),
        ],
        compiler_params=PARAMS,
        cost_estimate=cost(10**9, 8 * 10**6),
        name="pack",
    )(code, send, *coefs[:2], base, *nearby, *[jnp.asarray(m) for m in maps])


def make_advanced(base, ghosts, fix):
    count, lev = base.shape[:2]
    maps = [np.concatenate([ghost_map(2), ghost_map(3)], 0), ghost_map(0)[:, :128], ghost_map(1)[:, 896:]]
    block = pl.BlockSpec((CHUNK, lev, 1024), lambda i: (i, 0, 0))
    return pl.pallas_call(
        finish_kernel,
        grid=(count // CHUNK,),
        out_shape=jax.ShapeDtypeStruct(base.shape, jnp.float32),
        in_specs=[block, pl.BlockSpec((CHUNK * lev, 1024), lambda i: (i, 0)), pl.BlockSpec((CHUNK, 1024), lambda i: (i, 0))]
        + [VMEM] * 3,
        out_specs=block,
        compiler_params=PARAMS,
        cost_estimate=cost(2 * 10**9, 8 * 10**6),
        name="finish",
    )(
        pltpu.with_memory_space_constraint(base, pltpu.HBM),
        pltpu.with_memory_space_constraint(ghosts, pltpu.HBM),
        pltpu.with_memory_space_constraint(fix, pltpu.HBM),
        *[jnp.asarray(m) for m in maps],
    )


def make_refined(slots, live, received):
    fine = slots.shape[1]
    lev = received.shape[1]
    sizes = []
    for size in REFINE + (fine,) * fine:
        if sum(sizes) < fine:
            sizes.append(min(size, fine - sum(sizes)))
    return pl.pallas_call(
        functools.partial(refine_kernel, tuple(sizes)),
        out_shape=jax.ShapeDtypeStruct((fine, lev, 1024), jnp.bfloat16),
        in_specs=[SMEM, SMEM, VMEM, VMEM],
        out_specs=HBM,
        scratch_shapes=[
            pltpu.VMEM((fine, lev, 1024), jnp.bfloat16),
            pltpu.SemaphoreType.DMA((len(sizes),)),
            *[pltpu.VMEM((size * lev, 256), jnp.bfloat16) for size in sizes],
        ],
        compiler_params=PARAMS,
        name="refine",
    )(slots, live, received, jnp.asarray(refine_table()))


def body(
    state,
    courant_row,
    courant_col,
    mixing,
    nbr_block,
    nbr_side,
    nbr_flip,
    send_idx,
    fine_slot,
    fine_count,
):
    peers = lax.axis_size("blocks")
    far = [(i, (i + (1 if i % 2 else -1)) % peers) for i in range(peers)]
    near = [(i, i ^ 1) for i in range(peers)]
    coefs = (courant_row, courant_col, mixing)
    strips, edge = make_strips(state)
    first, base, code, strips = make_first(coefs, (nbr_block.T, nbr_side.T, nbr_flip.T), strips, state)
    nearby = (lax.ppermute(strips, "blocks", far), strips, lax.ppermute(strips, "blocks", near))
    second, base, edge = make_second(coefs, edge, state, base)
    edge = lax.ppermute(edge, "slab", [(0, 1), (1, 0)])
    wins, fix = add_edge(mixing, edge, first, second)
    payload, ghosts = make_payload(code, send_idx[0].T, coefs, wins, nearby)
    received = lax.all_to_all(
        payload, "blocks", split_axis=0, concat_axis=0, axis_index_groups=[send_order(peers)], tiled=True
    )
    advanced = make_advanced(base, ghosts, fix)
    return advanced, make_refined(fine_slot, fine_count, received)


def solution(mesh):
    in_specs = (
        P("blocks", "slab", None),
        P("slab"),
        P("slab"),
        P("slab"),
        P("blocks", None),
        P("blocks", None),
        P("blocks", None),
        P("blocks", None, None),
        P("blocks", None),
        P("blocks"),
    )
    out_specs = (P("blocks", "slab", None), P("blocks", "slab", None))
    return jax.shard_map(body, mesh=mesh, in_specs=in_specs, out_specs=out_specs, check_vma=False)
```
